32 devices in a mesh: groups: 2 (over y), dp: 8 (over z, x), mp: 2 (over core).
Axes of the slice: x: 2, y: 2, z: 4, core: 2. Of those that a mesh axis runs over, the one named last changes fastest.
Arguments:
- hidden_states: bfloat16 [32, 256, 5120], P(('groups', 'dp'), None, 'mp'), parts along dimension 0, may hold values from -6 to 6
- passage_states: bfloat16 [32, 256, 2048], P(('groups', 'dp')), parts along dimension 0, may hold values from -6 to 6
- down_weight: bfloat16 [2048, 5120], P('dp', 'mp'), may hold values from -0.078125 to 0.078125
- block_question: int32 [32, 1], P('groups'), parts along dimension 0, may hold values from 0 to 7; in each aligned block of 16 rows (0 to 15, 16 to 31, ...) at most 4 rows name the same one
- question_owner: int32 [16], P('groups'), parts along dimension 0, may hold values from 0 to 7, each once
- decoder_states: bfloat16 [16, 16, 2048], P(('groups', 'dp')), parts along dimension 0, may hold values from -60 to 60
Outputs:
- attended: bfloat16 [16, 16, 2048], P(('groups', 'dp')), parts along dimension 0
The draws below stay inside these ranges and needn't reach their ends.
There are 2 independent parts, one for each index of `groups`. The reference program is written for one: setup_inputs(seed, part) draws one part's arguments, and reference() takes and returns one part's arrays. A program takes and returns all parts, laid end to end along the dimension named above; an argument that names none is the same for every part. Nothing has to cross between parts.
Inputs may be any that keep to these rules, and one draw needn't show every extreme that they name: `block_question`: no question is named by more than 4 passages, one by exactly 4; every question is named by some passage. `question_owner`: A permutation: every decoder slot owns exactly one question.
All inputs are finite; a program needn't handle non-finite values.
Results may differ from the reference program's by a relative error of at most 0.009.
The reference program's roundings to bfloat16 on the way count: a program that leaves them out, or rounds other values in their place, can miss the bound.
Values may be sent and summed in bfloat16 or wider, within the bound.
No kernel may reach another device: no remote copies, remote signals or barrier semaphores. Data moves between devices by JAX's collectives and lax.ppermute only.
A program may use at most 64 MiB of HBM per device.

```python
import math
import jax
import jax.numpy as jnp
import numpy as np
from jax import lax

HEADS = 32
HEAD_DIM = 64
FF = 5120
BLK = 256
QT = 16
D = 2048
NQ = 8
NB = 16
QMOST = 4


def draw_decoder_states(key, part):
    key = jax.random.fold_in(key, 7)
    values = 0.25 * jnp.clip(jax.random.normal(key, (NQ, QT, D), jnp.float32), -6.0, 6.0)
    return values.astype(jnp.bfloat16)


def level_of(own_key, extent, cuts, low, high):
    level = 1.0
    for axis_at, parts in cuts:
        heights = jax.random.uniform(jax.random.fold_in(jax.random.fold_in(own_key, 6), axis_at), (parts,), jnp.float32, low / len(cuts), high / len(cuts))
        level = level * jnp.repeat(jnp.exp(heights), extent[axis_at] // parts).reshape((-1,) + (1,) * (len(extent) - 1 - axis_at))
    return level


def shared_out(stream_key, own, number, rows, amount, top, most, skew):
    sequence = jax.random.permutation(stream_key, amount)
    crowded, common = load_shares(amount, rows * top, most, skew, True), load_shares(amount, rows * top, most, skew, False)
    places = jnp.arange(amount)

    def named(lengths, offset_by):
        used = int((lengths > 0).sum())
        fixed = max(1, used // 4)
        moved = fixed + (places - fixed + offset_by * (used - fixed)) % max(1, amount - fixed)
        return jnp.zeros((amount,), jnp.int32).at[sequence[jnp.where(places < fixed, places, moved)]].set(jnp.asarray(lengths, jnp.int32))

    lengths = jnp.where(number % 4 == 0, named(crowded, number // 4), named(common, number - number // 4 - 1))
    mixed = jax.random.permutation(jax.random.fold_in(own, 3), amount)
    giver, sink = mixed[0:amount // 2 * 2:2], mixed[1:amount // 2 * 2:2]
    room = jnp.minimum(lengths[giver] - 1, most - lengths[sink]) // 2
    room = jnp.where((giver == sequence[0]) | (sink == sequence[0]) | (lengths[sink] == 0), 0, jnp.maximum(room, 0))
    moved = jax.random.randint(jax.random.fold_in(own, 4), (amount // 2,), 0, 1 << 20) % (room + 1)
    lengths = lengths.at[giver].add(-moved).at[sink].add(moved)
    members = jnp.searchsorted(jnp.cumsum(lengths), jnp.arange(rows * top), side="right").astype(jnp.int32)
    grid = members.reshape(top, rows).T
    grid = grid[jax.random.permutation(jax.random.fold_in(own, 1), rows)]
    offset_by = jax.random.randint(jax.random.fold_in(own, 2), (rows, 1), 0, top)
    return jnp.take_along_axis(grid, (jnp.arange(top)[None, :] + offset_by) % top, axis=1)


def load_shares(number_of, total, limit, skew, full):
    portions = [(1 << 20) // math.isqrt(rank ** skew) + 1 for rank in range(1, number_of + 1)]
    largest = limit if full else min(limit, max(-(-total // number_of), total * portions[0] // sum(portions)))
    least = 1 if total - largest >= number_of - 1 else 0
    holding, spare = [largest] + [least] * (number_of - 1), total - largest - least * (number_of - 1)
    while spare > 0:
        free = [i for i in range(1, number_of) if holding[i] < largest] or [i for i in range(1, number_of) if holding[i] < limit]
        pool, left = sum([portions[i] for i in free]), spare
        for i in free:
            more = min(limit - holding[i], max(1, left * portions[i] // pool), spare)
            holding[i] = holding[i] + more
            spare = spare - more
    return np.array(holding)


def noise(rng, extent, spread, bound, cuts=(), kind=jnp.bfloat16):
    entries = jax.random.normal(rng, extent, jnp.float32) * spread
    if len(cuts) > 0:
        entries = level_of(rng, extent, cuts, -0.22, 0.18) * entries
    return jnp.clip(entries, min=-bound, max=bound).astype(kind)


def setup_inputs(seed: int = 0, part: int = 0) -> dict:
    streams_of = jax.random.split(jax.random.key(seed), 7)
    own_keys = jax.random.split(jax.random.fold_in(streams_of[6], part), 7)
    hidden_states = noise(own_keys[0], (NB, BLK, FF), 1.0, 6.0, ((0, 8), (2, 2)))
    passage_states = noise(own_keys[1], (NB, BLK, D), 1.0, 6.0, ((0, 8),))
    down_weight = noise(streams_of[2], (D, FF), FF ** -0.5, 0.078125, ((0, 8), (1, 2)))
    block_question_keys = jax.random.split(jax.random.fold_in(own_keys[3], 1), NB // NB)
    block_question_turns = jax.random.permutation(jax.random.fold_in(own_keys[3], 3), NB // NB)
    block_question = jax.vmap(lambda own, number: shared_out(jax.random.fold_in(own_keys[3], 2), own, number, NB, NQ, 1, QMOST, 2))(block_question_keys, block_question_turns).reshape((NB, 1))
    question_owner = jax.random.permutation(own_keys[4], NQ).astype(jnp.int32)
    decoder_states = draw_decoder_states(jax.random.fold_in(jax.random.fold_in(streams_of[6], part), 71), part)
    return dict(hidden_states=hidden_states, passage_states=passage_states, down_weight=down_weight, block_question=block_question, question_owner=question_owner, decoder_states=decoder_states)


def reference(hidden_states, passage_states, down_weight, block_question, question_owner, decoder_states):
    def project(pair):
        hidden_block, passage_block = pair
        product = lax.dot_general(hidden_block, down_weight, (((1,), (1,)), ((), ())), preferred_element_type=jnp.float32)
        return (passage_block.astype(jnp.float32) + product).astype(jnp.bfloat16)

    encoded = lax.map(project, (hidden_states, passage_states))
    questions = block_question[:, 0].astype(jnp.int32)
    positions = jnp.arange(NB, dtype=jnp.int32)
    earlier = (questions[:, None] == questions[None, :]) & (positions[None, :] < positions[:, None])
    rank = jnp.sum(earlier.astype(jnp.int32), axis=1).astype(jnp.int32)
    table = jnp.zeros((NQ, QMOST), jnp.int32).at[questions, rank].set(positions)
    counts = jnp.sum((questions[:, None] == jnp.arange(NQ, dtype=jnp.int32)[None, :]).astype(jnp.int32), axis=0).astype(jnp.int32)
    slot_question = jnp.zeros((NQ,), jnp.int32).at[question_owner.astype(jnp.int32)].set(jnp.arange(NQ, dtype=jnp.int32))

    def attend(packed):
        query_rows, question = packed
        picked = encoded[table[question]]
        key_rows = picked.reshape(QMOST * BLK, HEADS, HEAD_DIM).astype(jnp.float32)
        usable = jnp.repeat(jnp.arange(QMOST, dtype=jnp.int32) < counts[question], BLK)
        scores = jnp.einsum("qhd,khd->hqk", query_rows.reshape(QT, HEADS, HEAD_DIM).astype(jnp.float32), key_rows)
        masked = jnp.where(usable[None, None, :], scores, -jnp.inf)
        row_top = jnp.max(masked, axis=2, keepdims=True)
        weights = jnp.exp(masked - row_top)
        totals = jnp.sum(weights, axis=2)
        rounded = lax.optimization_barrier(weights.astype(jnp.bfloat16))
        blended = jnp.einsum("hqk,khd->hqd", rounded.astype(jnp.float32), key_rows) / totals[:, :, None]
        return jnp.transpose(blended, (1, 0, 2)).reshape(QT, D).astype(jnp.bfloat16)

    return lax.map(attend, (decoder_states, slot_question))
```

```python
import functools

import jax
import jax.numpy as jnp
from jax import lax
from jax.experimental import pallas as pl
from jax.experimental.pallas import tpu as pltpu
from jax.sharding import Mesh, PartitionSpec as P

HEAD_DIM = 64
EMPTY = -3e38
VMEM_LIMIT = 40 * 1024 * 1024
SWAP = [(0, 1), (1, 0)]
CROSS = [(0, 3), (3, 0), (1, 2), (2, 1)]


def head_pick(tall, query_len):
    lanes = tall.shape[1]
    lane_head = lax.broadcasted_iota(jnp.int32, (query_len, lanes), 1) // HEAD_DIM
    picked = jnp.zeros((query_len, lanes), jnp.float32)
    for head in range(lanes // HEAD_DIM):
        picked = jnp.where(lane_head == head, tall[head * query_len : (head + 1) * query_len, :], picked)
    return picked


def attend_kernel(place_ref, query_ref, *refs):
    out_ref = refs[-1]
    pieces = refs[:-1]
    query_len, held = query_ref.shape[1:]
    heads = held // HEAD_DIM
    tall = heads * query_len
    out_ref[:, :, :held] = jnp.zeros(out_ref.shape[:2] + (held,), jnp.float32)
    ext_row = lax.broadcasted_iota(jnp.int32, out_ref.shape[:2] + (tall,), 1)
    out_ref[:, :, held:] = jnp.where(ext_row == 0, EMPTY, 0.0)
    row_head = lax.broadcasted_iota(jnp.int32, (tall, held), 0) // query_len
    lane_head = lax.broadcasted_iota(jnp.int32, (tall, held), 1) // HEAD_DIM
    diagonal = row_head == lane_head
    square = lax.broadcasted_iota(jnp.int32, (tall, tall), 0) == lax.broadcasted_iota(jnp.int32, (tall, tall), 1)
    ext = lax.broadcasted_iota(jnp.int32, (query_len, tall), 0)
    places, keys, scores, tops = [], [], [], []
    for piece in range(len(pieces) // 3):
        mine, other, residual = pieces[3 * piece : 3 * piece + 3]
        for block in range(mine.shape[0]):
            place = place_ref[len(places)]
            rows = residual[block].astype(jnp.float32) + (mine[block] + other[block])
            key_rows = rows.astype(jnp.bfloat16)
            query = jnp.concatenate([query_ref[place]] * heads, axis=0)
            query = jnp.where(diagonal, query, jnp.zeros_like(query))
            score = lax.dot_general(
                query, key_rows, (((1,), (1,)), ((), ())), preferred_element_type=jnp.float32
            )
            places.append(place)
            keys.append(key_rows)
            scores.append(score)
            tops.append(jnp.max(score, axis=1, keepdims=True))
    for at, place in enumerate(places):
        top = tops[at]
        for other_at, other_place in enumerate(places):
            if other_at != at:
                top = jnp.maximum(top, jnp.where(other_place == place, tops[other_at], EMPTY))
        weights = jnp.exp(scores[at] - top)
        total = jnp.sum(weights, axis=1, keepdims=True)
        blend = lax.dot_general(
            weights.astype(jnp.bfloat16), keys[at], (((1,), (0,)), ((), ())),
            preferred_element_type=jnp.float32,
        )
        top_row = jnp.sum(jnp.where(square, top, 0.0), axis=0, keepdims=True)
        total_row = jnp.sum(jnp.where(square, total, 0.0), axis=0, keepdims=True)
        out_ref[place, :, :held] = out_ref[place, :, :held] + head_pick(blend, query_len)
        before = out_ref[place, :, held:]
        out_ref[place, :, held:] = jnp.where(
            ext == 0, top_row, jnp.where(ext == 1, before + total_row, 0.0)
        )


def merge_kernel(*refs):
    out_ref = refs[-1]
    parts = refs[:-1]
    query_len, held = out_ref.shape[1:]
    tall = held // HEAD_DIM * query_len
    square = lax.broadcasted_iota(jnp.int32, (tall, tall), 0) == lax.broadcasted_iota(jnp.int32, (tall, tall), 1)

    def over(start, step):
        for part in parts:
            start = lax.fori_loop(
                0, part.shape[0], functools.partial(step, part), start, unroll=part.shape[0] <= 8
            )
        return start

    for slot in range(out_ref.shape[0]):
        def top_step(part, at, top):
            return jnp.maximum(top, part[at, slot, 0:1, held:])

        def total_step(part, at, total):
            return total + jnp.exp(part[at, slot, 0:1, held:] - top) * part[at, slot, 1:2, held:]

        def blend_step(part, at, blend):
            share = jnp.exp(part[at, slot, 0:1, held:] - top) / total
            column = jnp.sum(jnp.where(square, share, 0.0), axis=1, keepdims=True)
            spread = head_pick(jnp.broadcast_to(column, (tall, held)), query_len)
            return blend + spread * part[at, slot, :, :held]

        top = over(jnp.full((1, tall), EMPTY, jnp.float32), top_step)
        total = over(jnp.zeros((1, tall), jnp.float32), total_step)
        blend = over(jnp.zeros((query_len, held), jnp.float32), blend_step)
        out_ref[slot] = blend.astype(out_ref.dtype)


def in_vmem(count):
    return [pl.BlockSpec(memory_space=pltpu.VMEM)] * count


def body(hidden_states, passage_states, down_weight, block_question, question_owner, decoder_states):
    blocks, block_len, units = hidden_states.shape
    width = passage_states.shape[2]
    query_len = decoder_states.shape[1]
    highs, lows, cores = lax.axis_size("high"), lax.axis_size("low"), lax.axis_size("mp")
    group, high, side, low, core = (lax.axis_index(name) for name in ("groups", "high", "side", "low", "mp"))
    shard = down_weight.shape[0]
    stride = lows * shard
    held = width // 2 // cores
    heads = held // HEAD_DIM
    per_core = highs // cores
    members = highs * lows
    slot_total = question_owner.shape[0]
    rows = blocks * block_len

    def features(array, of_side):
        first = (core * per_core * 2 + of_side) * stride
        return jnp.concatenate(
            [
                lax.dynamic_slice_in_dim(array, first + at * 2 * stride, stride, axis=array.ndim - 1)
                for at in range(per_core)
            ],
            axis=-1,
        )

    partner_hidden = [lax.ppermute(hidden_states[at], "side", SWAP) for at in range(blocks)]
    partner_residual = lax.ppermute(features(passage_states, 1 - side), "side", SWAP)
    own_residual = features(passage_states, side)
    own_query = features(decoder_states, side)
    partner_query = lax.ppermute(features(decoder_states, 1 - side), "side", SWAP)
    queries = jnp.where(
        side == 0,
        jnp.concatenate([own_query, partner_query], axis=0),
        jnp.concatenate([partner_query, own_query], axis=0),
    )
    queries = lax.all_gather(queries, ("high", "low"), axis=0, tiled=True)

    if highs == 4 and lows == 1:
        half = shard // 2
        sent = lax.dynamic_slice_in_dim(down_weight, group * half, half, axis=0)
        after = [(at, (at + 1) % highs) for at in range(highs)]
        ahead = [(at, (at - 1) % highs) for at in range(highs)]
        from_one = lax.ppermute(sent, "high", after)
        from_three = lax.ppermute(sent, "high", ahead)
        from_two = lax.ppermute(from_one, "high", after)
        weight = jnp.zeros((highs * shard, units), down_weight.dtype)

        def placed(weight, piece, offset, of_half):
            at = lax.rem(high + offset + 2 * highs - core * per_core, highs)
            return lax.dynamic_update_slice_in_dim(weight, piece, at * shard + of_half * half, axis=0)

        weight = placed(weight, down_weight, 0, 0)
        for piece, offset in ((from_one, -1), (from_three, 1), (from_two, -2)):
            weight = placed(weight, piece, offset, group)
            weight = placed(weight, lax.ppermute(piece, "groups", SWAP), offset, 1 - group)
    else:
        weight = lax.all_gather(down_weight, ("high", "low"), axis=0, tiled=True)
        weight = jnp.where(core == 0, weight, jnp.roll(weight, held, axis=0))

    def project(flat):
        def part(rows_of):
            return lax.dot_general(
                flat, rows_of, (((1,), (1,)), ((), ())), preferred_element_type=jnp.float32
            ).reshape(-1, block_len, held)

        other = lax.ppermute(part(weight[held:]), "mp", SWAP)
        return part(weight[:held]), other

    questions = block_question[:, 0]
    question_ids = jnp.arange(slot_total, dtype=jnp.int32)
    owners = jnp.sum(jnp.where(questions[:, None] == question_ids[None, :], question_owner[None, :], 0), axis=1)
    owner_high, owner_side, owner_low = owners // (2 * lows), (owners // lows) % 2, owners % lows
    owner_place = (owner_high * lows + owner_low) * 2 + owner_side
    own_at = ((high * 2 + side) * lows + low) * blocks
    partner_at = ((high * 2 + 1 - side) * lows + low) * blocks
    places = jnp.concatenate(
        [lax.dynamic_slice_in_dim(owner_place, at, blocks) for at in (own_at, partner_at)]
    )

    pieces = [*project(hidden_states.reshape(rows, units)), own_residual]
    for at in range(blocks):
        pieces += [*project(partner_hidden[at]), partner_residual[at : at + 1]]
    partials = pl.pallas_call(
        attend_kernel,
        out_shape=jax.ShapeDtypeStruct((2 * members, query_len, held + heads * query_len), jnp.float32),
        in_specs=[pl.BlockSpec(memory_space=pltpu.SMEM)] + in_vmem(1 + len(pieces)),
        out_specs=pl.BlockSpec(memory_space=pltpu.VMEM),
        compiler_params=pltpu.CompilerParams(vmem_limit_bytes=VMEM_LIMIT),
        name="attend",
    )(places, queries, *pieces)
    partials = partials.reshape((members, 2) + partials.shape[1:])

    if highs == 4 and lows == 1:
        received = []
        for shift in range(highs):
            outgoing = lax.dynamic_slice_in_dim(partials, lax.rem(high + shift, highs), 1, axis=0)
            pairs = [(at, (at + shift) % highs) for at in range(highs)]
            received.append(lax.ppermute(outgoing, "high", pairs) if shift else outgoing)
    else:
        received = [lax.all_to_all(partials, ("high", "low"), split_axis=0, concat_axis=0, tiled=True)]
    merged = pl.pallas_call(
        merge_kernel,
        out_shape=jax.ShapeDtypeStruct((2, query_len, held), decoder_states.dtype),
        in_specs=in_vmem(len(received)),
        out_specs=pl.BlockSpec(memory_space=pltpu.VMEM),
        compiler_params=pltpu.CompilerParams(vmem_limit_bytes=VMEM_LIMIT),
        name="merge",
    )(*received)

    mine = lax.dynamic_slice_in_dim(merged, side, 1, axis=0)
    away = lax.dynamic_slice_in_dim(merged, 1 - side, 1, axis=0)
    by_core = lax.ppermute(mine, "mp", SWAP)
    by_side = lax.ppermute(away, "side", SWAP)
    by_both = lax.ppermute(away, ("side", "mp"), CROSS)
    near = [jnp.where(core == at, mine, by_core) for at in range(cores)]
    far = [jnp.where(core == at, by_side, by_both) for at in range(cores)]
    columns = []
    for at in range(highs):
        span = slice(at % per_core * stride, (at % per_core + 1) * stride)
        mine_span, away_span = near[at // per_core][:, :, span], far[at // per_core][:, :, span]
        columns += [jnp.where(side == 0, mine_span, away_span), jnp.where(side == 0, away_span, mine_span)]
    return jnp.concatenate(columns, axis=-1)


def solution(mesh):
    groups, dp, cores = mesh.shape["groups"], mesh.shape["dp"], mesh.shape["mp"]

    def run(hidden_states, passage_states, down_weight, block_question, question_owner, decoder_states):
        lows = max(1, HEAD_DIM * dp // down_weight.shape[0])
        fine = Mesh(
            mesh.devices.reshape(groups, dp // (2 * lows), 2, lows, cores),
            ("groups", "high", "side", "low", "mp"),
        )
        split = ("groups", "high", "side", "low")
        placed = (
            P(split, None, "mp"),
            P(split, None, None),
            P(("high", "side", "low"), "mp"),
            P("groups", None),
            P("groups"),
            P(split, None, None),
        )
        return jax.shard_map(
            body, mesh=fine, in_specs=placed, out_specs=P(split, None, None), check_vma=False
        )(hidden_states, passage_states, down_weight, block_question, question_owner, decoder_states)

    return run
```

```python
import functools

import jax
import jax.numpy as jnp
from jax import lax
from jax.experimental import pallas as pl
from jax.experimental.pallas import tpu as pltpu
from jax.sharding import Mesh, PartitionSpec as P

HEAD_DIM = 64
EMPTY = -3e38
VMEM_LIMIT = 40 * 1024 * 1024
SWAP = [(0, 1), (1, 0)]
CROSS = [(0, 3), (3, 0), (1, 2), (2, 1)]


def head_pick(tall, query_len):
    lanes = tall.shape[1]
    lane_head = lax.broadcasted_iota(jnp.int32, (query_len, lanes), 1) // HEAD_DIM
    picked = jnp.zeros((query_len, lanes), jnp.float32)
    for head in range(lanes // HEAD_DIM):
        picked = jnp.where(lane_head == head, tall[head * query_len : (head + 1) * query_len, :], picked)
    return picked


def project_kernel(flag_ref, *refs, jobs, sends):
    keep_ref, *send_refs = refs[-1 - len(sends) :]
    slots = [(ref, at) for ref in send_refs for at in range(ref.shape[0])]
    core, same = flag_ref[0], flag_ref[1]
    half = keep_ref.shape[2]
    for at, (rows_of, blocks_of) in enumerate(jobs):
        if len(blocks_of) == 1:
            whole = refs[blocks_of[0]]
            keep = whole[pl.ds(pl.multiple_of(core * half, half), half), :]
            send = whole[pl.ds(pl.multiple_of((1 - core) * half, half), half), :]
        else:
            first, second = (refs[block][...] for block in blocks_of)
            keep = jnp.where(same == 1, first, second)
            send = jnp.where(same == 1, second, first)
        product = lax.dot_general(
            refs[rows_of][...],
            jnp.concatenate([keep, send], axis=0),
            (((1,), (1,)), ((), ())),
            preferred_element_type=jnp.float32,
        )
        keep_ref[at] = product[:, :half]
        send_ref, slot = slots[at]
        send_ref[slot] = product[:, half:]


def attend_kernel(place_ref, spot_ref, query_ref, *refs, pieces):
    *refs, own_ref, partner_ref, out_ref, key_ref = refs
    residuals = own_ref, partner_ref
    partner_queries = own_ref.shape[0]
    query_len, held = query_ref.shape[1:]
    block_len = key_ref.shape[1]
    heads = held // HEAD_DIM
    tall = heads * query_len
    out_ref[:, :, :held] = jnp.zeros(out_ref.shape[:2] + (held,), jnp.float32)
    ext_row = lax.broadcasted_iota(jnp.int32, out_ref.shape[:2] + (tall,), 1)
    out_ref[:, :, held:] = jnp.where(ext_row == 0, EMPTY, 0.0)
    row_head = lax.broadcasted_iota(jnp.int32, (tall, held), 0) // query_len
    lane_head = lax.broadcasted_iota(jnp.int32, (tall, held), 1) // HEAD_DIM
    diagonal = row_head == lane_head
    square = lax.broadcasted_iota(jnp.int32, (tall, tall), 0) == lax.broadcasted_iota(jnp.int32, (tall, tall), 1)
    ext = lax.broadcasted_iota(jnp.int32, (query_len, tall), 0)
    blocks = key_ref.shape[0] // 2
    for source, kept, sent, spot in pieces:
        keep, other = (refs[summand].at[piece] for summand, piece in (kept, sent))
        residual = residuals[source]
        span = keep.shape[1]
        lanes = pl.ds(pl.multiple_of(spot_ref[spot] * span, span), span)
        for block in range(blocks):
            rows = slice(block * block_len, (block + 1) * block_len)
            key_ref[source * blocks + block, :, lanes] = (
                residual[rows, lanes].astype(jnp.float32) + (keep[rows, :] + other[rows, :])
            ).astype(jnp.bfloat16)
    places, scores, tops = [], [], []
    for at in range(key_ref.shape[0]):
        place = place_ref[at]
        first = pl.multiple_of(partner_queries + place // 2 * query_len, query_len)
        query = jnp.where(place % 2 == 0, query_ref[place // 2], partner_ref[pl.ds(first, query_len), :])
        query = jnp.concatenate([query] * heads, axis=0)
        query = jnp.where(diagonal, query, jnp.zeros_like(query))
        score = lax.dot_general(
            query, key_ref[at], (((1,), (1,)), ((), ())), preferred_element_type=jnp.float32
        )
        places.append(place)
        scores.append(score)
        tops.append(jnp.max(score, axis=1, keepdims=True))
    for at, place in enumerate(places):
        top = tops[at]
        for other_at, other_place in enumerate(places):
            if other_at != at:
                top = jnp.maximum(top, jnp.where(other_place == place, tops[other_at], EMPTY))
        weights = jnp.exp(scores[at] - top)
        total = jnp.sum(weights, axis=1, keepdims=True)
        blend = lax.dot_general(
            weights.astype(jnp.bfloat16), key_ref[at], (((1,), (0,)), ((), ())),
            preferred_element_type=jnp.float32,
        )
        top_row = jnp.sum(jnp.where(square, top, 0.0), axis=0, keepdims=True)
        total_row = jnp.sum(jnp.where(square, total, 0.0), axis=0, keepdims=True)
        out_ref[place, :, :held] = out_ref[place, :, :held] + head_pick(blend, query_len)
        before = out_ref[place, :, held:]
        out_ref[place, :, held:] = jnp.where(
            ext == 0, top_row, jnp.where(ext == 1, before + total_row, 0.0)
        )


def merge_kernel(*refs):
    out_ref = refs[-1]
    parts = refs[:-1]
    query_len, held = out_ref.shape[1:]
    tall = held // HEAD_DIM * query_len
    square = lax.broadcasted_iota(jnp.int32, (tall, tall), 0) == lax.broadcasted_iota(jnp.int32, (tall, tall), 1)

    def over(start, step):
        for part in parts:
            start = lax.fori_loop(
                0, part.shape[0], functools.partial(step, part), start, unroll=part.shape[0] <= 8
            )
        return start

    for slot in range(out_ref.shape[0]):
        def top_step(part, at, top):
            return jnp.maximum(top, part[at, slot, 0:1, held:])

        def total_step(part, at, total):
            return total + jnp.exp(part[at, slot, 0:1, held:] - top) * part[at, slot, 1:2, held:]

        def blend_step(part, at, blend):
            share = jnp.exp(part[at, slot, 0:1, held:] - top) / total
            column = jnp.sum(jnp.where(square, share, 0.0), axis=1, keepdims=True)
            spread = head_pick(jnp.broadcast_to(column, (tall, held)), query_len)
            return blend + spread * part[at, slot, :, :held]

        top = over(jnp.full((1, tall), EMPTY, jnp.float32), top_step)
        total = over(jnp.zeros((1, tall), jnp.float32), total_step)
        blend = over(jnp.zeros((query_len, held), jnp.float32), blend_step)
        out_ref[slot] = blend.astype(out_ref.dtype)


def in_vmem(count):
    return [pl.BlockSpec(memory_space=pltpu.VMEM)] * count


def in_smem(count):
    return [pl.BlockSpec(memory_space=pltpu.SMEM)] * count


def project(flags, operands, jobs, sends, name):
    rows, units = operands[0].shape
    half = min(operand.shape[0] for operand in operands)
    shapes = [jax.ShapeDtypeStruct((count, rows, half), jnp.float32) for count in [len(jobs)] + sends]
    return pl.pallas_call(
        functools.partial(project_kernel, jobs=jobs, sends=sends),
        out_shape=shapes,
        in_specs=in_smem(1) + in_vmem(len(operands)),
        out_specs=in_vmem(len(shapes)),
        compiler_params=pltpu.CompilerParams(vmem_limit_bytes=VMEM_LIMIT),
        cost_estimate=pl.CostEstimate(flops=1, bytes_accessed=1, transcendentals=0),
        name=name,
    )(flags, *operands)


def body(hidden_states, passage_states, down_weight, block_question, question_owner, decoder_states):
    blocks, block_len, units = hidden_states.shape
    width = passage_states.shape[2]
    query_len = decoder_states.shape[1]
    highs, lows, cores = lax.axis_size("high"), lax.axis_size("low"), lax.axis_size("mp")
    group, high, side, low, core = (lax.axis_index(name) for name in ("groups", "high", "side", "low", "mp"))
    shard = down_weight.shape[0]
    stride = lows * shard
    held = width // 2 // cores
    heads = held // HEAD_DIM
    members = highs * lows
    slot_total = question_owner.shape[0]
    rows = blocks * block_len
    lined = highs == 4 and lows == 1 and stride % (cores * 128) == 0
    span = stride // cores if lined else stride
    spans = held // span

    def features(array, of_side):
        if lined:
            starts = [(at * 2 + of_side) * stride + core * span for at in range(spans)]
        else:
            starts = [((core * spans + at) * 2 + of_side) * stride for at in range(spans)]
        taken = [lax.dynamic_slice_in_dim(array, start, span, axis=array.ndim - 1) for start in starts]
        return jnp.concatenate(taken, axis=-1)

    def shifted(array, shift):
        return lax.ppermute(array, "high", [(at, (at + shift) % highs) for at in range(highs)])

    hidden = hidden_states.reshape(rows, units)
    partner_hidden = lax.ppermute(hidden, "side", SWAP)
    queries = jnp.concatenate([features(decoder_states, side), features(decoder_states, 1 - side)], axis=0)[None]
    passages = passage_states.reshape(rows, width)
    own_residual = features(passages, side)
    leaving = features(passages, 1 - side)

    if lined:
        half = shard // 2
        sent = lax.dynamic_slice_in_dim(down_weight, group * half, half, axis=0)
        below = shifted(sent, 1)
        above = shifted(sent, -1)
        opposite = shifted(below, 1)
        queries, _ = lax.optimization_barrier((queries, opposite))
        queries = jnp.concatenate([queries] + [shifted(queries, -ahead) for ahead in range(1, highs)], axis=0)
        weights = [down_weight]
        for piece in (above, below, opposite):
            weights += [piece, lax.ppermute(piece, "groups", SWAP)]
        flags = jnp.stack([core, (group == core).astype(core.dtype)])
        blocks_of = [(0,), (1, 2), (3, 4), (5, 6)]
        spots = lax.rem(high + jnp.array([0, 1, 3, 2], jnp.int32), highs)

        def jobs_of(rows_of, chosen, count):
            return [(rows_of, tuple(at + count for at in blocks_of[one])) for one in chosen]

        kept, *away = project(flags, [hidden] + weights[:5], jobs_of(0, (0, 1, 2), 1), [3], "project_own")
        flags, kept, away = lax.optimization_barrier((flags, kept, away))
        late_kept, *late_away = project(
            flags,
            [hidden, partner_hidden] + weights,
            jobs_of(0, (3,), 2) + jobs_of(1, range(4), 2),
            [2, 2, 1],
            "project_rest",
        )
        others = [lax.ppermute(piece, "mp", SWAP) for piece in away + late_away]
        summands = [kept, late_kept] + others
        pieces = [(0, (0, at), (2, at), at) for at in range(3)] + [(0, (1, 0), (3, 0), 3)]
        pieces += [(1, (1, 1 + at), (3 + (1 + at) // 2, (1 + at) % 2), at) for at in range(4)]
        origin = high
    else:
        queries = lax.all_gather(queries, ("high", "low"), axis=0, tiled=True)
        weight = lax.all_gather(down_weight, ("high", "low"), axis=0, tiled=True)
        weight = jnp.where(core == 0, weight, jnp.roll(weight, held, axis=0))
        spots = jnp.zeros((1,), jnp.int32)
        summands, pieces = [], []
        for source, flat in enumerate((hidden, partner_hidden)):
            kept, away = (
                lax.dot_general(flat, part, (((1,), (1,)), ((), ())), preferred_element_type=jnp.float32)[None]
                for part in (weight[:held], weight[held:])
            )
            summands += [kept, lax.ppermute(away, "mp", SWAP)]
            pieces.append((source, (2 * source, 0), (2 * source + 1, 0), 0))
        origin = 0

    questions = block_question[:, 0]
    question_ids = jnp.arange(slot_total, dtype=jnp.int32)
    owners = jnp.sum(jnp.where(questions[:, None] == question_ids[None, :], question_owner[None, :], 0), axis=1)
    owner_high, owner_side, owner_low = owners // (2 * lows), (owners // lows) % 2, owners % lows
    owner_high = lax.rem(owner_high - origin + highs, highs)
    owner_place = (owner_high * lows + owner_low) * 2 + (owner_side != side)
    own_at = ((high * 2 + side) * lows + low) * blocks
    partner_at = ((high * 2 + 1 - side) * lows + low) * blocks
    places = jnp.concatenate(
        [lax.dynamic_slice_in_dim(owner_place, at, blocks) for at in (own_at, partner_at)]
    )

    leaving = jnp.concatenate([leaving, queries[:, 1].reshape(-1, held)], axis=0)
    partner = lax.ppermute(leaving, "side", SWAP)
    operands = summands + [own_residual, partner]
    partials = pl.pallas_call(
        functools.partial(attend_kernel, pieces=pieces),
        out_shape=jax.ShapeDtypeStruct((2 * members, query_len, held + heads * query_len), jnp.float32),
        in_specs=in_smem(2) + in_vmem(1 + len(operands)),
        out_specs=pl.BlockSpec(memory_space=pltpu.VMEM),
        scratch_shapes=[pltpu.VMEM((2 * blocks, block_len, held), jnp.bfloat16)],
        compiler_params=pltpu.CompilerParams(vmem_limit_bytes=VMEM_LIMIT),
        name="attend",
    )(places, spots, queries[:, 0], *operands)
    partials = partials.reshape((members, 2) + partials.shape[1:])

    if lined:
        received = [partials[0:1]] + [shifted(partials[ahead : ahead + 1], ahead) for ahead in range(1, highs)]
    else:
        received = [lax.all_to_all(partials, ("high", "low"), split_axis=0, concat_axis=0, tiled=True)]
    merged = pl.pallas_call(
        merge_kernel,
        out_shape=jax.ShapeDtypeStruct((2, query_len, held), decoder_states.dtype),
        in_specs=in_vmem(len(received)),
        out_specs=pl.BlockSpec(memory_space=pltpu.VMEM),
        compiler_params=pltpu.CompilerParams(vmem_limit_bytes=VMEM_LIMIT),
        name="merge",
    )(*received)

    mine, away = merged[0:1], merged[1:2]
    by_core = lax.ppermute(mine, "mp", SWAP)
    by_side = lax.ppermute(away, "side", SWAP)
    by_both = lax.ppermute(away, ("side", "mp"), CROSS)
    near = [jnp.where(core == at, mine, by_core) for at in range(cores)]
    far = [jnp.where(core == at, by_side, by_both) for at in range(cores)]
    sides = [[jnp.where(side == at, near[of], far[of]) for of in range(cores)] for at in range(2)]
    columns = []
    if lined:
        order = [(at, of_side, of) for at in range(spans) for of_side in range(2) for of in range(cores)]
    else:
        order = [(at, of_side, of) for of in range(cores) for at in range(spans) for of_side in range(2)]
    for at, of_side, of in order:
        columns.append(sides[of_side][of][:, :, at * span : (at + 1) * span])
    return jnp.concatenate(columns, axis=-1)


def solution(mesh):
    groups, dp, cores = mesh.shape["groups"], mesh.shape["dp"], mesh.shape["mp"]

    def run(hidden_states, passage_states, down_weight, block_question, question_owner, decoder_states):
        lows = max(1, HEAD_DIM * dp // down_weight.shape[0])
        fine = Mesh(
            mesh.devices.reshape(groups, dp // (2 * lows), 2, lows, cores),
            ("groups", "high", "side", "low", "mp"),
        )
        split = ("groups", "high", "side", "low")
        placed = (
            P(split, None, "mp"),
            P(split, None, None),
            P(("high", "side", "low"), "mp"),
            P("groups", None),
            P("groups"),
            P(split, None, None),
        )
        return jax.shard_map(
            body, mesh=fine, in_specs=placed, out_specs=P(split, None, None), check_vma=False
        )(hidden_states, passage_states, down_weight, block_question, question_owner, decoder_states)

    return run
```

```python
import functools

import jax
import jax.numpy as jnp
from jax import lax
from jax.experimental import pallas as pl
from jax.experimental.pallas import tpu as pltpu
from jax.sharding import Mesh, PartitionSpec as P

HEAD_DIM = 64
EMPTY = -(2.0**127)
CHUNKS = 2
VMEM_LIMIT = 40 * 1024 * 1024
SWAP = [(0, 1), (1, 0)]
CROSS = [(0, 3), (3, 0), (1, 2), (2, 1)]


def head_pick(tall, query_len):
    lanes = tall.shape[1]
    lane_head = lax.broadcasted_iota(jnp.int32, (query_len, lanes), 1) // HEAD_DIM
    picked = jnp.zeros((query_len, lanes), jnp.float32)
    for head in range(lanes // HEAD_DIM):
        picked = jnp.where(lane_head == head, tall[head * query_len : (head + 1) * query_len, :], picked)
    return picked


def project_kernel(flag_ref, *refs, jobs, sends):
    keep_ref, *send_refs = refs[-1 - len(sends) :]
    slots = [(ref, at) for ref in send_refs for at in range(ref.shape[0])]
    core, same = flag_ref[0], flag_ref[1]
    half = keep_ref.shape[2]
    for at, (rows_of, blocks_of) in enumerate(jobs):
        if len(blocks_of) == 1:
            whole = refs[blocks_of[0]]
            keep = whole[pl.ds(pl.multiple_of(core * half, half), half), :]
            send = whole[pl.ds(pl.multiple_of((1 - core) * half, half), half), :]
        else:
            parts = [refs[block][...] for block in blocks_of]
            first, second = (
                jnp.concatenate(part, axis=0) for part in (parts[: len(parts) // 2], parts[len(parts) // 2 :])
            )
            keep = jnp.where(same == 1, first, second)
            send = jnp.where(same == 1, second, first)
        product = lax.dot_general(
            refs[rows_of][...],
            jnp.concatenate([keep, send], axis=0),
            (((1,), (1,)), ((), ())),
            preferred_element_type=jnp.float32,
        )
        keep_ref[at] = product[:, :half]
        send_ref, slot = slots[at]
        send_ref[slot] = product[:, half:]


def attend_kernel(place_ref, spot_ref, query_ref, *refs, pieces):
    *refs, own_ref, partner_ref, packed_ref, key_ref, out_ref = refs
    residuals = own_ref, partner_ref
    partner_queries = own_ref.shape[0]
    query_len, held = query_ref.shape[1:]
    block_len = key_ref.shape[1]
    heads = held // HEAD_DIM
    tall = heads * query_len
    out_ref[:, :, :held] = jnp.zeros(out_ref.shape[:2] + (held,), jnp.float32)
    ext_row = lax.broadcasted_iota(jnp.int32, out_ref.shape[:2] + (tall,), 1)
    out_ref[:, :, held:] = jnp.where(ext_row == 0, EMPTY, 0.0)
    row_head = lax.broadcasted_iota(jnp.int32, (tall, held), 0) // query_len
    lane_head = lax.broadcasted_iota(jnp.int32, (tall, held), 1) // HEAD_DIM
    diagonal = row_head == lane_head
    square = lax.broadcasted_iota(jnp.int32, (tall, tall), 0) == lax.broadcasted_iota(jnp.int32, (tall, tall), 1)
    ext = lax.broadcasted_iota(jnp.int32, (query_len, tall), 0)
    blocks = key_ref.shape[0] // 2
    for source, kept, sent, spot in pieces:
        keep, other = (refs[summand].at[piece] for summand, piece in (kept, sent))
        residual = residuals[source]
        span = keep.shape[1]
        lanes = pl.ds(pl.multiple_of(spot_ref[spot] * span, span), span)
        for block in range(blocks):
            rows = slice(block * block_len, (block + 1) * block_len)
            key_ref[source * blocks + block, :, lanes] = (
                residual[rows, lanes].astype(jnp.float32) + (keep[rows, :] + other[rows, :])
            ).astype(jnp.bfloat16)
    places, scores, tops = [], [], []
    for at in range(key_ref.shape[0]):
        place = place_ref[at]
        first = pl.multiple_of(partner_queries + place // 2 * query_len, query_len)
        query = jnp.where(place % 2 == 0, query_ref[place // 2], partner_ref[pl.ds(first, query_len), :])
        query = jnp.concatenate([query] * heads, axis=0)
        query = jnp.where(diagonal, query, jnp.zeros_like(query))
        score = lax.dot_general(
            query, key_ref[at], (((1,), (1,)), ((), ())), preferred_element_type=jnp.float32
        )
        places.append(place)
        scores.append(score)
        tops.append(jnp.max(score, axis=1, keepdims=True))
    for at, place in enumerate(places):
        top = tops[at]
        for other_at, other_place in enumerate(places):
            if other_at != at:
                top = jnp.maximum(top, jnp.where(other_place == place, tops[other_at], EMPTY))
        weights = jnp.exp(scores[at] - top)
        total = jnp.sum(weights, axis=1, keepdims=True)
        blend = lax.dot_general(
            weights.astype(jnp.bfloat16), key_ref[at], (((1,), (0,)), ((), ())),
            preferred_element_type=jnp.float32,
        )
        top_row = jnp.sum(jnp.where(square, top, 0.0), axis=0, keepdims=True)
        total_row = jnp.sum(jnp.where(square, total, 0.0), axis=0, keepdims=True)
        out_ref[place, :, :held] = out_ref[place, :, :held] + head_pick(blend, query_len)
        before = out_ref[place, :, held:]
        out_ref[place, :, held:] = jnp.where(
            ext == 0, top_row, jnp.where(ext == 1, before + total_row, 0.0)
        )
    packed_ref[:, :, :held] = out_ref[:, :, :held].astype(jnp.bfloat16)
    rest = out_ref[:, 0:2, held:]
    for part in range(3):
        rounded = rest.astype(jnp.bfloat16)
        rest = rest - rounded.astype(jnp.float32)
        packed_ref[:, 2 * part : 2 * part + 2, held:] = rounded
    packed_ref[:, 6:, held:] = jnp.zeros_like(packed_ref[:, 6:, held:])


def merge_kernel(*refs):
    out_ref = refs[-1]
    parts = refs[:-1]
    query_len, held = out_ref.shape[1:]
    tall = held // HEAD_DIM * query_len
    square = lax.broadcasted_iota(jnp.int32, (tall, tall), 0) == lax.broadcasted_iota(jnp.int32, (tall, tall), 1)

    def over(start, step):
        for part in parts:
            start = lax.fori_loop(
                0, part.shape[0], functools.partial(step, part), start, unroll=part.shape[0] <= 8
            )
        return start

    def row_of(part, at, slot, row):
        packed = part[at, slot, :, held:].astype(jnp.float32)
        return packed[row : row + 1] + packed[row + 2 : row + 3] + packed[row + 4 : row + 5]

    for slot in range(out_ref.shape[0]):
        def top_step(part, at, top):
            return jnp.maximum(top, row_of(part, at, slot, 0))

        def total_step(part, at, total):
            return total + jnp.exp(row_of(part, at, slot, 0) - top) * row_of(part, at, slot, 1)

        def blend_step(part, at, blend):
            share = jnp.exp(row_of(part, at, slot, 0) - top) / total
            column = jnp.sum(jnp.where(square, share, 0.0), axis=1, keepdims=True)
            spread = head_pick(jnp.broadcast_to(column, (tall, held)), query_len)
            return blend + spread * part[at, slot, :, :held].astype(jnp.float32)

        top = over(jnp.full((1, tall), EMPTY, jnp.float32), top_step)
        total = over(jnp.zeros((1, tall), jnp.float32), total_step)
        blend = over(jnp.zeros((query_len, held), jnp.float32), blend_step)
        out_ref[slot] = blend.astype(out_ref.dtype)


def assemble_kernel(flag_ref, mine_ref, core_ref, side_ref, both_ref, out_ref, *, order, span):
    side, core = flag_ref[0], flag_ref[1]
    mine, by_core, by_side, by_both = (ref[0] for ref in (mine_ref, core_ref, side_ref, both_ref))
    taken = {}
    for of_side in range(2):
        for of in range(2):
            near = jnp.where(core == of, mine, by_core)
            far = jnp.where(core == of, by_side, by_both)
            taken[of_side, of] = jnp.where(side == of_side, near, far)
    out_ref[0] = jnp.concatenate(
        [taken[of_side, of][:, first : first + span] for of_side, of, first in order], axis=1
    )


def in_vmem(count):
    return [pl.BlockSpec(memory_space=pltpu.VMEM)] * count


def in_smem(count):
    return [pl.BlockSpec(memory_space=pltpu.SMEM)] * count


def project(flags, operands, jobs, sends, flops, name):
    rows, units = operands[0].shape
    half = operands[-1].shape[0] * CHUNKS
    shapes = [jax.ShapeDtypeStruct((count, rows, half), jnp.float32) for count in [len(jobs)] + sends]
    return pl.pallas_call(
        functools.partial(project_kernel, jobs=jobs, sends=sends),
        out_shape=shapes,
        in_specs=in_smem(1) + in_vmem(len(operands)),
        out_specs=in_vmem(len(shapes)),
        compiler_params=pltpu.CompilerParams(vmem_limit_bytes=VMEM_LIMIT),
        cost_estimate=pl.CostEstimate(flops=flops, bytes_accessed=1, transcendentals=0),
        name=name,
    )(flags, *operands)


def after(array, earlier):
    return lax.optimization_barrier((array, *earlier))[0] if earlier else array


def body(hidden_states, passage_states, down_weight, block_question, question_owner, decoder_states):
    blocks, block_len, units = hidden_states.shape
    width = passage_states.shape[2]
    query_len = decoder_states.shape[1]
    highs, lows, cores = lax.axis_size("high"), lax.axis_size("low"), lax.axis_size("mp")
    group, high, side, low, core = (lax.axis_index(name) for name in ("groups", "high", "side", "low", "mp"))
    shard = down_weight.shape[0]
    stride = lows * shard
    held = width // 2 // cores
    heads = held // HEAD_DIM
    members = highs * lows
    slot_total = question_owner.shape[0]
    rows = blocks * block_len
    lined = highs == 4 and lows == 1 and stride % (cores * 128) == 0
    span = stride // cores if lined else stride
    spans = held // span

    def features(array, of_side):
        if lined:
            starts = [(at * 2 + of_side) * stride + core * span for at in range(spans)]
        else:
            starts = [((core * spans + at) * 2 + of_side) * stride for at in range(spans)]
        taken = [lax.dynamic_slice_in_dim(array, start, span, axis=array.ndim - 1) for start in starts]
        return jnp.concatenate(taken, axis=-1)

    def shifted(array, shift):
        return lax.ppermute(array, "high", [(at, (at + shift) % highs) for at in range(highs)])

    hidden = hidden_states.reshape(rows, units)
    partner_hidden = lax.ppermute(hidden, "side", SWAP)
    queries = jnp.concatenate([features(decoder_states, side), features(decoder_states, 1 - side)], axis=0)[None]
    passages = passage_states.reshape(rows, width)
    own_residual = features(passages, side)
    leaving = features(passages, 1 - side)

    if lined:
        half = shard // 2
        chunk = half // CHUNKS
        sent = [
            lax.dynamic_slice_in_dim(down_weight, group * half + at * chunk, chunk, axis=0) for at in range(CHUNKS)
        ]
        below, above, opposite = [], [], []
        for at in range(CHUNKS):
            below.append(shifted(after(sent[at], below[-1:]), 1))
            above.append(shifted(after(sent[at], above[-1:]), -1))
        opposite.append(shifted(after(below[0], below[-1:]), 1))
        opposite.append(shifted(after(below[1], above[-1:]), 1))
        swapped = []
        for at, piece in enumerate([below[0], above[0], below[1], above[1]] + opposite):
            swapped.append(lax.ppermute(after(piece, swapped[max(at - 2, 0) : max(at - 1, 0)]), "groups", SWAP))
        weights = [down_weight] + above + swapped[1:4:2] + below + swapped[0:4:2] + opposite + swapped[4:]
        queries = after(queries, opposite)
        queries = jnp.concatenate([queries] + [shifted(queries, -ahead) for ahead in range(1, highs)], axis=0)
        flags = after(jnp.stack([core, (group == core).astype(core.dtype)]), opposite)
        blocks_of = [(0,)] + [tuple(range(1 + at * 2 * CHUNKS, 1 + (at + 1) * 2 * CHUNKS)) for at in range(3)]
        spots = lax.rem(high + jnp.array([0, 1, 3, 2], jnp.int32), highs)

        def jobs_of(rows_of, chosen, count):
            return [(rows_of, tuple(at + count for at in blocks_of[one])) for one in chosen]

        kept, *away = project(flags, [hidden] + weights[: 1 + 4 * CHUNKS], jobs_of(0, (0, 1, 2), 1), [3], 12 * rows * half * units, "project_own")
        flags, kept, away = lax.optimization_barrier((flags, kept, away))
        late_kept, *late_away = project(
            flags,
            [hidden, partner_hidden] + weights,
            jobs_of(0, (3,), 2) + jobs_of(1, range(4), 2),
            [2, 2, 1],
            1,
            "project_rest",
        )
        others = [lax.ppermute(piece, "mp", SWAP) for piece in away + late_away]
        summands = [kept, late_kept] + others
        pieces = [(0, (0, at), (2, at), at) for at in range(3)] + [(0, (1, 0), (3, 0), 3)]
        pieces += [(1, (1, 1 + at), (3 + (1 + at) // 2, (1 + at) % 2), at) for at in range(4)]
        origin = high
    else:
        queries = lax.all_gather(queries, ("high", "low"), axis=0, tiled=True)
        weight = lax.all_gather(down_weight, ("high", "low"), axis=0, tiled=True)
        weight = jnp.where(core == 0, weight, jnp.roll(weight, held, axis=0))
        spots = jnp.zeros((1,), jnp.int32)
        summands, pieces = [], []
        for source, flat in enumerate((hidden, partner_hidden)):
            kept, away = (
                lax.dot_general(flat, part, (((1,), (1,)), ((), ())), preferred_element_type=jnp.float32)[None]
                for part in (weight[:held], weight[held:])
            )
            summands += [kept, lax.ppermute(away, "mp", SWAP)]
            pieces.append((source, (2 * source, 0), (2 * source + 1, 0), 0))
        origin = 0

    questions = block_question[:, 0]
    question_ids = jnp.arange(slot_total, dtype=jnp.int32)
    owners = jnp.sum(jnp.where(questions[:, None] == question_ids[None, :], question_owner[None, :], 0), axis=1)
    owner_high, owner_side, owner_low = owners // (2 * lows), (owners // lows) % 2, owners % lows
    owner_high = lax.rem(owner_high - origin + highs, highs)
    owner_place = (owner_high * lows + owner_low) * 2 + (owner_side != side)
    own_at = ((high * 2 + side) * lows + low) * blocks
    partner_at = ((high * 2 + 1 - side) * lows + low) * blocks
    places = jnp.concatenate(
        [lax.dynamic_slice_in_dim(owner_place, at, blocks) for at in (own_at, partner_at)]
    )

    leaving = jnp.concatenate([leaving, queries[:, 1].reshape(-1, held)], axis=0)
    partner = lax.ppermute(leaving, "side", SWAP)
    packed = (2 * members, query_len, held + heads * query_len)
    operands = summands + [own_residual, partner]
    partials = pl.pallas_call(
        functools.partial(attend_kernel, pieces=pieces),
        out_shape=jax.ShapeDtypeStruct(packed, jnp.bfloat16),
        in_specs=in_smem(2) + in_vmem(1 + len(operands)),
        out_specs=pl.BlockSpec(memory_space=pltpu.VMEM),
        scratch_shapes=[
            pltpu.VMEM((2 * blocks, block_len, held), jnp.bfloat16),
            pltpu.VMEM(packed, jnp.float32),
        ],
        compiler_params=pltpu.CompilerParams(vmem_limit_bytes=VMEM_LIMIT),
        name="attend",
    )(places, spots, queries[:, 0], *operands)
    partials = partials.reshape((members, 2) + partials.shape[1:])

    if lined:
        received = [partials[0:1]] + [shifted(partials[ahead : ahead + 1], ahead) for ahead in range(1, highs)]
    else:
        received = [lax.all_to_all(partials, ("high", "low"), split_axis=0, concat_axis=0, tiled=True)]
    merged = pl.pallas_call(
        merge_kernel,
        out_shape=jax.ShapeDtypeStruct((2, query_len, held), decoder_states.dtype),
        in_specs=in_vmem(len(received)),
        out_specs=pl.BlockSpec(memory_space=pltpu.VMEM),
        compiler_params=pltpu.CompilerParams(vmem_limit_bytes=VMEM_LIMIT),
        name="merge",
    )(*received)

    mine, away = merged[0:1], merged[1:2]
    by_core = lax.ppermute(mine, "mp", SWAP)
    by_side = lax.ppermute(away, "side", SWAP)
    by_both = lax.ppermute(away, ("side", "mp"), CROSS)
    if lined:
        order = [(at, of_side, of) for at in range(spans) for of_side in range(2) for of in range(cores)]
    else:
        order = [(at, of_side, of) for of in range(cores) for at in range(spans) for of_side in range(2)]
    flags = jnp.stack([side, core])
    order = [(of_side, of, at * span) for at, of_side, of in order]
    return pl.pallas_call(
        functools.partial(assemble_kernel, order=order, span=span),
        out_shape=jax.ShapeDtypeStruct((1, query_len, width), decoder_states.dtype),
        in_specs=in_smem(1) + in_vmem(4),
        out_specs=pl.BlockSpec(memory_space=pltpu.VMEM),
        compiler_params=pltpu.CompilerParams(vmem_limit_bytes=VMEM_LIMIT),
        name="assemble",
    )(flags, mine, by_core, by_side, by_both)


def solution(mesh):
    groups, dp, cores = mesh.shape["groups"], mesh.shape["dp"], mesh.shape["mp"]

    def run(hidden_states, passage_states, down_weight, block_question, question_owner, decoder_states):
        lows = max(1, HEAD_DIM * dp // down_weight.shape[0])
        fine = Mesh(
            mesh.devices.reshape(groups, dp // (2 * lows), 2, lows, cores),
            ("groups", "high", "side", "low", "mp"),
        )
        split = ("groups", "high", "side", "low")
        placed = (
            P(split, None, "mp"),
            P(split, None, None),
            P(("high", "side", "low"), "mp"),
            P("groups", None),
            P("groups"),
            P(split, None, None),
        )
        return jax.shard_map(
            body, mesh=fine, in_specs=placed, out_specs=P(split, None, None), check_vma=False
        )(hidden_states, passage_states, down_weight, block_question, question_owner, decoder_states)

    return run
```

```python
import functools
import math

import jax
import jax.numpy as jnp
from jax import lax
from jax.experimental import pallas as pl
from jax.experimental.pallas import tpu as pltpu
from jax.sharding import Mesh, PartitionSpec as P

HEAD_DIM = 64
EMPTY = -3e38
FIRST_EIGHTHS = 4
VMEM_LIMIT = 22 * 1024 * 1024
SWAP = [(0, 1), (1, 0)]
CROSS = [(0, 3), (3, 0), (1, 2), (2, 1)]


def head_pick(tall, query_len):
    lanes = tall.shape[1]
    lane_head = lax.broadcasted_iota(jnp.int32, (query_len, lanes), 1) // HEAD_DIM
    picked = jnp.zeros((query_len, lanes), jnp.float32)
    for head in range(lanes // HEAD_DIM):
        picked = jnp.where(lane_head == head, tall[head * query_len : (head + 1) * query_len, :], picked)
    return picked


def project_kernel(flag_ref, *refs, jobs, sends):
    keep_ref, *send_refs = refs[-1 - len(sends) :]
    slots = [(ref, at) for ref in send_refs for at in range(ref.shape[0])]
    core, same = flag_ref[0], flag_ref[1]
    half = keep_ref.shape[2]
    for at, (rows_of, blocks_of) in enumerate(jobs):
        if len(blocks_of) == 1:
            whole = refs[blocks_of[0][0]]
            keep = whole[pl.ds(pl.multiple_of(core * half, half), half), :]
            send = whole[pl.ds(pl.multiple_of((1 - core) * half, half), half), :]
        else:
            parts = [refs[block][:length] for block, length in blocks_of]
            first, second = (
                jnp.concatenate(part, axis=0) for part in (parts[: len(parts) // 2], parts[len(parts) // 2 :])
            )
            keep = jnp.where(same == 1, first, second)
            send = jnp.where(same == 1, second, first)
        product = lax.dot_general(
            refs[rows_of][...],
            jnp.concatenate([keep, send], axis=0),
            (((1,), (1,)), ((), ())),
            preferred_element_type=jnp.float32,
        )
        keep_ref[at] = product[:, :half]
        send_ref, slot = slots[at]
        send_ref[slot] = product[:, half:]


def attend_kernel(place_ref, spot_ref, query_ref, *refs, pieces):
    *refs, own_ref, partner_ref, out_ref, key_ref = refs
    residuals = own_ref, partner_ref
    partner_queries = own_ref.shape[0]
    query_len, held = query_ref.shape[1:]
    block_len = key_ref.shape[1]
    heads = held // HEAD_DIM
    tall = heads * query_len
    out_ref[:, :, :held] = jnp.zeros(out_ref.shape[:2] + (held,), jnp.float32)
    ext_row = lax.broadcasted_iota(jnp.int32, out_ref.shape[:2] + (tall,), 1)
    out_ref[:, :, held:] = jnp.where(ext_row == 0, EMPTY, 0.0)
    row_head = lax.broadcasted_iota(jnp.int32, (tall, held), 0) // query_len
    lane_head = lax.broadcasted_iota(jnp.int32, (tall, held), 1) // HEAD_DIM
    diagonal = row_head == lane_head
    square = lax.broadcasted_iota(jnp.int32, (tall, tall), 0) == lax.broadcasted_iota(jnp.int32, (tall, tall), 1)
    ext = lax.broadcasted_iota(jnp.int32, (query_len, tall), 0)
    blocks = key_ref.shape[0] // 2
    for source, kept, sent, spot in pieces:
        keep, other = (refs[summand].at[piece] for summand, piece in (kept, sent))
        residual = residuals[source]
        span = keep.shape[1]
        lanes, given = (pl.ds(pl.multiple_of(spot_ref[of, spot], 128), span) for of in (1, source))
        for block in range(blocks):
            rows = slice(block * block_len, (block + 1) * block_len)
            key_ref[source * blocks + block, :, lanes] = (
                residual[rows, given].astype(jnp.float32) + (keep[rows, :] + other[rows, :])
            ).astype(jnp.bfloat16)
    places, scores, tops = [], [], []
    for at in range(key_ref.shape[0]):
        place = place_ref[at]
        first = pl.multiple_of(partner_queries + place // 2 * query_len, query_len)
        query = jnp.where(place % 2 == 0, query_ref[place // 2], partner_ref[pl.ds(first, query_len), :])
        query = jnp.concatenate([query] * heads, axis=0)
        query = jnp.where(diagonal, query, jnp.zeros_like(query))
        score = lax.dot_general(
            query, key_ref[at], (((1,), (1,)), ((), ())), preferred_element_type=jnp.float32
        )
        places.append(place)
        scores.append(score)
        tops.append(jnp.max(score, axis=1, keepdims=True))
    for at, place in enumerate(places):
        top = tops[at]
        for other_at, other_place in enumerate(places):
            if other_at != at:
                top = jnp.maximum(top, jnp.where(other_place == place, tops[other_at], EMPTY))
        weights = jnp.exp(scores[at] - top)
        total = jnp.sum(weights, axis=1, keepdims=True)
        blend = lax.dot_general(
            weights.astype(jnp.bfloat16), key_ref[at], (((1,), (0,)), ((), ())),
            preferred_element_type=jnp.float32,
        )
        top_row = jnp.sum(jnp.where(square, top, 0.0), axis=0, keepdims=True)
        total_row = jnp.sum(jnp.where(square, total, 0.0), axis=0, keepdims=True)
        out_ref[place, :, :held] = out_ref[place, :, :held] + head_pick(blend, query_len)
        before = out_ref[place, :, held:]
        out_ref[place, :, held:] = jnp.where(
            ext == 0, top_row, jnp.where(ext == 1, before + total_row, 0.0)
        )


def merge_kernel(*refs):
    out_ref = refs[-1]
    parts = refs[:-1]
    query_len, held = out_ref.shape[1:]
    tall = held // HEAD_DIM * query_len
    square = lax.broadcasted_iota(jnp.int32, (tall, tall), 0) == lax.broadcasted_iota(jnp.int32, (tall, tall), 1)

    def over(start, step):
        for part in parts:
            start = lax.fori_loop(
                0, part.shape[0], functools.partial(step, part), start, unroll=part.shape[0] <= 8
            )
        return start

    def row_of(part, at, slot, row):
        return part[at, slot, row : row + 1, held:]

    for slot in range(out_ref.shape[0]):
        def top_step(part, at, top):
            return jnp.maximum(top, row_of(part, at, slot, 0))

        def total_step(part, at, total):
            return total + jnp.exp(row_of(part, at, slot, 0) - top) * row_of(part, at, slot, 1)

        def blend_step(part, at, blend):
            share = jnp.exp(row_of(part, at, slot, 0) - top) / total
            column = jnp.sum(jnp.where(square, share, 0.0), axis=1, keepdims=True)
            spread = head_pick(jnp.broadcast_to(column, (tall, held)), query_len)
            return blend + spread * part[at, slot, :, :held]

        top = over(jnp.full((1, tall), EMPTY, jnp.float32), top_step)
        total = over(jnp.zeros((1, tall), jnp.float32), total_step)
        blend = over(jnp.zeros((query_len, held), jnp.float32), blend_step)
        out_ref[slot] = blend.astype(out_ref.dtype)


def assemble_kernel(flag_ref, mine_ref, core_ref, side_ref, both_ref, out_ref, *, order, span):
    side, core = flag_ref[0], flag_ref[1]
    mine, by_core, by_side, by_both = (ref[0] for ref in (mine_ref, core_ref, side_ref, both_ref))
    taken = {}
    for of_side in range(2):
        for of in range(2):
            near = jnp.where(core == of, mine, by_core)
            far = jnp.where(core == of, by_side, by_both)
            taken[of_side, of] = jnp.where(side == of_side, near, far)
    out_ref[0] = jnp.concatenate(
        [taken[of_side, of][:, first : first + span] for of_side, of, first in order], axis=1
    )


def in_vmem(count):
    return [pl.BlockSpec(memory_space=pltpu.VMEM)] * count


def in_smem(count):
    return [pl.BlockSpec(memory_space=pltpu.SMEM)] * count


def project(flags, operands, jobs, sends, half, flops, name):
    rows, units = operands[0].shape
    shapes = [jax.ShapeDtypeStruct((count, rows, half), jnp.float32) for count in [len(jobs)] + sends]
    return pl.pallas_call(
        functools.partial(project_kernel, jobs=jobs, sends=sends),
        out_shape=shapes,
        in_specs=in_smem(1) + in_vmem(len(operands)),
        out_specs=in_vmem(len(shapes)),
        compiler_params=pltpu.CompilerParams(vmem_limit_bytes=VMEM_LIMIT),
        cost_estimate=pl.CostEstimate(flops=flops, bytes_accessed=1, transcendentals=0),
        name=name,
    )(flags, *operands)


def after(array, earlier):
    return lax.optimization_barrier((array, *earlier))[0] if earlier else array


def with_rows(array, units):
    flat = array.reshape(-1, array.shape[-1])
    spread = jnp.concatenate([flat[at : at + 8] for at in range(0, flat.shape[0], 8)], axis=1)
    return jnp.pad(spread, ((0, 0), (0, units - spread.shape[1])))


def from_rows(spread, shape):
    pieces = [spread[:, at : at + shape[-1]] for at in range(0, math.prod(shape) // 8, shape[-1])]
    return jnp.concatenate(pieces, axis=0).reshape(shape)


def body(hidden_states, passage_states, down_weight, block_question, question_owner, decoder_states):
    blocks, block_len, units = hidden_states.shape
    width = passage_states.shape[2]
    query_len = decoder_states.shape[1]
    highs, lows, cores = lax.axis_size("high"), lax.axis_size("low"), lax.axis_size("mp")
    group, high, side, low, core = (lax.axis_index(name) for name in ("groups", "high", "side", "low", "mp"))
    shard = down_weight.shape[0]
    stride = lows * shard
    held = width // 2 // cores
    heads = held // HEAD_DIM
    members = highs * lows
    slot_total = question_owner.shape[0]
    rows = blocks * block_len
    lined = highs == 4 and lows == 1 and stride % (cores * 128) == 0
    span = stride // cores if lined else stride
    spans = held // span

    def features(array, of_side):
        if lined:
            starts = [(at * 2 + of_side) * stride + core * span for at in range(spans)]
        else:
            starts = [((core * spans + at) * 2 + of_side) * stride for at in range(spans)]
        taken = [lax.dynamic_slice_in_dim(array, start, span, axis=array.ndim - 1) for start in starts]
        return jnp.concatenate(taken, axis=-1)

    def shifted(array, shift):
        return lax.ppermute(array, "high", [(at, (at + shift) % highs) for at in range(highs)])

    hidden = hidden_states.reshape(rows, units)
    partner_hidden = lax.ppermute(hidden, "side", SWAP)
    queries = jnp.concatenate([features(decoder_states, side), features(decoder_states, 1 - side)], axis=0)[None]
    passages = passage_states.reshape(rows, width)
    leaving = features(passages, 1 - side)

    if lined:
        half = shard // 2
        lengths = [half * FIRST_EIGHTHS // 8, half - half * FIRST_EIGHTHS // 8]
        sent = [
            lax.dynamic_slice_in_dim(down_weight, group * half + first, length, axis=0)
            for first, length in zip((0, lengths[0]), lengths)
        ]
        sent[1] = jnp.concatenate([sent[1], with_rows(queries, units)], axis=0)
        below, above = [], []
        for at in range(2):
            below.append(shifted(after(sent[at], below[-1:]), 1))
            above.append(shifted(after(sent[at], above[-1:]), -1))
        opposite = [jnp.concatenate([shifted(after(below[0], below[1:]), 1), shifted(below[1], 1)], axis=0)]
        around = [from_rows(piece[-1][-8:], queries.shape) for piece in (above, opposite, below)]
        queries = jnp.concatenate([queries] + around, axis=0)
        swapped = []
        for at, piece in enumerate([below[0], above[0], below[1], above[1]] + opposite):
            swapped.append(lax.ppermute(after(piece, swapped[max(at - 2, 0) : max(at - 1, 0)]), "groups", SWAP))
        weights = [down_weight] + above + swapped[1:4:2] + below + swapped[0:4:2] + opposite + swapped[4:]
        flags = jnp.stack([core, (group == core).astype(core.dtype)])
        blocks_of = [[(2, shard)], list(zip(range(3, 7), 2 * lengths)), list(zip(range(7, 11), 2 * lengths))]
        spots = lax.rem(high + jnp.array([0, 1, 3, 2], jnp.int32), highs)
        spots = jnp.stack([(spots * 2 + side) * stride + core * span, spots * span])
        own_residual = passages

        kept, *away = project(
            flags,
            [hidden, partner_hidden] + weights[:9],
            [(source, blocks_of[at]) for source in range(2) for at in range(3)],
            [2, 2, 2],
            half,
            24 * rows * half * units,
            "project_near",
        )
        flags, kept, *away = lax.optimization_barrier((flags, kept, *away))
        late_kept, *late_away = project(
            flags,
            [hidden, partner_hidden] + weights[9:],
            [(source, [(2, half), (3, half)]) for source in range(2)],
            [2],
            half,
            1,
            "project_far",
        )
        others = [lax.ppermute(piece, "mp", SWAP) for piece in away + late_away]
        summands = [kept, late_kept] + others
        pieces = [(at // 3, (0, at), (2 + at // 2, at % 2), at % 3) for at in range(6)]
        pieces += [(source, (1, source), (5, source), 3) for source in range(2)]
        origin = high
    else:
        queries = lax.all_gather(queries, ("high", "low"), axis=0, tiled=True)
        weight = lax.all_gather(down_weight, ("high", "low"), axis=0, tiled=True)
        weight = jnp.where(core == 0, weight, jnp.roll(weight, held, axis=0))
        spots = jnp.zeros((2, 1), jnp.int32)
        own_residual = features(passages, side)
        summands, pieces = [], []
        for source, flat in enumerate((hidden, partner_hidden)):
            kept, away = (
                lax.dot_general(flat, part, (((1,), (1,)), ((), ())), preferred_element_type=jnp.float32)[None]
                for part in (weight[:held], weight[held:])
            )
            summands += [kept, lax.ppermute(away, "mp", SWAP)]
            pieces.append((source, (2 * source, 0), (2 * source + 1, 0), 0))
        origin = 0

    questions = block_question[:, 0]
    question_ids = jnp.arange(slot_total, dtype=jnp.int32)
    owners = jnp.sum(jnp.where(questions[:, None] == question_ids[None, :], question_owner[None, :], 0), axis=1)
    owner_high, owner_side, owner_low = owners // (2 * lows), (owners // lows) % 2, owners % lows
    owner_high = lax.rem(owner_high - origin + highs, highs)
    owner_place = (owner_high * lows + owner_low) * 2 + (owner_side != side)
    own_at = ((high * 2 + side) * lows + low) * blocks
    partner_at = ((high * 2 + 1 - side) * lows + low) * blocks
    places = jnp.concatenate(
        [lax.dynamic_slice_in_dim(owner_place, at, blocks) for at in (own_at, partner_at)]
    )

    leaving = jnp.concatenate([leaving, queries[:, 1].reshape(-1, held)], axis=0)
    partner = lax.ppermute(leaving, "side", SWAP)
    packed = (2 * members, query_len, held + heads * query_len)
    operands = summands + [own_residual, partner]
    partials = pl.pallas_call(
        functools.partial(attend_kernel, pieces=pieces),
        out_shape=jax.ShapeDtypeStruct(packed, jnp.float32),
        in_specs=in_smem(2) + in_vmem(1 + len(operands)),
        out_specs=pl.BlockSpec(memory_space=pltpu.VMEM),
        scratch_shapes=[pltpu.VMEM((2 * blocks, block_len, held), jnp.bfloat16)],
        compiler_params=pltpu.CompilerParams(vmem_limit_bytes=VMEM_LIMIT),
        name="attend",
    )(places, spots, queries[:, 0], *operands)
    partials = partials.reshape((members, 2) + partials.shape[1:])

    if lined:
        received = [partials[0:1]] + [shifted(partials[ahead : ahead + 1], ahead) for ahead in range(1, highs)]
    else:
        received = [lax.all_to_all(partials, ("high", "low"), split_axis=0, concat_axis=0, tiled=True)]
    merged = pl.pallas_call(
        merge_kernel,
        out_shape=jax.ShapeDtypeStruct((2, query_len, held), decoder_states.dtype),
        in_specs=in_vmem(len(received)),
        out_specs=pl.BlockSpec(memory_space=pltpu.VMEM),
        compiler_params=pltpu.CompilerParams(vmem_limit_bytes=VMEM_LIMIT),
        name="merge",
    )(*received)

    mine, away = merged[0:1], merged[1:2]
    by_core = lax.ppermute(mine, "mp", SWAP)
    by_side = lax.ppermute(away, "side", SWAP)
    by_both = lax.ppermute(away, ("side", "mp"), CROSS)
    if lined:
        order = [(at, of_side, of) for at in range(spans) for of_side in range(2) for of in range(cores)]
    else:
        order = [(at, of_side, of) for of in range(cores) for at in range(spans) for of_side in range(2)]
    flags = jnp.stack([side, core])
    order = [(of_side, of, at * span) for at, of_side, of in order]
    return pl.pallas_call(
        functools.partial(assemble_kernel, order=order, span=span),
        out_shape=jax.ShapeDtypeStruct((1, query_len, width), decoder_states.dtype),
        in_specs=in_smem(1) + in_vmem(4),
        out_specs=pl.BlockSpec(memory_space=pltpu.VMEM),
        compiler_params=pltpu.CompilerParams(vmem_limit_bytes=VMEM_LIMIT),
        name="assemble",
    )(flags, mine, by_core, by_side, by_both)


def solution(mesh):
    groups, dp, cores = mesh.shape["groups"], mesh.shape["dp"], mesh.shape["mp"]

    def run(hidden_states, passage_states, down_weight, block_question, question_owner, decoder_states):
        lows = max(1, HEAD_DIM * dp // down_weight.shape[0])
        fine = Mesh(
            mesh.devices.reshape(groups, dp // (2 * lows), 2, lows, cores),
            ("groups", "high", "side", "low", "mp"),
        )
        split = ("groups", "high", "side", "low")
        placed = (
            P(split, None, "mp"),
            P(split, None, None),
            P(("high", "side", "low"), "mp"),
            P("groups", None),
            P("groups"),
            P(split, None, None),
        )
        return jax.shard_map(
            body, mesh=fine, in_specs=placed, out_specs=P(split, None, None), check_vma=False
        )(hidden_states, passage_states, down_weight, block_question, question_owner, decoder_states)

    return run
```

```python
import functools
import math

import jax
import jax.numpy as jnp
from jax import lax
from jax.experimental import pallas as pl
from jax.experimental.pallas import tpu as pltpu
from jax.sharding import Mesh, PartitionSpec as P

HEAD_DIM = 64
EMPTY = -3e38
FIRST_EIGHTHS = 4
VMEM_LIMIT = 22 * 1024 * 1024
SWAP = [(0, 1), (1, 0)]
CROSS = [(0, 3), (3, 0), (1, 2), (2, 1)]


def head_pick(tall, query_len):
    lanes = tall.shape[1]
    lane_head = lax.broadcasted_iota(jnp.int32, (query_len, lanes), 1) // HEAD_DIM
    picked = jnp.zeros((query_len, lanes), jnp.float32)
    for head in range(lanes // HEAD_DIM):
        picked = jnp.where(lane_head == head, tall[head * query_len : (head + 1) * query_len, :], picked)
    return picked


def project_kernel(flag_ref, *refs, jobs, sends):
    keep_ref, *send_refs = refs[-1 - len(sends) :]
    slots = [(ref, at) for ref in send_refs for at in range(ref.shape[0])]
    core, same = flag_ref[0], flag_ref[1]
    half = keep_ref.shape[2]
    for at, (rows_of, blocks_of) in enumerate(jobs):
        if len(blocks_of) == 1:
            whole = refs[blocks_of[0][0]]
            keep = whole[pl.ds(pl.multiple_of(core * half, half), half), :]
            send = whole[pl.ds(pl.multiple_of((1 - core) * half, half), half), :]
        else:
            parts = [refs[block][:length] for block, length in blocks_of]
            first, second = (
                jnp.concatenate(part, axis=0) for part in (parts[: len(parts) // 2], parts[len(parts) // 2 :])
            )
            keep = jnp.where(same == 1, first, second)
            send = jnp.where(same == 1, second, first)
        product = lax.dot_general(
            refs[rows_of][...],
            jnp.concatenate([keep, send], axis=0),
            (((1,), (1,)), ((), ())),
            preferred_element_type=jnp.float32,
        )
        keep_ref[at] = product[:, :half]
        send_ref, slot = slots[at]
        send_ref[slot] = product[:, half:]


def attend_kernel(place_ref, spot_ref, query_ref, *refs, pieces):
    *refs, own_ref, partner_ref, out_ref, key_ref = refs
    residuals = own_ref, partner_ref
    partner_queries = own_ref.shape[0]
    query_len, held = query_ref.shape[1:]
    block_len = key_ref.shape[1]
    heads = held // HEAD_DIM
    tall = heads * query_len
    members, packed_rows, lanes_packed = out_ref.shape
    extra = packed_rows - 8
    row = lax.broadcasted_iota(jnp.int32, out_ref.shape, 1)
    out_ref[...] = jnp.where((row == extra) | (row == extra + 1), EMPTY, 0.0)
    row_head = lax.broadcasted_iota(jnp.int32, (tall, held), 0) // query_len
    lane_head = lax.broadcasted_iota(jnp.int32, (tall, held), 1) // HEAD_DIM
    diagonal = row_head == lane_head
    square = lax.broadcasted_iota(jnp.int32, (tall, tall), 0) == lax.broadcasted_iota(jnp.int32, (tall, tall), 1)
    ext = lax.broadcasted_iota(jnp.int32, (8, tall), 0)
    blocks = key_ref.shape[0] // 2
    for source, kept, sent, spot in pieces:
        keep, other = (refs[summand].at[piece] for summand, piece in (kept, sent))
        residual = residuals[source]
        span = keep.shape[1]
        lanes, given = (pl.ds(pl.multiple_of(spot_ref[of, spot], 128), span) for of in (1, source))
        for block in range(blocks):
            rows = slice(block * block_len, (block + 1) * block_len)
            key_ref[source * blocks + block, :, lanes] = (
                residual[rows, given].astype(jnp.float32) + (keep[rows, :] + other[rows, :])
            ).astype(jnp.bfloat16)
    places, scores, tops = [], [], []
    for at in range(key_ref.shape[0]):
        place = place_ref[at]
        first = pl.multiple_of(partner_queries + place // 2 * query_len, query_len)
        query = jnp.where(place % 2 == 0, query_ref[place // 2], partner_ref[pl.ds(first, query_len), :])
        query = jnp.concatenate([query] * heads, axis=0)
        query = jnp.where(diagonal, query, jnp.zeros_like(query))
        score = lax.dot_general(
            query, key_ref[at], (((1,), (1,)), ((), ())), preferred_element_type=jnp.float32
        )
        places.append(place)
        scores.append(score)
        tops.append(jnp.max(score, axis=1, keepdims=True))
    for at, place in enumerate(places):
        top = tops[at]
        for other_at, other_place in enumerate(places):
            if other_at != at:
                top = jnp.maximum(top, jnp.where(other_place == place, tops[other_at], EMPTY))
        weights = jnp.exp(scores[at] - top)
        total = jnp.sum(weights, axis=1, keepdims=True)
        blend = lax.dot_general(
            weights.astype(jnp.bfloat16), key_ref[at], (((1,), (0,)), ((), ())),
            preferred_element_type=jnp.float32,
        )
        top_row = jnp.sum(jnp.where(square, top, 0.0), axis=0, keepdims=True)
        total_row = jnp.sum(jnp.where(square, total, 0.0), axis=0, keepdims=True)
        blend = head_pick(blend, query_len)
        member, slot = place // 2, place % 2
        for block in range(held // lanes_packed):
            first = pl.multiple_of(slot * (extra // 2) + block * query_len, query_len)
            lanes = slice(block * lanes_packed, (block + 1) * lanes_packed)
            spot = pl.ds(first, query_len)
            out_ref[member, spot, :] = out_ref[member, spot, :] + blend[:, lanes]
        before = out_ref[member, extra:, :]
        out_ref[member, extra:, :] = jnp.where(
            ext == slot, top_row, jnp.where(ext == slot + 2, before + total_row, before)
        )


def merge_kernel(*refs):
    out_ref = refs[-1]
    parts = refs[:-1]
    query_len, held = out_ref.shape[1:]
    tall = held // HEAD_DIM * query_len
    square = lax.broadcasted_iota(jnp.int32, (tall, tall), 0) == lax.broadcasted_iota(jnp.int32, (tall, tall), 1)

    def over(start, step):
        for part in parts:
            start = lax.fori_loop(
                0, part.shape[0], functools.partial(step, part), start, unroll=part.shape[0] <= 8
            )
        return start

    packed_rows, lanes_packed = parts[0].shape[1:]
    extra = packed_rows - 8
    for slot in range(out_ref.shape[0]):
        top_row, total_row = (slice(extra + slot + at, extra + slot + at + 1) for at in (0, 2))

        def top_step(part, at, top):
            return jnp.maximum(top, part[at, top_row, :])

        def total_step(part, at, total):
            return total + jnp.exp(part[at, top_row, :] - top) * part[at, total_row, :]

        def blend_step(part, at, blend):
            share = jnp.exp(part[at, top_row, :] - top) / total
            column = jnp.sum(jnp.where(square, share, 0.0), axis=1, keepdims=True)
            spread = head_pick(jnp.broadcast_to(column, (tall, held)), query_len)
            first = slot * (extra // 2)
            rows = [
                part[at, first + block * query_len : first + (block + 1) * query_len, :]
                for block in range(held // lanes_packed)
            ]
            return blend + spread * jnp.concatenate(rows, axis=1)

        top = over(jnp.full((1, tall), EMPTY, jnp.float32), top_step)
        total = over(jnp.zeros((1, tall), jnp.float32), total_step)
        blend = over(jnp.zeros((query_len, held), jnp.float32), blend_step)
        out_ref[slot] = blend.astype(out_ref.dtype)


def assemble_kernel(flag_ref, mine_ref, core_ref, side_ref, both_ref, out_ref, *, order, span):
    side, core = flag_ref[0], flag_ref[1]
    mine, by_core, by_side, by_both = (ref[0] for ref in (mine_ref, core_ref, side_ref, both_ref))
    taken = {}
    for of_side in range(2):
        for of in range(2):
            near = jnp.where(core == of, mine, by_core)
            far = jnp.where(core == of, by_side, by_both)
            taken[of_side, of] = jnp.where(side == of_side, near, far)
    out_ref[0] = jnp.concatenate(
        [taken[of_side, of][:, first : first + span] for of_side, of, first in order], axis=1
    )


def in_vmem(count):
    return [pl.BlockSpec(memory_space=pltpu.VMEM)] * count


def in_smem(count):
    return [pl.BlockSpec(memory_space=pltpu.SMEM)] * count


def project(flags, operands, jobs, sends, half, flops, name):
    rows, units = operands[0].shape
    shapes = [jax.ShapeDtypeStruct((count, rows, half), jnp.float32) for count in [len(jobs)] + sends]
    return pl.pallas_call(
        functools.partial(project_kernel, jobs=jobs, sends=sends),
        out_shape=shapes,
        in_specs=in_smem(1) + in_vmem(len(operands)),
        out_specs=in_vmem(len(shapes)),
        compiler_params=pltpu.CompilerParams(vmem_limit_bytes=VMEM_LIMIT),
        cost_estimate=pl.CostEstimate(flops=flops, bytes_accessed=1, transcendentals=0),
        name=name,
    )(flags, *operands)


def after(array, earlier):
    return lax.optimization_barrier((array, *earlier))[0] if earlier else array


def with_rows(array, units):
    flat = array.reshape(-1, array.shape[-1])
    spread = jnp.concatenate([flat[at : at + 8] for at in range(0, flat.shape[0], 8)], axis=1)
    return jnp.pad(spread, ((0, 0), (0, units - spread.shape[1])))


def from_rows(spread, shape):
    pieces = [spread[:, at : at + shape[-1]] for at in range(0, math.prod(shape) // 8, shape[-1])]
    return jnp.concatenate(pieces, axis=0).reshape(shape)


def body(hidden_states, passage_states, down_weight, block_question, question_owner, decoder_states):
    blocks, block_len, units = hidden_states.shape
    width = passage_states.shape[2]
    query_len = decoder_states.shape[1]
    highs, lows, cores = lax.axis_size("high"), lax.axis_size("low"), lax.axis_size("mp")
    group, high, side, low, core = (lax.axis_index(name) for name in ("groups", "high", "side", "low", "mp"))
    shard = down_weight.shape[0]
    stride = lows * shard
    held = width // 2 // cores
    heads = held // HEAD_DIM
    members = highs * lows
    slot_total = question_owner.shape[0]
    rows = blocks * block_len
    lined = highs == 4 and lows == 1 and stride % (cores * 128) == 0
    span = stride // cores if lined else stride
    spans = held // span

    def features(array, of_side):
        if lined:
            starts = [(at * 2 + of_side) * stride + core * span for at in range(spans)]
        else:
            starts = [((core * spans + at) * 2 + of_side) * stride for at in range(spans)]
        taken = [lax.dynamic_slice_in_dim(array, start, span, axis=array.ndim - 1) for start in starts]
        return jnp.concatenate(taken, axis=-1)

    def shifted(array, shift):
        return lax.ppermute(array, "high", [(at, (at + shift) % highs) for at in range(highs)])

    hidden = hidden_states.reshape(rows, units)
    partner_hidden = lax.ppermute(hidden, "side", SWAP)
    queries = jnp.concatenate([features(decoder_states, side), features(decoder_states, 1 - side)], axis=0)[None]
    passages = passage_states.reshape(rows, width)
    leaving = features(passages, 1 - side)

    if lined:
        half = shard // 2
        lengths = [half * FIRST_EIGHTHS // 8, half - half * FIRST_EIGHTHS // 8]
        sent = [
            lax.dynamic_slice_in_dim(down_weight, group * half + first, length, axis=0)
            for first, length in zip((0, lengths[0]), lengths)
        ]
        sent[1] = jnp.concatenate([sent[1], with_rows(queries, units)], axis=0)
        below = [shifted(sent[0], 1)]
        sent = [after(piece, below) for piece in sent]
        below.append(shifted(sent[1], 1))
        above = [shifted(sent[0], -1)]
        above.append(shifted(after(sent[1], above), -1))
        opposite = [shifted(after(below[0], below[1:]), 1), shifted(below[1], 1)]
        around = [from_rows(piece[-1][-8:], queries.shape) for piece in (above, opposite, below)]
        queries = jnp.concatenate([queries] + around, axis=0)
        swapped = []
        for at, piece in enumerate([below[0], above[0], below[1], above[1]] + opposite):
            swapped.append(lax.ppermute(after(piece, swapped[max(at - 2, 0) : max(at - 1, 0)]), "groups", SWAP))
        weights = [down_weight] + above + swapped[1:4:2] + below + swapped[0:4:2] + opposite + swapped[4:]
        flags = jnp.stack([core, (group == core).astype(core.dtype)])
        blocks_of = [[(1, shard)]] + [list(zip(range(at, at + 4), 2 * lengths)) for at in (2, 6, 10)]
        spots = lax.rem(high + jnp.array([0, 1, 3, 2], jnp.int32), highs)
        spots = jnp.stack([(spots * 2 + side) * stride + core * span, spots * span])
        own_residual = passages

        flags = after(flags, swapped[4:5])
        kept, *away = project(
            flags, [hidden] + weights[:9], [(0, blocks_of[at]) for at in range(3)], [3], half, 1, "project_own"
        )
        flags, kept, *away = lax.optimization_barrier((flags, kept, *away))
        late_kept, *late_away = project(
            flags,
            [hidden] + weights + [partner_hidden],
            [(14, blocks_of[at]) for at in range(4)] + [(0, blocks_of[3])],
            [2, 2, 1],
            half,
            1,
            "project_rest",
        )
        others = [lax.ppermute(piece, "mp", SWAP) for piece in away + late_away]
        summands = [kept, late_kept] + others
        pieces = [(0, (0, at), (2, at), at) for at in range(3)] + [(0, (1, 4), (5, 0), 3)]
        pieces += [(1, (1, at), (3 + at // 2, at % 2), at) for at in range(4)]
        origin = high
    else:
        queries = lax.all_gather(queries, ("high", "low"), axis=0, tiled=True)
        weight = lax.all_gather(down_weight, ("high", "low"), axis=0, tiled=True)
        weight = jnp.where(core == 0, weight, jnp.roll(weight, held, axis=0))
        spots = jnp.zeros((2, 1), jnp.int32)
        own_residual = features(passages, side)
        summands, pieces = [], []
        for source, flat in enumerate((hidden, partner_hidden)):
            kept, away = (
                lax.dot_general(flat, part, (((1,), (1,)), ((), ())), preferred_element_type=jnp.float32)[None]
                for part in (weight[:held], weight[held:])
            )
            summands += [kept, lax.ppermute(away, "mp", SWAP)]
            pieces.append((source, (2 * source, 0), (2 * source + 1, 0), 0))
        origin = 0

    questions = block_question[:, 0]
    question_ids = jnp.arange(slot_total, dtype=jnp.int32)
    owners = jnp.sum(jnp.where(questions[:, None] == question_ids[None, :], question_owner[None, :], 0), axis=1)
    owner_high, owner_side, owner_low = owners // (2 * lows), (owners // lows) % 2, owners % lows
    owner_high = lax.rem(owner_high - origin + highs, highs)
    owner_place = (owner_high * lows + owner_low) * 2 + (owner_side != side)
    own_at = ((high * 2 + side) * lows + low) * blocks
    partner_at = ((high * 2 + 1 - side) * lows + low) * blocks
    places = jnp.concatenate(
        [lax.dynamic_slice_in_dim(owner_place, at, blocks) for at in (own_at, partner_at)]
    )

    leaving = jnp.concatenate([leaving, queries[:, 1].reshape(-1, held)], axis=0)
    partner = lax.ppermute(leaving, "side", SWAP)
    packed = (members, 2 * held // 128 * query_len + 8, 128)
    operands = summands + [own_residual, partner]
    partials = pl.pallas_call(
        functools.partial(attend_kernel, pieces=pieces),
        out_shape=jax.ShapeDtypeStruct(packed, jnp.float32),
        in_specs=in_smem(2) + in_vmem(1 + len(operands)),
        out_specs=pl.BlockSpec(memory_space=pltpu.VMEM),
        scratch_shapes=[pltpu.VMEM((2 * blocks, block_len, held), jnp.bfloat16)],
        compiler_params=pltpu.CompilerParams(vmem_limit_bytes=VMEM_LIMIT),
        name="attend",
    )(places, spots, queries[:, 0], *operands)
    if lined:
        received = [partials[0:1]] + [shifted(partials[ahead : ahead + 1], ahead) for ahead in range(1, highs)]
    else:
        received = [lax.all_to_all(partials, ("high", "low"), split_axis=0, concat_axis=0, tiled=True)]
    merged = pl.pallas_call(
        merge_kernel,
        out_shape=jax.ShapeDtypeStruct((2, query_len, held), decoder_states.dtype),
        in_specs=in_vmem(len(received)),
        out_specs=pl.BlockSpec(memory_space=pltpu.VMEM),
        compiler_params=pltpu.CompilerParams(vmem_limit_bytes=VMEM_LIMIT),
        name="merge",
    )(*received)

    mine, away = merged[0:1], merged[1:2]
    by_core = lax.ppermute(mine, "mp", SWAP)
    by_side = lax.ppermute(away, "side", SWAP)
    by_both = lax.ppermute(away, ("side", "mp"), CROSS)
    if lined:
        order = [(at, of_side, of) for at in range(spans) for of_side in range(2) for of in range(cores)]
    else:
        order = [(at, of_side, of) for of in range(cores) for at in range(spans) for of_side in range(2)]
    flags = jnp.stack([side, core])
    order = [(of_side, of, at * span) for at, of_side, of in order]
    return pl.pallas_call(
        functools.partial(assemble_kernel, order=order, span=span),
        out_shape=jax.ShapeDtypeStruct((1, query_len, width), decoder_states.dtype),
        in_specs=in_smem(1) + in_vmem(4),
        out_specs=pl.BlockSpec(memory_space=pltpu.VMEM),
        compiler_params=pltpu.CompilerParams(vmem_limit_bytes=VMEM_LIMIT),
        name="assemble",
    )(flags, mine, by_core, by_side, by_both)


def solution(mesh):
    groups, dp, cores = mesh.shape["groups"], mesh.shape["dp"], mesh.shape["mp"]

    def run(hidden_states, passage_states, down_weight, block_question, question_owner, decoder_states):
        lows = max(1, HEAD_DIM * dp // down_weight.shape[0])
        fine = Mesh(
            mesh.devices.reshape(groups, dp // (2 * lows), 2, lows, cores),
            ("groups", "high", "side", "low", "mp"),
        )
        split = ("groups", "high", "side", "low")
        placed = (
            P(split, None, "mp"),
            P(split, None, None),
            P(("high", "side", "low"), "mp"),
            P("groups", None),
            P("groups"),
            P(split, None, None),
        )
        return jax.shard_map(
            body, mesh=fine, in_specs=placed, out_specs=P(split, None, None), check_vma=False
        )(hidden_states, passage_states, down_weight, block_question, question_owner, decoder_states)

    return run
```

```python
import functools
import math

import jax
import jax.numpy as jnp
from jax import lax
from jax.experimental import pallas as pl
from jax.experimental.pallas import tpu as pltpu
from jax.sharding import Mesh, PartitionSpec as P

HEAD_DIM = 64
EMPTY = -3e38
FIRST_EIGHTHS = 4
VMEM_LIMIT = 22 * 1024 * 1024
SWAP = [(0, 1), (1, 0)]
CROSS = [(0, 3), (3, 0), (1, 2), (2, 1)]


def head_pick(tall, query_len):
    lanes = tall.shape[1]
    lane_head = lax.broadcasted_iota(jnp.int32, (query_len, lanes), 1) // HEAD_DIM
    picked = jnp.zeros((query_len, lanes), jnp.float32)
    for head in range(lanes // HEAD_DIM):
        picked = jnp.where(lane_head == head, tall[head * query_len : (head + 1) * query_len, :], picked)
    return picked


def project_kernel(flag_ref, partner_ref, hidden_ref, *refs, blocks, sends):
    *refs, rows_ref, semaphore = refs
    keep_ref, *send_refs = refs[-1 - len(sends) :]
    slots = [(ref, at) for ref in send_refs for at in range(ref.shape[0])]
    core, same = flag_ref[0], flag_ref[1]
    half = keep_ref.shape[2]
    copy = pltpu.make_async_copy(partner_ref, rows_ref, semaphore)
    copy.start()
    for source in range(2):
        if source == 1:
            copy.wait()
        for at, pieces in enumerate(blocks):
            if len(pieces) == 1:
                whole = refs[pieces[0][0]]
                keep = whole[pl.ds(pl.multiple_of(core * half, half), half), :]
                send = whole[pl.ds(pl.multiple_of((1 - core) * half, half), half), :]
            else:
                parts = [refs[piece][:length] for piece, length in pieces]
                first, second = (
                    jnp.concatenate(part, axis=0) for part in (parts[: len(parts) // 2], parts[len(parts) // 2 :])
                )
                keep = jnp.where(same == 1, first, second)
                send = jnp.where(same == 1, second, first)
            product = lax.dot_general(
                (rows_ref if source else hidden_ref)[...],
                jnp.concatenate([keep, send], axis=0),
                (((1,), (1,)), ((), ())),
                preferred_element_type=jnp.float32,
            )
            keep_ref[source * len(blocks) + at] = product[:, :half]
            send_ref, slot = slots[source * len(blocks) + at]
            send_ref[slot] = product[:, half:]


def attend_kernel(place_ref, spot_ref, query_ref, *refs, pieces):
    *refs, own_ref, partner_ref, out_ref, key_ref = refs
    residuals = own_ref, partner_ref
    partner_queries = own_ref.shape[0]
    held = query_ref.shape[1]
    query_len = query_ref.shape[0] // out_ref.shape[0]
    block_len = key_ref.shape[1]
    heads = held // HEAD_DIM
    tall = heads * query_len
    members, packed_rows, lanes_packed = out_ref.shape
    extra = packed_rows - 8
    row = lax.broadcasted_iota(jnp.int32, out_ref.shape, 1)
    out_ref[...] = jnp.where((row == extra) | (row == extra + 1), EMPTY, 0.0)
    row_head = lax.broadcasted_iota(jnp.int32, (tall, held), 0) // query_len
    lane_head = lax.broadcasted_iota(jnp.int32, (tall, held), 1) // HEAD_DIM
    diagonal = row_head == lane_head
    square = lax.broadcasted_iota(jnp.int32, (tall, tall), 0) == lax.broadcasted_iota(jnp.int32, (tall, tall), 1)
    ext = lax.broadcasted_iota(jnp.int32, (8, tall), 0)
    blocks = key_ref.shape[0] // 2
    for source, kept, sent, spot in pieces:
        keep, other = (refs[summand].at[piece] for summand, piece in (kept, sent))
        residual = residuals[source]
        span = keep.shape[1]
        lanes, given = (pl.ds(pl.multiple_of(spot_ref[of, spot], 128), span) for of in (1, source))
        for block in range(blocks):
            rows = slice(block * block_len, (block + 1) * block_len)
            key_ref[source * blocks + block, :, lanes] = (
                residual[rows, given].astype(jnp.float32) + (keep[rows, :] + other[rows, :])
            ).astype(jnp.bfloat16)
    places, scores, tops = [], [], []
    for at in range(key_ref.shape[0]):
        place = place_ref[at]
        first = pl.multiple_of(place // 2 * query_len, query_len)
        own_query = query_ref[pl.ds(first, query_len), :]
        partner_query = partner_ref[pl.ds(partner_queries + first, query_len), :]
        query = jnp.where(place % 2 == 0, own_query, partner_query)
        query = jnp.concatenate([query] * heads, axis=0)
        query = jnp.where(diagonal, query, jnp.zeros_like(query))
        score = lax.dot_general(
            query, key_ref[at], (((1,), (1,)), ((), ())), preferred_element_type=jnp.float32
        )
        places.append(place)
        scores.append(score)
        tops.append(jnp.max(score, axis=1, keepdims=True))
    for at, place in enumerate(places):
        top = tops[at]
        for other_at, other_place in enumerate(places):
            if other_at != at:
                top = jnp.maximum(top, jnp.where(other_place == place, tops[other_at], EMPTY))
        weights = jnp.exp(scores[at] - top)
        total = jnp.sum(weights, axis=1, keepdims=True)
        blend = lax.dot_general(
            weights.astype(jnp.bfloat16), key_ref[at], (((1,), (0,)), ((), ())),
            preferred_element_type=jnp.float32,
        )
        top_row = jnp.sum(jnp.where(square, top, 0.0), axis=0, keepdims=True)
        total_row = jnp.sum(jnp.where(square, total, 0.0), axis=0, keepdims=True)
        blend = head_pick(blend, query_len)
        member, slot = place // 2, place % 2
        for block in range(held // lanes_packed):
            first = pl.multiple_of(slot * (extra // 2) + block * query_len, query_len)
            lanes = slice(block * lanes_packed, (block + 1) * lanes_packed)
            spot = pl.ds(first, query_len)
            out_ref[member, spot, :] = out_ref[member, spot, :] + blend[:, lanes]
        before = out_ref[member, extra:, :]
        out_ref[member, extra:, :] = jnp.where(
            ext == slot, top_row, jnp.where(ext == slot + 2, before + total_row, before)
        )


def merge_kernel(*refs):
    out_ref = refs[-1]
    parts = refs[:-1]
    query_len, held = out_ref.shape[1:]
    tall = held // HEAD_DIM * query_len
    square = lax.broadcasted_iota(jnp.int32, (tall, tall), 0) == lax.broadcasted_iota(jnp.int32, (tall, tall), 1)

    def over(start, step):
        for part in parts:
            start = lax.fori_loop(
                0, part.shape[0], functools.partial(step, part), start, unroll=part.shape[0] <= 8
            )
        return start

    packed_rows, lanes_packed = parts[0].shape[1:]
    extra = packed_rows - 8
    for slot in range(out_ref.shape[0]):
        top_row, total_row = (slice(extra + slot + at, extra + slot + at + 1) for at in (0, 2))

        def top_step(part, at, top):
            return jnp.maximum(top, part[at, top_row, :])

        def total_step(part, at, total):
            return total + jnp.exp(part[at, top_row, :] - top) * part[at, total_row, :]

        def blend_step(part, at, blend):
            share = jnp.exp(part[at, top_row, :] - top) / total
            column = jnp.sum(jnp.where(square, share, 0.0), axis=1, keepdims=True)
            spread = head_pick(jnp.broadcast_to(column, (tall, held)), query_len)
            first = slot * (extra // 2)
            rows = [
                part[at, first + block * query_len : first + (block + 1) * query_len, :]
                for block in range(held // lanes_packed)
            ]
            return blend + spread * jnp.concatenate(rows, axis=1)

        top = over(jnp.full((1, tall), EMPTY, jnp.float32), top_step)
        total = over(jnp.zeros((1, tall), jnp.float32), total_step)
        blend = over(jnp.zeros((query_len, held), jnp.float32), blend_step)
        out_ref[slot] = blend.astype(out_ref.dtype)


def assemble_kernel(flag_ref, mine_ref, core_ref, side_ref, both_ref, out_ref, *, order, span):
    side, core = flag_ref[0], flag_ref[1]
    mine, by_core, by_side, by_both = (ref[0] for ref in (mine_ref, core_ref, side_ref, both_ref))
    taken = {}
    for of_side in range(2):
        for of in range(2):
            near = jnp.where(core == of, mine, by_core)
            far = jnp.where(core == of, by_side, by_both)
            taken[of_side, of] = jnp.where(side == of_side, near, far)
    out_ref[0] = jnp.concatenate(
        [taken[of_side, of][:, first : first + span] for of_side, of, first in order], axis=1
    )


def in_vmem(count):
    return [pl.BlockSpec(memory_space=pltpu.VMEM)] * count


def in_smem(count):
    return [pl.BlockSpec(memory_space=pltpu.SMEM)] * count


def project(flags, hidden, partner, weights, blocks, sends, half, name):
    rows, units = hidden.shape
    counts = [2 * len(blocks)] + sends
    return pl.pallas_call(
        functools.partial(project_kernel, blocks=blocks, sends=sends),
        out_shape=[jax.ShapeDtypeStruct((count, rows, half), jnp.float32) for count in counts],
        in_specs=in_smem(1) + [pl.BlockSpec(memory_space=pl.ANY)] + in_vmem(1 + len(weights)),
        out_specs=in_vmem(len(counts)),
        scratch_shapes=[pltpu.VMEM((rows, units), hidden.dtype), pltpu.SemaphoreType.DMA(())],
        compiler_params=pltpu.CompilerParams(vmem_limit_bytes=VMEM_LIMIT),
        cost_estimate=pl.CostEstimate(flops=1, bytes_accessed=1, transcendentals=0),
        name=name,
    )(flags, partner, hidden, *weights)


def after(array, earlier):
    return lax.optimization_barrier((array, *earlier))[0] if earlier else array


def with_rows(array, units):
    flat = array.reshape(-1, array.shape[-1])
    spread = jnp.concatenate([flat[at : at + 8] for at in range(0, flat.shape[0], 8)], axis=1)
    return jnp.pad(spread, ((0, 0), (0, units - spread.shape[1])))


def from_rows(spreads, slot, shape):
    taken = []
    for spread in spreads:
        for at in range(shape[0] // 8):
            first = (slot * shape[0] // 8 + at) * shape[1]
            taken.append(spread[-8:, first : first + shape[1]])
    return jnp.concatenate(taken, axis=0)


def body(hidden_states, passage_states, down_weight, block_question, question_owner, decoder_states):
    blocks, block_len, units = hidden_states.shape
    width = passage_states.shape[2]
    query_len = decoder_states.shape[1]
    highs, lows, cores = lax.axis_size("high"), lax.axis_size("low"), lax.axis_size("mp")
    group, high, side, low, core = (lax.axis_index(name) for name in ("groups", "high", "side", "low", "mp"))
    shard = down_weight.shape[0]
    stride = lows * shard
    held = width // 2 // cores
    heads = held // HEAD_DIM
    members = highs * lows
    slot_total = question_owner.shape[0]
    rows = blocks * block_len
    lined = highs == 4 and lows == 1 and stride % (cores * 128) == 0
    span = stride // cores if lined else stride
    spans = held // span

    def features(array, of_side):
        if lined:
            starts = [(at * 2 + of_side) * stride + core * span for at in range(spans)]
        else:
            starts = [((core * spans + at) * 2 + of_side) * stride for at in range(spans)]
        taken = [lax.dynamic_slice_in_dim(array, start, span, axis=array.ndim - 1) for start in starts]
        return jnp.concatenate(taken, axis=-1)

    def shifted(array, shift):
        return lax.ppermute(array, "high", [(at, (at + shift) % highs) for at in range(highs)])

    hidden = hidden_states.reshape(rows, units)
    partner_hidden = lax.ppermute(hidden, "side", SWAP)
    queries = jnp.concatenate([features(decoder_states, side), features(decoder_states, 1 - side)], axis=0)[None]
    passages = passage_states.reshape(rows, width)
    leaving = features(passages, 1 - side)

    if lined:
        half = shard // 2
        lengths = [half * FIRST_EIGHTHS // 8, half - half * FIRST_EIGHTHS // 8]
        sent = [
            lax.dynamic_slice_in_dim(down_weight, group * half + first, length, axis=0)
            for first, length in zip((0, lengths[0]), lengths)
        ]
        sent[1] = jnp.concatenate([sent[1], with_rows(queries, units)], axis=0)
        below, above = [], []
        for at in range(2):
            below.append(shifted(after(sent[at], below[-1:]), 1))
            above.append(shifted(after(sent[at], above[-1:]), -1))
        opposite = [shifted(after(below[0], below[1:]), 1), shifted(below[1], 1)]
        spreads = [sent[1], above[1], opposite[1], below[1]]
        own_queries, partner_queries = (from_rows(spreads, slot, (query_len, held)) for slot in range(2))
        swapped = []
        for at, piece in enumerate([below[0], above[0], below[1], above[1]] + opposite):
            swapped.append(lax.ppermute(after(piece, swapped[max(at - 2, 0) : max(at - 1, 0)]), "groups", SWAP))
        weights = [down_weight] + above + swapped[1:4:2] + below + swapped[0:4:2] + opposite + swapped[4:]
        flags = jnp.stack([core, (group == core).astype(core.dtype)])
        blocks_of = [[(0, shard)]] + [list(zip(range(at, at + 4), 2 * lengths)) for at in (1, 5, 0)]
        spots = lax.rem(high + jnp.array([0, 1, 3, 2], jnp.int32), highs)
        spots = jnp.stack([(spots * 2 + side) * stride + core * span, spots * span])
        own_residual = passages

        kept, *away = project(
            flags, hidden, partner_hidden, weights[:9], blocks_of[:3], [2, 2, 2], half, "project_near"
        )
        flags, kept, *away = lax.optimization_barrier((flags, kept, *away))
        late_kept, *late_away = project(
            flags, hidden, partner_hidden, weights[9:], blocks_of[3:], [2], half, "project_far"
        )
        others = [lax.ppermute(piece, "mp", SWAP) for piece in away + late_away]
        summands = [kept, late_kept] + others
        pieces = [(at // 3, (0, at), (2 + at // 2, at % 2), at % 3) for at in range(6)]
        pieces += [(source, (1, source), (5, source), 3) for source in range(2)]
        origin = high
    else:
        queries = lax.all_gather(queries, ("high", "low"), axis=0, tiled=True)
        own_queries, partner_queries = (queries[:, slot].reshape(-1, held) for slot in range(2))
        weight = lax.all_gather(down_weight, ("high", "low"), axis=0, tiled=True)
        weight = jnp.where(core == 0, weight, jnp.roll(weight, held, axis=0))
        spots = jnp.zeros((2, 1), jnp.int32)
        own_residual = features(passages, side)
        summands, pieces = [], []
        for source, flat in enumerate((hidden, partner_hidden)):
            kept, away = (
                lax.dot_general(flat, part, (((1,), (1,)), ((), ())), preferred_element_type=jnp.float32)[None]
                for part in (weight[:held], weight[held:])
            )
            summands += [kept, lax.ppermute(away, "mp", SWAP)]
            pieces.append((source, (2 * source, 0), (2 * source + 1, 0), 0))
        origin = 0

    questions = block_question[:, 0]
    question_ids = jnp.arange(slot_total, dtype=jnp.int32)
    owners = jnp.sum(jnp.where(questions[:, None] == question_ids[None, :], question_owner[None, :], 0), axis=1)
    owner_high, owner_side, owner_low = owners // (2 * lows), (owners // lows) % 2, owners % lows
    owner_high = lax.rem(owner_high - origin + highs, highs)
    owner_place = (owner_high * lows + owner_low) * 2 + (owner_side != side)
    own_at = ((high * 2 + side) * lows + low) * blocks
    partner_at = ((high * 2 + 1 - side) * lows + low) * blocks
    places = jnp.concatenate(
        [lax.dynamic_slice_in_dim(owner_place, at, blocks) for at in (own_at, partner_at)]
    )

    leaving = jnp.concatenate([leaving, partner_queries], axis=0)
    partner = lax.ppermute(leaving, "side", SWAP)
    packed = (members, 2 * held // 128 * query_len + 8, 128)
    operands = summands + [own_residual, partner]
    partials = pl.pallas_call(
        functools.partial(attend_kernel, pieces=pieces),
        out_shape=jax.ShapeDtypeStruct(packed, jnp.float32),
        in_specs=in_smem(2) + in_vmem(1 + len(operands)),
        out_specs=pl.BlockSpec(memory_space=pltpu.VMEM),
        scratch_shapes=[pltpu.VMEM((2 * blocks, block_len, held), jnp.bfloat16)],
        compiler_params=pltpu.CompilerParams(vmem_limit_bytes=VMEM_LIMIT),
        name="attend",
    )(places, spots, own_queries, *operands)
    if lined:
        received = [partials[0:1]] + [shifted(partials[ahead : ahead + 1], ahead) for ahead in range(1, highs)]
    else:
        received = [lax.all_to_all(partials, ("high", "low"), split_axis=0, concat_axis=0, tiled=True)]
    merged = pl.pallas_call(
        merge_kernel,
        out_shape=jax.ShapeDtypeStruct((2, query_len, held), decoder_states.dtype),
        in_specs=in_vmem(len(received)),
        out_specs=pl.BlockSpec(memory_space=pltpu.VMEM),
        compiler_params=pltpu.CompilerParams(vmem_limit_bytes=VMEM_LIMIT),
        name="merge",
    )(*received)

    mine, away = merged[0:1], merged[1:2]
    by_core = lax.ppermute(mine, "mp", SWAP)
    by_side = lax.ppermute(away, "side", SWAP)
    by_both = lax.ppermute(away, ("side", "mp"), CROSS)
    if lined:
        order = [(at, of_side, of) for at in range(spans) for of_side in range(2) for of in range(cores)]
    else:
        order = [(at, of_side, of) for of in range(cores) for at in range(spans) for of_side in range(2)]
    flags = jnp.stack([side, core])
    order = [(of_side, of, at * span) for at, of_side, of in order]
    return pl.pallas_call(
        functools.partial(assemble_kernel, order=order, span=span),
        out_shape=jax.ShapeDtypeStruct((1, query_len, width), decoder_states.dtype),
        in_specs=in_smem(1) + in_vmem(4),
        out_specs=pl.BlockSpec(memory_space=pltpu.VMEM),
        compiler_params=pltpu.CompilerParams(vmem_limit_bytes=VMEM_LIMIT),
        name="assemble",
    )(flags, mine, by_core, by_side, by_both)


def solution(mesh):
    groups, dp, cores = mesh.shape["groups"], mesh.shape["dp"], mesh.shape["mp"]

    def run(hidden_states, passage_states, down_weight, block_question, question_owner, decoder_states):
        lows = max(1, HEAD_DIM * dp // down_weight.shape[0])
        fine = Mesh(
            mesh.devices.reshape(groups, dp // (2 * lows), 2, lows, cores),
            ("groups", "high", "side", "low", "mp"),
        )
        split = ("groups", "high", "side", "low")
        placed = (
            P(split, None, "mp"),
            P(split, None, None),
            P(("high", "side", "low"), "mp"),
            P("groups", None),
            P("groups"),
            P(split, None, None),
        )
        return jax.shard_map(
            body, mesh=fine, in_specs=placed, out_specs=P(split, None, None), check_vma=False
        )(hidden_states, passage_states, down_weight, block_question, question_owner, decoder_states)

    return run
```

```python
import functools
import math

import jax
import jax.numpy as jnp
from jax import lax
from jax.experimental import pallas as pl
from jax.experimental.pallas import tpu as pltpu
from jax.sharding import Mesh, PartitionSpec as P

HEAD_DIM = 64
EMPTY = -3e38
FIRST_EIGHTHS = 4
VMEM_LIMIT = 22 * 1024 * 1024
SWAP = [(0, 1), (1, 0)]
CROSS = [(0, 3), (3, 0), (1, 2), (2, 1)]


def head_pick(tall, query_len):
    lanes = tall.shape[1]
    lane_head = lax.broadcasted_iota(jnp.int32, (query_len, lanes), 1) // HEAD_DIM
    picked = jnp.zeros((query_len, lanes), jnp.float32)
    for head in range(lanes // HEAD_DIM):
        picked = jnp.where(lane_head == head, tall[head * query_len : (head + 1) * query_len, :], picked)
    return picked


def project_kernel(flag_ref, hidden_ref, partner_ref, *refs, blocks, sends, copies):
    waiting = []
    if copies:
        *refs, semaphores = refs
        *refs, rows_ref = refs
        step = partner_ref.shape[1] // copies
        for at in range(copies):
            rows = pl.ds(at * step, step)
            waiting.append(pltpu.make_async_copy(partner_ref.at[flag_ref[2], rows], rows_ref.at[rows], semaphores.at[at]))
            waiting[-1].start()
        partner_ref = rows_ref
    keep_ref, *send_refs = refs[-1 - len(sends) :]
    slots = [(ref, at) for ref in send_refs for at in range(ref.shape[0])]
    core, same = flag_ref[0], flag_ref[1]
    half = keep_ref.shape[2]
    for source in range(2):
        for copy in waiting if source else []:
            copy.wait()
        for at, pieces in enumerate(blocks):
            if len(pieces) == 1:
                whole = refs[pieces[0][0]]
                keep = whole[pl.ds(pl.multiple_of(core * half, half), half), :]
                send = whole[pl.ds(pl.multiple_of((1 - core) * half, half), half), :]
            else:
                parts = [refs[piece][:length] for piece, length in pieces]
                first, second = (
                    jnp.concatenate(part, axis=0) for part in (parts[: len(parts) // 2], parts[len(parts) // 2 :])
                )
                keep = jnp.where(same == 1, first, second)
                send = jnp.where(same == 1, second, first)
            product = lax.dot_general(
                (partner_ref if source else hidden_ref)[...],
                jnp.concatenate([keep, send], axis=0),
                (((1,), (1,)), ((), ())),
                preferred_element_type=jnp.float32,
            )
            keep_ref[source * len(blocks) + at] = product[:, :half]
            send_ref, slot = slots[source * len(blocks) + at]
            send_ref[slot] = product[:, half:]


def attend_kernel(place_ref, spot_ref, query_ref, *refs, pieces):
    *refs, own_ref, partner_ref, out_ref, key_ref = refs
    residuals = own_ref, partner_ref
    partner_queries = own_ref.shape[0]
    held = query_ref.shape[1]
    query_len = query_ref.shape[0] // out_ref.shape[0]
    block_len = key_ref.shape[1]
    heads = held // HEAD_DIM
    tall = heads * query_len
    members, packed_rows, lanes_packed = out_ref.shape
    extra = packed_rows - 8
    row = lax.broadcasted_iota(jnp.int32, out_ref.shape, 1)
    out_ref[...] = jnp.where((row == extra) | (row == extra + 1), EMPTY, 0.0)
    row_head = lax.broadcasted_iota(jnp.int32, (tall, held), 0) // query_len
    lane_head = lax.broadcasted_iota(jnp.int32, (tall, held), 1) // HEAD_DIM
    diagonal = row_head == lane_head
    square = lax.broadcasted_iota(jnp.int32, (tall, tall), 0) == lax.broadcasted_iota(jnp.int32, (tall, tall), 1)
    ext = lax.broadcasted_iota(jnp.int32, (8, tall), 0)
    blocks = key_ref.shape[0] // 2
    for source, kept, sent, spot in pieces:
        keep, other = (refs[summand].at[piece] for summand, piece in (kept, sent))
        residual = residuals[source]
        span = keep.shape[1]
        lanes, given = (pl.ds(pl.multiple_of(spot_ref[of, spot], 128), span) for of in (1, source))
        for block in range(blocks):
            rows = slice(block * block_len, (block + 1) * block_len)
            key_ref[source * blocks + block, :, lanes] = (
                residual[rows, given].astype(jnp.float32) + (keep[rows, :] + other[rows, :])
            ).astype(jnp.bfloat16)
    places, scores, tops = [], [], []
    for at in range(key_ref.shape[0]):
        place = place_ref[at]
        first = pl.multiple_of(place // 2 * query_len, query_len)
        own_query = query_ref[pl.ds(first, query_len), :]
        partner_query = partner_ref[pl.ds(partner_queries + first, query_len), :]
        query = jnp.where(place % 2 == 0, own_query, partner_query)
        query = jnp.concatenate([query] * heads, axis=0)
        query = jnp.where(diagonal, query, jnp.zeros_like(query))
        score = lax.dot_general(
            query, key_ref[at], (((1,), (1,)), ((), ())), preferred_element_type=jnp.float32
        )
        places.append(place)
        scores.append(score)
        tops.append(jnp.max(score, axis=1, keepdims=True))
    for at, place in enumerate(places):
        top = tops[at]
        for other_at, other_place in enumerate(places):
            if other_at != at:
                top = jnp.maximum(top, jnp.where(other_place == place, tops[other_at], EMPTY))
        weights = jnp.exp(scores[at] - top)
        total = jnp.sum(weights, axis=1, keepdims=True)
        blend = lax.dot_general(
            weights.astype(jnp.bfloat16), key_ref[at], (((1,), (0,)), ((), ())),
            preferred_element_type=jnp.float32,
        )
        top_row = jnp.sum(jnp.where(square, top, 0.0), axis=0, keepdims=True)
        total_row = jnp.sum(jnp.where(square, total, 0.0), axis=0, keepdims=True)
        blend = head_pick(blend, query_len)
        member, slot = place // 2, place % 2
        for block in range(held // lanes_packed):
            first = pl.multiple_of(slot * (extra // 2) + block * query_len, query_len)
            lanes = slice(block * lanes_packed, (block + 1) * lanes_packed)
            spot = pl.ds(first, query_len)
            out_ref[member, spot, :] = out_ref[member, spot, :] + blend[:, lanes]
        before = out_ref[member, extra:, :]
        out_ref[member, extra:, :] = jnp.where(
            ext == slot, top_row, jnp.where(ext == slot + 2, before + total_row, before)
        )


def merge_kernel(*refs):
    out_ref = refs[-1]
    parts = refs[:-1]
    query_len, held = out_ref.shape[1:]
    tall = held // HEAD_DIM * query_len
    square = lax.broadcasted_iota(jnp.int32, (tall, tall), 0) == lax.broadcasted_iota(jnp.int32, (tall, tall), 1)

    def over(start, step):
        for part in parts:
            start = lax.fori_loop(
                0, part.shape[0], functools.partial(step, part), start, unroll=part.shape[0] <= 8
            )
        return start

    packed_rows, lanes_packed = parts[0].shape[1:]
    extra = packed_rows - 8
    for slot in range(out_ref.shape[0]):
        top_row, total_row = (slice(extra + slot + at, extra + slot + at + 1) for at in (0, 2))

        def top_step(part, at, top):
            return jnp.maximum(top, part[at, top_row, :])

        def total_step(part, at, total):
            return total + jnp.exp(part[at, top_row, :] - top) * part[at, total_row, :]

        def blend_step(part, at, blend):
            share = jnp.exp(part[at, top_row, :] - top) / total
            column = jnp.sum(jnp.where(square, share, 0.0), axis=1, keepdims=True)
            spread = head_pick(jnp.broadcast_to(column, (tall, held)), query_len)
            first = slot * (extra // 2)
            rows = [
                part[at, first + block * query_len : first + (block + 1) * query_len, :]
                for block in range(held // lanes_packed)
            ]
            return blend + spread * jnp.concatenate(rows, axis=1)

        top = over(jnp.full((1, tall), EMPTY, jnp.float32), top_step)
        total = over(jnp.zeros((1, tall), jnp.float32), total_step)
        blend = over(jnp.zeros((query_len, held), jnp.float32), blend_step)
        out_ref[slot] = blend.astype(out_ref.dtype)


def assemble_kernel(flag_ref, mine_ref, core_ref, side_ref, both_ref, out_ref, *, order, span):
    side, core = flag_ref[0], flag_ref[1]
    mine, by_core, by_side, by_both = (ref[0] for ref in (mine_ref, core_ref, side_ref, both_ref))
    taken = {}
    for of_side in range(2):
        for of in range(2):
            near = jnp.where(core == of, mine, by_core)
            far = jnp.where(core == of, by_side, by_both)
            taken[of_side, of] = jnp.where(side == of_side, near, far)
    out_ref[0] = jnp.concatenate(
        [taken[of_side, of][:, first : first + span] for of_side, of, first in order], axis=1
    )


def in_vmem(count):
    return [pl.BlockSpec(memory_space=pltpu.VMEM)] * count


def in_smem(count):
    return [pl.BlockSpec(memory_space=pltpu.SMEM)] * count


def project(flags, hidden, partner, weights, blocks, sends, half, copies, name):
    rows, units = hidden.shape
    shapes = [jax.ShapeDtypeStruct((count, rows, half), jnp.float32) for count in [2 * len(blocks)] + sends]
    if copies:
        shapes.append(jax.ShapeDtypeStruct((rows, units), hidden.dtype))
    held = [pl.BlockSpec(memory_space=pl.ANY)] if copies else in_vmem(1)
    return pl.pallas_call(
        functools.partial(project_kernel, blocks=blocks, sends=sends, copies=copies),
        out_shape=shapes,
        in_specs=in_smem(1) + in_vmem(1) + held + in_vmem(len(weights)),
        out_specs=in_vmem(len(shapes)),
        scratch_shapes=[pltpu.SemaphoreType.DMA((copies,))] if copies else [],
        compiler_params=pltpu.CompilerParams(vmem_limit_bytes=VMEM_LIMIT),
        cost_estimate=pl.CostEstimate(flops=1, bytes_accessed=1, transcendentals=0),
        name=name,
    )(flags, hidden, partner, *weights)


def after(array, earlier):
    return lax.optimization_barrier((array, *earlier))[0] if earlier else array


def with_rows(array, units):
    flat = array.reshape(-1, array.shape[-1])
    spread = jnp.concatenate([flat[at : at + 8] for at in range(0, flat.shape[0], 8)], axis=1)
    return jnp.pad(spread, ((0, 0), (0, units - spread.shape[1])))


def from_rows(spreads, slot, shape):
    taken = []
    for spread in spreads:
        for at in range(shape[0] // 8):
            first = (slot * shape[0] // 8 + at) * shape[1]
            taken.append(spread[-8:, first : first + shape[1]])
    return jnp.concatenate(taken, axis=0)


def body(hidden_states, passage_states, down_weight, block_question, question_owner, decoder_states):
    blocks, block_len, units = hidden_states.shape
    width = passage_states.shape[2]
    query_len = decoder_states.shape[1]
    highs, lows, cores = lax.axis_size("high"), lax.axis_size("low"), lax.axis_size("mp")
    group, high, side, low, core = (lax.axis_index(name) for name in ("groups", "high", "side", "low", "mp"))
    shard = down_weight.shape[0]
    stride = lows * shard
    held = width // 2 // cores
    heads = held // HEAD_DIM
    members = highs * lows
    slot_total = question_owner.shape[0]
    rows = blocks * block_len
    lined = highs == 4 and lows == 1 and stride % (cores * 128) == 0
    span = stride // cores if lined else stride
    spans = held // span

    def features(array, of_side):
        if lined:
            starts = [(at * 2 + of_side) * stride + core * span for at in range(spans)]
        else:
            starts = [((core * spans + at) * 2 + of_side) * stride for at in range(spans)]
        taken = [lax.dynamic_slice_in_dim(array, start, span, axis=array.ndim - 1) for start in starts]
        return jnp.concatenate(taken, axis=-1)

    def shifted(array, shift):
        return lax.ppermute(array, "high", [(at, (at + shift) % highs) for at in range(highs)])

    hidden = hidden_states.reshape(rows, units)
    partner_hidden = lax.all_gather(hidden, "side")
    queries = jnp.concatenate([features(decoder_states, side), features(decoder_states, 1 - side)], axis=0)[None]
    passages = passage_states.reshape(rows, width)
    leaving = features(passages, 1 - side)

    if lined:
        half = shard // 2
        lengths = [half * FIRST_EIGHTHS // 8, half - half * FIRST_EIGHTHS // 8]
        sent = [
            lax.dynamic_slice_in_dim(down_weight, group * half + first, length, axis=0)
            for first, length in zip((0, lengths[0]), lengths)
        ]
        sent[1] = jnp.concatenate([sent[1], with_rows(queries, units)], axis=0)
        below, above = [], []
        for at in range(2):
            below.append(shifted(after(sent[at], below[-1:]), 1))
            above.append(shifted(after(sent[at], above[-1:]), -1))
        opposite = [shifted(after(below[0], below[1:]), 1), shifted(below[1], 1)]
        spreads = [sent[1], above[1], opposite[1], below[1]]
        own_queries, partner_queries = (from_rows(spreads, slot, (query_len, held)) for slot in range(2))
        leaving = jnp.concatenate([leaving, partner_queries], axis=0)
        leaving_pieces = [below[0], above[0], below[1], above[1], opposite[0], after(opposite[1], [leaving])]
        swapped = []
        for at, piece in enumerate(leaving_pieces):
            swapped.append(lax.ppermute(after(piece, swapped[max(at - 2, 0) : max(at - 1, 0)]), "groups", SWAP))
        weights = [down_weight] + above + swapped[1:4:2] + below + swapped[0:4:2] + opposite + swapped[4:]
        flags = jnp.stack([core, (group == core).astype(core.dtype), 1 - side])
        blocks_of = [[(0, shard)]] + [list(zip(range(at, at + 4), 2 * lengths)) for at in (1, 5, 0)]
        spots = lax.rem(high + jnp.array([0, 1, 3, 2], jnp.int32), highs)
        spots = jnp.stack([(spots * 2 + side) * stride + core * span, spots * span])
        own_residual = passages

        kept, *away, partner_rows = project(
            flags, hidden, partner_hidden, weights[:9], blocks_of[:3], [2, 2, 2], half, 4, "project_near"
        )
        flags, kept, *away = lax.optimization_barrier((flags, kept, *away))
        late_kept, *late_away = project(
            flags, hidden, partner_rows, weights[9:], blocks_of[3:], [2], half, 0, "project_far"
        )
        others = [lax.ppermute(piece, "mp", SWAP) for piece in away + late_away]
        summands = [kept, late_kept] + others
        pieces = [(at // 3, (0, at), (2 + at // 2, at % 2), at % 3) for at in range(6)]
        pieces += [(source, (1, source), (5, source), 3) for source in range(2)]
        origin = high
    else:
        queries = lax.all_gather(queries, ("high", "low"), axis=0, tiled=True)
        own_queries, partner_queries = (queries[:, slot].reshape(-1, held) for slot in range(2))
        leaving = jnp.concatenate([leaving, partner_queries], axis=0)
        weight = lax.all_gather(down_weight, ("high", "low"), axis=0, tiled=True)
        weight = jnp.where(core == 0, weight, jnp.roll(weight, held, axis=0))
        spots = jnp.zeros((2, 1), jnp.int32)
        own_residual = features(passages, side)
        summands, pieces = [], []
        partner_hidden = lax.dynamic_index_in_dim(partner_hidden, 1 - side, keepdims=False)
        for source, flat in enumerate((hidden, partner_hidden)):
            kept, away = (
                lax.dot_general(flat, part, (((1,), (1,)), ((), ())), preferred_element_type=jnp.float32)[None]
                for part in (weight[:held], weight[held:])
            )
            summands += [kept, lax.ppermute(away, "mp", SWAP)]
            pieces.append((source, (2 * source, 0), (2 * source + 1, 0), 0))
        origin = 0

    questions = block_question[:, 0]
    question_ids = jnp.arange(slot_total, dtype=jnp.int32)
    owners = jnp.sum(jnp.where(questions[:, None] == question_ids[None, :], question_owner[None, :], 0), axis=1)
    owner_high, owner_side, owner_low = owners // (2 * lows), (owners // lows) % 2, owners % lows
    owner_high = lax.rem(owner_high - origin + highs, highs)
    owner_place = (owner_high * lows + owner_low) * 2 + (owner_side != side)
    own_at = ((high * 2 + side) * lows + low) * blocks
    partner_at = ((high * 2 + 1 - side) * lows + low) * blocks
    places = jnp.concatenate(
        [lax.dynamic_slice_in_dim(owner_place, at, blocks) for at in (own_at, partner_at)]
    )

    leaving = after(leaving, [partner_hidden])
    partner = lax.ppermute(leaving, "side", SWAP)
    packed = (members, 2 * held // 128 * query_len + 8, 128)
    operands = summands + [own_residual, partner]
    partials = pl.pallas_call(
        functools.partial(attend_kernel, pieces=pieces),
        out_shape=jax.ShapeDtypeStruct(packed, jnp.float32),
        in_specs=in_smem(2) + in_vmem(1 + len(operands)),
        out_specs=pl.BlockSpec(memory_space=pltpu.VMEM),
        scratch_shapes=[pltpu.VMEM((2 * blocks, block_len, held), jnp.bfloat16)],
        compiler_params=pltpu.CompilerParams(vmem_limit_bytes=VMEM_LIMIT),
        name="attend",
    )(places, spots, own_queries, *operands)
    if lined:
        received = [partials[0:1]] + [shifted(partials[ahead : ahead + 1], ahead) for ahead in range(1, highs)]
    else:
        received = [lax.all_to_all(partials, ("high", "low"), split_axis=0, concat_axis=0, tiled=True)]
    merged = pl.pallas_call(
        merge_kernel,
        out_shape=jax.ShapeDtypeStruct((2, query_len, held), decoder_states.dtype),
        in_specs=in_vmem(len(received)),
        out_specs=pl.BlockSpec(memory_space=pltpu.VMEM),
        compiler_params=pltpu.CompilerParams(vmem_limit_bytes=VMEM_LIMIT),
        name="merge",
    )(*received)

    mine, away = merged[0:1], merged[1:2]
    by_core = lax.ppermute(mine, "mp", SWAP)
    by_side = lax.ppermute(away, "side", SWAP)
    by_both = lax.ppermute(away, ("side", "mp"), CROSS)
    if lined:
        order = [(at, of_side, of) for at in range(spans) for of_side in range(2) for of in range(cores)]
    else:
        order = [(at, of_side, of) for of in range(cores) for at in range(spans) for of_side in range(2)]
    flags = jnp.stack([side, core])
    order = [(of_side, of, at * span) for at, of_side, of in order]
    return pl.pallas_call(
        functools.partial(assemble_kernel, order=order, span=span),
        out_shape=jax.ShapeDtypeStruct((1, query_len, width), decoder_states.dtype),
        in_specs=in_smem(1) + in_vmem(4),
        out_specs=pl.BlockSpec(memory_space=pltpu.VMEM),
        compiler_params=pltpu.CompilerParams(vmem_limit_bytes=VMEM_LIMIT),
        name="assemble",
    )(flags, mine, by_core, by_side, by_both)


def solution(mesh):
    groups, dp, cores = mesh.shape["groups"], mesh.shape["dp"], mesh.shape["mp"]

    def run(hidden_states, passage_states, down_weight, block_question, question_owner, decoder_states):
        lows = max(1, HEAD_DIM * dp // down_weight.shape[0])
        fine = Mesh(
            mesh.devices.reshape(groups, dp // (2 * lows), 2, lows, cores),
            ("groups", "high", "side", "low", "mp"),
        )
        split = ("groups", "high", "side", "low")
        placed = (
            P(split, None, "mp"),
            P(split, None, None),
            P(("high", "side", "low"), "mp"),
            P("groups", None),
            P("groups"),
            P(split, None, None),
        )
        return jax.shard_map(
            body, mesh=fine, in_specs=placed, out_specs=P(split, None, None), check_vma=False
        )(hidden_states, passage_states, down_weight, block_question, question_owner, decoder_states)

    return run
```

```python
import functools
import math

import jax
import jax.numpy as jnp
from jax import lax
from jax.experimental import pallas as pl
from jax.experimental.pallas import tpu as pltpu
from jax.sharding import Mesh, PartitionSpec as P

HEAD_DIM = 64
EMPTY = -3e38
FIRST_EIGHTHS = 4
VMEM_LIMIT = 22 * 1024 * 1024
SWAP = [(0, 1), (1, 0)]
CROSS = [(0, 3), (3, 0), (1, 2), (2, 1)]


def head_pick(tall, query_len):
    lanes = tall.shape[1]
    lane_head = lax.broadcasted_iota(jnp.int32, (query_len, lanes), 1) // HEAD_DIM
    picked = jnp.zeros((query_len, lanes), jnp.float32)
    for head in range(lanes // HEAD_DIM):
        picked = jnp.where(lane_head == head, tall[head * query_len : (head + 1) * query_len, :], picked)
    return picked


def project_kernel(flag_ref, hidden_ref, partner_ref, *refs, blocks, sends, copies):
    partner_copies, weight_copies = [], []
    if copies:
        *refs, rows_ref, shard_ref, semaphores = refs
        for of, (source, target) in enumerate(((partner_ref, rows_ref), (refs[0], shard_ref))):
            step = source.shape[0] // copies
            for at in range(copies):
                rows = pl.ds(at * step, step)
                copy = pltpu.make_async_copy(source.at[rows], target.at[rows], semaphores.at[of, at])
                (weight_copies if of else partner_copies).append(copy)
        for copy in weight_copies + partner_copies:
            copy.start()
        partner_ref = rows_ref
        refs = [shard_ref] + refs[1:]
    keep_ref, *send_refs = refs[-1 - len(sends) :]
    slots = [(ref, at) for ref in send_refs for at in range(ref.shape[0])]
    core, same = flag_ref[0], flag_ref[1]
    half = keep_ref.shape[2]
    for source in range(2):
        for copy in partner_copies if source else []:
            copy.wait()
        for at, pieces in enumerate(blocks):
            if len(pieces) == 1:
                for copy in [] if source else weight_copies:
                    copy.wait()
                whole = refs[pieces[0][0]]
                keep = whole[pl.ds(pl.multiple_of(core * half, half), half), :]
                send = whole[pl.ds(pl.multiple_of((1 - core) * half, half), half), :]
            else:
                parts = [refs[piece][:length] for piece, length in pieces]
                first, second = (
                    jnp.concatenate(part, axis=0) for part in (parts[: len(parts) // 2], parts[len(parts) // 2 :])
                )
                keep = jnp.where(same == 1, first, second)
                send = jnp.where(same == 1, second, first)
            product = lax.dot_general(
                (partner_ref if source else hidden_ref)[...],
                jnp.concatenate([keep, send], axis=0),
                (((1,), (1,)), ((), ())),
                preferred_element_type=jnp.float32,
            )
            keep_ref[source * len(blocks) + at] = product[:, :half]
            send_ref, slot = slots[source * len(blocks) + at]
            send_ref[slot] = product[:, half:]


def attend_kernel(place_ref, spot_ref, query_ref, *refs, pieces):
    *refs, own_ref, partner_ref, out_ref, key_ref = refs
    residuals = own_ref, partner_ref
    partner_queries = own_ref.shape[0]
    held = query_ref.shape[1]
    query_len = query_ref.shape[0] // out_ref.shape[0]
    block_len = key_ref.shape[1]
    heads = held // HEAD_DIM
    tall = heads * query_len
    members, packed_rows, lanes_packed = out_ref.shape
    extra = packed_rows - 8
    row = lax.broadcasted_iota(jnp.int32, out_ref.shape, 1)
    out_ref[...] = jnp.where((row == extra) | (row == extra + 1), EMPTY, 0.0)
    row_head = lax.broadcasted_iota(jnp.int32, (tall, held), 0) // query_len
    lane_head = lax.broadcasted_iota(jnp.int32, (tall, held), 1) // HEAD_DIM
    diagonal = row_head == lane_head
    square = lax.broadcasted_iota(jnp.int32, (tall, tall), 0) == lax.broadcasted_iota(jnp.int32, (tall, tall), 1)
    ext = lax.broadcasted_iota(jnp.int32, (8, tall), 0)
    blocks = key_ref.shape[0] // 2
    for source, kept, sent, spot in pieces:
        keep, other = (refs[summand].at[piece] for summand, piece in (kept, sent))
        residual = residuals[source]
        span = keep.shape[1]
        lanes, given = (pl.ds(pl.multiple_of(spot_ref[of, spot], 128), span) for of in (1, source))
        for block in range(blocks):
            rows = slice(block * block_len, (block + 1) * block_len)
            key_ref[source * blocks + block, :, lanes] = (
                residual[rows, given].astype(jnp.float32) + (keep[rows, :] + other[rows, :])
            ).astype(jnp.bfloat16)
    places, scores, tops = [], [], []
    for at in range(key_ref.shape[0]):
        place = place_ref[at]
        first = pl.multiple_of(place // 2 * query_len, query_len)
        own_query = query_ref[pl.ds(first, query_len), :]
        partner_query = partner_ref[pl.ds(partner_queries + first, query_len), :]
        query = jnp.where(place % 2 == 0, own_query, partner_query)
        query = jnp.concatenate([query] * heads, axis=0)
        query = jnp.where(diagonal, query, jnp.zeros_like(query))
        score = lax.dot_general(
            query, key_ref[at], (((1,), (1,)), ((), ())), preferred_element_type=jnp.float32
        )
        places.append(place)
        scores.append(score)
        tops.append(jnp.max(score, axis=1, keepdims=True))
    for at, place in enumerate(places):
        top = tops[at]
        for other_at, other_place in enumerate(places):
            if other_at != at:
                top = jnp.maximum(top, jnp.where(other_place == place, tops[other_at], EMPTY))
        weights = jnp.exp(scores[at] - top)
        total = jnp.sum(weights, axis=1, keepdims=True)
        blend = lax.dot_general(
            weights.astype(jnp.bfloat16), key_ref[at], (((1,), (0,)), ((), ())),
            preferred_element_type=jnp.float32,
        )
        top_row = jnp.sum(jnp.where(square, top, 0.0), axis=0, keepdims=True)
        total_row = jnp.sum(jnp.where(square, total, 0.0), axis=0, keepdims=True)
        blend = head_pick(blend, query_len)
        member, slot = place // 2, place % 2
        for block in range(held // lanes_packed):
            first = pl.multiple_of(slot * (extra // 2) + block * query_len, query_len)
            lanes = slice(block * lanes_packed, (block + 1) * lanes_packed)
            spot = pl.ds(first, query_len)
            out_ref[member, spot, :] = out_ref[member, spot, :] + blend[:, lanes]
        before = out_ref[member, extra:, :]
        out_ref[member, extra:, :] = jnp.where(
            ext == slot, top_row, jnp.where(ext == slot + 2, before + total_row, before)
        )


def merge_kernel(*refs):
    out_ref = refs[-1]
    parts = refs[:-1]
    query_len, held = out_ref.shape[1:]
    tall = held // HEAD_DIM * query_len
    square = lax.broadcasted_iota(jnp.int32, (tall, tall), 0) == lax.broadcasted_iota(jnp.int32, (tall, tall), 1)

    def over(start, step):
        for part in parts:
            start = lax.fori_loop(
                0, part.shape[0], functools.partial(step, part), start, unroll=part.shape[0] <= 8
            )
        return start

    packed_rows, lanes_packed = parts[0].shape[1:]
    extra = packed_rows - 8
    for slot in range(out_ref.shape[0]):
        top_row, total_row = (slice(extra + slot + at, extra + slot + at + 1) for at in (0, 2))

        def top_step(part, at, top):
            return jnp.maximum(top, part[at, top_row, :])

        def total_step(part, at, total):
            return total + jnp.exp(part[at, top_row, :] - top) * part[at, total_row, :]

        def blend_step(part, at, blend):
            share = jnp.exp(part[at, top_row, :] - top) / total
            column = jnp.sum(jnp.where(square, share, 0.0), axis=1, keepdims=True)
            spread = head_pick(jnp.broadcast_to(column, (tall, held)), query_len)
            first = slot * (extra // 2)
            rows = [
                part[at, first + block * query_len : first + (block + 1) * query_len, :]
                for block in range(held // lanes_packed)
            ]
            return blend + spread * jnp.concatenate(rows, axis=1)

        top = over(jnp.full((1, tall), EMPTY, jnp.float32), top_step)
        total = over(jnp.zeros((1, tall), jnp.float32), total_step)
        blend = over(jnp.zeros((query_len, held), jnp.float32), blend_step)
        out_ref[slot] = blend.astype(out_ref.dtype)


def assemble_kernel(flag_ref, mine_ref, core_ref, side_ref, both_ref, out_ref, *, order, span):
    side, core = flag_ref[0], flag_ref[1]
    mine, by_core, by_side, by_both = (ref[0] for ref in (mine_ref, core_ref, side_ref, both_ref))
    taken = {}
    for of_side in range(2):
        for of in range(2):
            near = jnp.where(core == of, mine, by_core)
            far = jnp.where(core == of, by_side, by_both)
            taken[of_side, of] = jnp.where(side == of_side, near, far)
    out_ref[0] = jnp.concatenate(
        [taken[of_side, of][:, first : first + span] for of_side, of, first in order], axis=1
    )


def in_vmem(count):
    return [pl.BlockSpec(memory_space=pltpu.VMEM)] * count


def in_smem(count):
    return [pl.BlockSpec(memory_space=pltpu.SMEM)] * count


def project(flags, hidden, partner, weights, blocks, sends, half, copies, name):
    rows, units = hidden.shape
    shapes = [jax.ShapeDtypeStruct((count, rows, half), jnp.float32) for count in [2 * len(blocks)] + sends]
    if copies:
        shapes.append(jax.ShapeDtypeStruct((rows, units), hidden.dtype))
    held = [pl.BlockSpec(memory_space=pltpu.HBM)] * 2 if copies else in_vmem(2)
    scratch = [pltpu.VMEM(weights[0].shape, weights[0].dtype), pltpu.SemaphoreType.DMA((2, copies))]
    return pl.pallas_call(
        functools.partial(project_kernel, blocks=blocks, sends=sends, copies=copies),
        out_shape=shapes,
        in_specs=in_smem(1) + in_vmem(1) + held + in_vmem(len(weights) - 1),
        out_specs=in_vmem(len(shapes)),
        scratch_shapes=scratch if copies else [],
        compiler_params=pltpu.CompilerParams(vmem_limit_bytes=VMEM_LIMIT),
        cost_estimate=pl.CostEstimate(flops=1, bytes_accessed=1, transcendentals=0),
        name=name,
    )(flags, hidden, partner, *weights)


def after(array, earlier):
    return lax.optimization_barrier((array, *earlier))[0] if earlier else array


def with_rows(array, units):
    flat = array.reshape(-1, array.shape[-1])
    spread = jnp.concatenate([flat[at : at + 8] for at in range(0, flat.shape[0], 8)], axis=1)
    return jnp.pad(spread, ((0, 0), (0, units - spread.shape[1])))


def from_rows(spreads, slot, shape):
    taken = []
    for spread in spreads:
        for at in range(shape[0] // 8):
            first = (slot * shape[0] // 8 + at) * shape[1]
            taken.append(spread[-8:, first : first + shape[1]])
    return jnp.concatenate(taken, axis=0)


def body(hidden_states, passage_states, down_weight, block_question, question_owner, decoder_states):
    blocks, block_len, units = hidden_states.shape
    width = passage_states.shape[2]
    query_len = decoder_states.shape[1]
    highs, lows, cores = lax.axis_size("high"), lax.axis_size("low"), lax.axis_size("mp")
    group, high, side, low, core = (lax.axis_index(name) for name in ("groups", "high", "side", "low", "mp"))
    shard = down_weight.shape[0]
    stride = lows * shard
    held = width // 2 // cores
    heads = held // HEAD_DIM
    members = highs * lows
    slot_total = question_owner.shape[0]
    rows = blocks * block_len
    lined = highs == 4 and lows == 1 and stride % (cores * 128) == 0
    span = stride // cores if lined else stride
    spans = held // span

    def features(array, of_side):
        if lined:
            starts = [(at * 2 + of_side) * stride + core * span for at in range(spans)]
        else:
            starts = [((core * spans + at) * 2 + of_side) * stride for at in range(spans)]
        taken = [lax.dynamic_slice_in_dim(array, start, span, axis=array.ndim - 1) for start in starts]
        return jnp.concatenate(taken, axis=-1)

    def shifted(array, shift):
        return lax.ppermute(array, "high", [(at, (at + shift) % highs) for at in range(highs)])

    hidden = hidden_states.reshape(rows, units)
    partner_hidden = lax.ppermute(hidden, "side", SWAP)
    queries = jnp.concatenate([features(decoder_states, side), features(decoder_states, 1 - side)], axis=0)[None]
    passages = passage_states.reshape(rows, width)
    leaving = features(passages, 1 - side)

    if lined:
        half = shard // 2
        lengths = [half * FIRST_EIGHTHS // 8, half - half * FIRST_EIGHTHS // 8]
        sent = [
            lax.dynamic_slice_in_dim(down_weight, group * half + first, length, axis=0)
            for first, length in zip((0, lengths[0]), lengths)
        ]
        sent[1] = jnp.concatenate([sent[1], with_rows(queries, units)], axis=0)
        below, above = [], []
        for at in range(2):
            below.append(shifted(after(sent[at], below[-1:]), 1))
            above.append(shifted(after(sent[at], above[-1:]), -1))
        opposite = [shifted(after(below[0], below[1:]), 1), shifted(below[1], 1)]
        spreads = [piece[1][-8:] for piece in (sent, above, opposite, below)]
        *spreads, leaving, _ = lax.optimization_barrier(
            (*spreads, jnp.pad(leaving, ((0, highs * query_len), (0, 0))), partner_hidden)
        )
        own_queries, partner_queries = (from_rows(spreads, slot, (query_len, held)) for slot in range(2))
        leaving = lax.dynamic_update_slice(leaving, partner_queries, (rows, 0))
        leaving_pieces = [below[0], above[0], below[1], above[1], opposite[0], opposite[1]]
        swapped = []
        for at, piece in enumerate(leaving_pieces):
            swapped.append(lax.ppermute(after(piece, swapped[max(at - 2, 0) : max(at - 1, 0)]), "groups", SWAP))
        weights = [down_weight] + above + swapped[1:4:2] + below + swapped[0:4:2] + opposite + swapped[4:]
        flags = jnp.stack([core, (group == core).astype(core.dtype)])
        blocks_of = [list(zip(range(at, at + 4), 2 * lengths)) for at in (1, 5, 0)]
        blocks_of.insert(2, [(0, shard)])
        spots = lax.rem(high + jnp.array([1, 3, 0, 2], jnp.int32), highs)
        spots = jnp.stack([(spots * 2 + side) * stride + core * span, spots * span])
        own_residual = passages

        kept, *away, partner_rows = project(
            flags, hidden, partner_hidden, weights[:9], blocks_of[:3], [2, 2, 2], half, 4, "project_near"
        )
        flags, kept, *away = lax.optimization_barrier((flags, kept, *away))
        late_kept, *late_away = project(
            flags, hidden, partner_rows, weights[9:], blocks_of[3:], [2], half, 0, "project_far"
        )
        others = [lax.ppermute(piece, "mp", SWAP) for piece in away + late_away]
        summands = [kept, late_kept] + others
        pieces = [(at // 3, (0, at), (2 + at // 2, at % 2), at % 3) for at in range(6)]
        pieces += [(source, (1, source), (5, source), 3) for source in range(2)]
        origin = high
    else:
        queries = lax.all_gather(queries, ("high", "low"), axis=0, tiled=True)
        own_queries, partner_queries = (queries[:, slot].reshape(-1, held) for slot in range(2))
        leaving = jnp.concatenate([leaving, partner_queries], axis=0)
        weight = lax.all_gather(down_weight, ("high", "low"), axis=0, tiled=True)
        weight = jnp.where(core == 0, weight, jnp.roll(weight, held, axis=0))
        spots = jnp.zeros((2, 1), jnp.int32)
        own_residual = features(passages, side)
        summands, pieces = [], []
        for source, flat in enumerate((hidden, partner_hidden)):
            kept, away = (
                lax.dot_general(flat, part, (((1,), (1,)), ((), ())), preferred_element_type=jnp.float32)[None]
                for part in (weight[:held], weight[held:])
            )
            summands += [kept, lax.ppermute(away, "mp", SWAP)]
            pieces.append((source, (2 * source, 0), (2 * source + 1, 0), 0))
        origin = 0

    questions = block_question[:, 0]
    question_ids = jnp.arange(slot_total, dtype=jnp.int32)
    owners = jnp.sum(jnp.where(questions[:, None] == question_ids[None, :], question_owner[None, :], 0), axis=1)
    owner_high, owner_side, owner_low = owners // (2 * lows), (owners // lows) % 2, owners % lows
    owner_high = lax.rem(owner_high - origin + highs, highs)
    owner_place = (owner_high * lows + owner_low) * 2 + (owner_side != side)
    own_at = ((high * 2 + side) * lows + low) * blocks
    partner_at = ((high * 2 + 1 - side) * lows + low) * blocks
    places = jnp.concatenate(
        [lax.dynamic_slice_in_dim(owner_place, at, blocks) for at in (own_at, partner_at)]
    )

    partner = lax.ppermute(leaving, "side", SWAP)
    packed = (members, 2 * held // 128 * query_len + 8, 128)
    operands = summands + [own_residual, partner]
    partials = pl.pallas_call(
        functools.partial(attend_kernel, pieces=pieces),
        out_shape=jax.ShapeDtypeStruct(packed, jnp.float32),
        in_specs=in_smem(2) + in_vmem(1 + len(operands)),
        out_specs=pl.BlockSpec(memory_space=pltpu.VMEM),
        scratch_shapes=[pltpu.VMEM((2 * blocks, block_len, held), jnp.bfloat16)],
        compiler_params=pltpu.CompilerParams(vmem_limit_bytes=VMEM_LIMIT),
        name="attend",
    )(places, spots, own_queries, *operands)
    if lined:
        received = [partials[0:1]] + [shifted(partials[ahead : ahead + 1], ahead) for ahead in range(1, highs)]
    else:
        received = [lax.all_to_all(partials, ("high", "low"), split_axis=0, concat_axis=0, tiled=True)]
    merged = pl.pallas_call(
        merge_kernel,
        out_shape=jax.ShapeDtypeStruct((2, query_len, held), decoder_states.dtype),
        in_specs=in_vmem(len(received)),
        out_specs=pl.BlockSpec(memory_space=pltpu.VMEM),
        compiler_params=pltpu.CompilerParams(vmem_limit_bytes=VMEM_LIMIT),
        name="merge",
    )(*received)

    mine, away = merged[0:1], merged[1:2]
    by_core = lax.ppermute(mine, "mp", SWAP)
    by_side = lax.ppermute(away, "side", SWAP)
    by_both = lax.ppermute(away, ("side", "mp"), CROSS)
    if lined:
        order = [(at, of_side, of) for at in range(spans) for of_side in range(2) for of in range(cores)]
    else:
        order = [(at, of_side, of) for of in range(cores) for at in range(spans) for of_side in range(2)]
    flags = jnp.stack([side, core])
    order = [(of_side, of, at * span) for at, of_side, of in order]
    return pl.pallas_call(
        functools.partial(assemble_kernel, order=order, span=span),
        out_shape=jax.ShapeDtypeStruct((1, query_len, width), decoder_states.dtype),
        in_specs=in_smem(1) + in_vmem(4),
        out_specs=pl.BlockSpec(memory_space=pltpu.VMEM),
        compiler_params=pltpu.CompilerParams(vmem_limit_bytes=VMEM_LIMIT),
        name="assemble",
    )(flags, mine, by_core, by_side, by_both)


def solution(mesh):
    groups, dp, cores = mesh.shape["groups"], mesh.shape["dp"], mesh.shape["mp"]

    def run(hidden_states, passage_states, down_weight, block_question, question_owner, decoder_states):
        lows = max(1, HEAD_DIM * dp // down_weight.shape[0])
        fine = Mesh(
            mesh.devices.reshape(groups, dp // (2 * lows), 2, lows, cores),
            ("groups", "high", "side", "low", "mp"),
        )
        split = ("groups", "high", "side", "low")
        placed = (
            P(split, None, "mp"),
            P(split, None, None),
            P(("high", "side", "low"), "mp"),
            P("groups", None),
            P("groups"),
            P(split, None, None),
        )
        return jax.shard_map(
            body, mesh=fine, in_specs=placed, out_specs=P(split, None, None), check_vma=False
        )(hidden_states, passage_states, down_weight, block_question, question_owner, decoder_states)

    return run
```

```python
import functools
import math

import jax
import jax.numpy as jnp
from jax import lax
from jax.experimental import pallas as pl
from jax.experimental.pallas import tpu as pltpu
from jax.sharding import Mesh, PartitionSpec as P

HEAD_DIM = 64
EMPTY = -3e38
FIRST_EIGHTHS = 4
ROW_COPIES = 4
PROJECT_LIMIT = 48 * 1024 * 1024
VMEM_LIMIT = 22 * 1024 * 1024
SWAP = [(0, 1), (1, 0)]
CROSS = [(0, 3), (3, 0), (1, 2), (2, 1)]


def head_pick(tall, query_len):
    lanes = tall.shape[1]
    lane_head = lax.broadcasted_iota(jnp.int32, (query_len, lanes), 1) // HEAD_DIM
    picked = jnp.zeros((query_len, lanes), jnp.float32)
    for head in range(lanes // HEAD_DIM):
        picked = jnp.where(lane_head == head, tall[head * query_len : (head + 1) * query_len, :], picked)
    return picked


def project_kernel(flag_ref, *refs, sources, blocks, sends):
    *refs, rows_ref, block_ref, row_sems, block_sems = refs
    keep_ref, *send_refs = refs[-1 - len(sends) :]
    slots = [(ref, at) for ref in send_refs for at in range(ref.shape[0])]
    core, same = flag_ref[0], flag_ref[1]
    half = keep_ref.shape[2]
    row_copies, block_copies = [], []
    for at in range(sources):
        step = rows_ref.shape[1] // ROW_COPIES
        row_copies.append([])
        for part in range(ROW_COPIES):
            rows = pl.ds(part * step, step)
            row_copies[-1].append(
                pltpu.make_async_copy(refs[at].at[rows], rows_ref.at[at, rows], row_sems.at[at, part])
            )
    for at, pieces in enumerate(blocks):
        block_copies.append([])
        for part, (operand, first, rows, where) in enumerate(pieces):
            place = where + half * {"came": 1 - same, "swapped": same, "low": core, "high": 1 - core}[operand[0]]
            block_copies[-1].append(
                pltpu.make_async_copy(
                    refs[operand[1]].at[pl.ds(first, rows)],
                    block_ref.at[at, pl.ds(pl.multiple_of(place, 16), rows)],
                    block_sems.at[at, part],
                )
            )
    for copies in row_copies[:1] + block_copies + row_copies[1:]:
        for copy in copies:
            copy.start()
    for source in range(sources):
        for copy in row_copies[source]:
            copy.wait()
        for at in range(len(blocks)):
            for copy in [] if source else block_copies[at]:
                copy.wait()
            product = lax.dot_general(
                rows_ref[source], block_ref[at], (((1,), (1,)), ((), ())), preferred_element_type=jnp.float32
            )
            keep_ref[source * len(blocks) + at] = product[:, :half]
            send_ref, slot = slots[source * len(blocks) + at]
            send_ref[slot] = product[:, half:]


def attend_kernel(place_ref, spot_ref, query_ref, *refs, pieces):
    *refs, own_ref, partner_ref, out_ref, key_ref = refs
    residuals = own_ref, partner_ref
    partner_queries = own_ref.shape[0]
    held = query_ref.shape[1]
    query_len = query_ref.shape[0] // out_ref.shape[0]
    block_len = key_ref.shape[1]
    heads = held // HEAD_DIM
    tall = heads * query_len
    members, packed_rows, lanes_packed = out_ref.shape
    extra = packed_rows - 8
    row = lax.broadcasted_iota(jnp.int32, out_ref.shape, 1)
    out_ref[...] = jnp.where((row == extra) | (row == extra + 1), EMPTY, 0.0)
    row_head = lax.broadcasted_iota(jnp.int32, (tall, held), 0) // query_len
    lane_head = lax.broadcasted_iota(jnp.int32, (tall, held), 1) // HEAD_DIM
    diagonal = row_head == lane_head
    square = lax.broadcasted_iota(jnp.int32, (tall, tall), 0) == lax.broadcasted_iota(jnp.int32, (tall, tall), 1)
    ext = lax.broadcasted_iota(jnp.int32, (8, tall), 0)
    blocks = key_ref.shape[0] // 2
    for source, kept, sent, spot in pieces:
        keep, other = (refs[summand].at[piece] for summand, piece in (kept, sent))
        residual = residuals[source]
        span = keep.shape[1]
        lanes, given = (pl.ds(pl.multiple_of(spot_ref[of, spot], 128), span) for of in (1, source))
        for block in range(blocks):
            rows = slice(block * block_len, (block + 1) * block_len)
            key_ref[source * blocks + block, :, lanes] = (
                residual[rows, given].astype(jnp.float32) + (keep[rows, :] + other[rows, :])
            ).astype(jnp.bfloat16)
    places, scores, tops = [], [], []
    for at in range(key_ref.shape[0]):
        place = place_ref[at]
        first = pl.multiple_of(place // 2 * query_len, query_len)
        own_query = query_ref[pl.ds(first, query_len), :]
        partner_query = partner_ref[pl.ds(partner_queries + first, query_len), :]
        query = jnp.where(place % 2 == 0, own_query, partner_query)
        query = jnp.concatenate([query] * heads, axis=0)
        query = jnp.where(diagonal, query, jnp.zeros_like(query))
        score = lax.dot_general(
            query, key_ref[at], (((1,), (1,)), ((), ())), preferred_element_type=jnp.float32
        )
        places.append(place)
        scores.append(score)
        tops.append(jnp.max(score, axis=1, keepdims=True))
    for at, place in enumerate(places):
        top = tops[at]
        for other_at, other_place in enumerate(places):
            if other_at != at:
                top = jnp.maximum(top, jnp.where(other_place == place, tops[other_at], EMPTY))
        weights = jnp.exp(scores[at] - top)
        total = jnp.sum(weights, axis=1, keepdims=True)
        blend = lax.dot_general(
            weights.astype(jnp.bfloat16), key_ref[at], (((1,), (0,)), ((), ())),
            preferred_element_type=jnp.float32,
        )
        top_row = jnp.sum(jnp.where(square, top, 0.0), axis=0, keepdims=True)
        total_row = jnp.sum(jnp.where(square, total, 0.0), axis=0, keepdims=True)
        blend = head_pick(blend, query_len)
        member, slot = place // 2, place % 2
        for block in range(held // lanes_packed):
            first = pl.multiple_of(slot * (extra // 2) + block * query_len, query_len)
            lanes = slice(block * lanes_packed, (block + 1) * lanes_packed)
            spot = pl.ds(first, query_len)
            out_ref[member, spot, :] = out_ref[member, spot, :] + blend[:, lanes]
        before = out_ref[member, extra:, :]
        out_ref[member, extra:, :] = jnp.where(
            ext == slot, top_row, jnp.where(ext == slot + 2, before + total_row, before)
        )


def merge_kernel(*refs):
    out_ref = refs[-1]
    parts = refs[:-1]
    query_len, held = out_ref.shape[1:]
    tall = held // HEAD_DIM * query_len
    square = lax.broadcasted_iota(jnp.int32, (tall, tall), 0) == lax.broadcasted_iota(jnp.int32, (tall, tall), 1)

    def over(start, step):
        for part in parts:
            start = lax.fori_loop(
                0, part.shape[0], functools.partial(step, part), start, unroll=part.shape[0] <= 8
            )
        return start

    packed_rows, lanes_packed = parts[0].shape[1:]
    extra = packed_rows - 8
    for slot in range(out_ref.shape[0]):
        top_row, total_row = (slice(extra + slot + at, extra + slot + at + 1) for at in (0, 2))

        def top_step(part, at, top):
            return jnp.maximum(top, part[at, top_row, :])

        def total_step(part, at, total):
            return total + jnp.exp(part[at, top_row, :] - top) * part[at, total_row, :]

        def blend_step(part, at, blend):
            share = jnp.exp(part[at, top_row, :] - top) / total
            column = jnp.sum(jnp.where(square, share, 0.0), axis=1, keepdims=True)
            spread = head_pick(jnp.broadcast_to(column, (tall, held)), query_len)
            first = slot * (extra // 2)
            rows = [
                part[at, first + block * query_len : first + (block + 1) * query_len, :]
                for block in range(held // lanes_packed)
            ]
            return blend + spread * jnp.concatenate(rows, axis=1)

        top = over(jnp.full((1, tall), EMPTY, jnp.float32), top_step)
        total = over(jnp.zeros((1, tall), jnp.float32), total_step)
        blend = over(jnp.zeros((query_len, held), jnp.float32), blend_step)
        out_ref[slot] = blend.astype(out_ref.dtype)


def assemble_kernel(flag_ref, mine_ref, core_ref, side_ref, both_ref, out_ref, *, order, span):
    side, core = flag_ref[0], flag_ref[1]
    mine, by_core, by_side, by_both = (ref[0] for ref in (mine_ref, core_ref, side_ref, both_ref))
    taken = {}
    for of_side in range(2):
        for of in range(2):
            near = jnp.where(core == of, mine, by_core)
            far = jnp.where(core == of, by_side, by_both)
            taken[of_side, of] = jnp.where(side == of_side, near, far)
    out_ref[0] = jnp.concatenate(
        [taken[of_side, of][:, first : first + span] for of_side, of, first in order], axis=1
    )


def in_vmem(count):
    return [pl.BlockSpec(memory_space=pltpu.VMEM)] * count


def in_smem(count):
    return [pl.BlockSpec(memory_space=pltpu.SMEM)] * count


def project(flags, sources, weights, blocks, sends, half, name):
    rows, units = sources[0].shape
    counts = [len(sources) * len(blocks)] + sends
    parts = max(len(pieces) for pieces in blocks)
    blocks = [[((piece[0], piece[1] + len(sources)), *rest) for piece, *rest in pieces] for pieces in blocks]
    return pl.pallas_call(
        functools.partial(project_kernel, sources=len(sources), blocks=blocks, sends=sends),
        out_shape=[jax.ShapeDtypeStruct((count, rows, half), jnp.float32) for count in counts],
        in_specs=in_smem(1) + [pl.BlockSpec(memory_space=pl.ANY)] * (len(sources) + len(weights)),
        out_specs=in_vmem(len(counts)),
        scratch_shapes=[
            pltpu.VMEM((len(sources), rows, units), sources[0].dtype),
            pltpu.VMEM((len(blocks), 2 * half, units), sources[0].dtype),
            pltpu.SemaphoreType.DMA((len(sources), ROW_COPIES)),
            pltpu.SemaphoreType.DMA((len(blocks), parts)),
        ],
        compiler_params=pltpu.CompilerParams(vmem_limit_bytes=PROJECT_LIMIT),
        cost_estimate=pl.CostEstimate(flops=1, bytes_accessed=1, transcendentals=0),
        name=name,
    )(flags, *sources, *weights)


def after(array, earlier):
    return lax.optimization_barrier((array, *earlier))[0] if earlier else array


def with_rows(array, units):
    flat = array.reshape(-1, array.shape[-1])
    spread = jnp.concatenate([flat[at : at + 8] for at in range(0, flat.shape[0], 8)], axis=1)
    return jnp.pad(spread, ((0, 0), (0, units - spread.shape[1])))


def from_rows(spreads, slot, shape):
    taken = []
    for spread in spreads:
        for at in range(shape[0] // 8):
            first = (slot * shape[0] // 8 + at) * shape[1]
            taken.append(spread[-8:, first : first + shape[1]])
    return jnp.concatenate(taken, axis=0)


def body(hidden_states, passage_states, down_weight, block_question, question_owner, decoder_states):
    blocks, block_len, units = hidden_states.shape
    width = passage_states.shape[2]
    query_len = decoder_states.shape[1]
    highs, lows, cores = lax.axis_size("high"), lax.axis_size("low"), lax.axis_size("mp")
    group, high, side, low, core = (lax.axis_index(name) for name in ("groups", "high", "side", "low", "mp"))
    shard = down_weight.shape[0]
    stride = lows * shard
    held = width // 2 // cores
    heads = held // HEAD_DIM
    members = highs * lows
    slot_total = question_owner.shape[0]
    rows = blocks * block_len
    lined = highs == 4 and lows == 1 and stride % (cores * 128) == 0
    span = stride // cores if lined else stride
    spans = held // span

    def features(array, of_side):
        if lined:
            starts = [(at * 2 + of_side) * stride + core * span for at in range(spans)]
        else:
            starts = [((core * spans + at) * 2 + of_side) * stride for at in range(spans)]
        taken = [lax.dynamic_slice_in_dim(array, start, span, axis=array.ndim - 1) for start in starts]
        return jnp.concatenate(taken, axis=-1)

    def shifted(array, shift):
        return lax.ppermute(array, "high", [(at, (at + shift) % highs) for at in range(highs)])

    hidden = hidden_states.reshape(rows, units)
    partner_hidden = lax.ppermute(hidden, "side", SWAP)
    queries = jnp.concatenate([features(decoder_states, side), features(decoder_states, 1 - side)], axis=0)[None]
    passages = passage_states.reshape(rows, width)
    leaving = features(passages, 1 - side)

    if lined:
        half = shard // 2
        lengths = [half * FIRST_EIGHTHS // 8, half - half * FIRST_EIGHTHS // 8]
        sent = [
            lax.dynamic_slice_in_dim(down_weight, group * half + first, length, axis=0)
            for first, length in zip((0, lengths[0]), lengths)
        ]
        sent[1] = jnp.concatenate([sent[1], with_rows(queries, units)], axis=0)
        below, above = [], []
        for at in range(2):
            below.append(shifted(after(sent[at], below[-1:]), 1))
            above.append(shifted(after(sent[at], above[-1:]), -1))
        opposite = [shifted(piece, 1) for piece in below]
        spreads = [piece[1][-8:] for piece in (sent, above, opposite, below)]
        *spreads, leaving, _ = lax.optimization_barrier(
            (*spreads, jnp.pad(leaving, ((0, highs * query_len), (0, 0))), partner_hidden)
        )
        own_queries, partner_queries = (from_rows(spreads, slot, (query_len, held)) for slot in range(2))
        leaving = lax.dynamic_update_slice(leaving, partner_queries, (rows, 0))
        first, second = lengths
        swapped = []
        for at, piece in enumerate([below[0], above[0], opposite[0], below[1], above[1], opposite[1]]):
            swapped.append(lax.ppermute(after(piece, swapped[max(at - 2, 0) : max(at - 1, 0)]), "groups", SWAP))
        far = swapped[2::3]
        flags = jnp.stack([core, (group == core).astype(core.dtype)])
        near_weights = [down_weight] + above + below + swapped[:2] + swapped[3:5]
        near = [
            [(("low", 0), 0, half, 0), (("high", 0), half, half, 0)],
            [
                (("came", 1), 0, first, 0),
                (("came", 2), 0, second, first),
                (("swapped", 6), 0, first, 0),
                (("swapped", 8), 0, second, first),
            ],
            [
                (("came", 3), 0, first, 0),
                (("came", 4), 0, second, first),
                (("swapped", 5), 0, first, 0),
                (("swapped", 7), 0, second, first),
            ],
        ]
        far_block = [
            (("came", 0), 0, first, 0),
            (("came", 1), 0, second, first),
            (("swapped", 2), 0, first, 0),
            (("swapped", 3), 0, second, first),
        ]
        spots = lax.rem(high + jnp.array([0, 1, 3, 2], jnp.int32), highs)
        spots = jnp.stack([(spots * 2 + side) * stride + core * span, spots * span])
        own_residual = passages

        kept, *away = project(
            flags, [hidden], near_weights, near, [2, 1], half, "project_own"
        )
        flags, kept, *away = lax.optimization_barrier((flags, kept, *away))
        partner_kept, *partner_away = project(
            flags, [partner_hidden], near_weights, near, [2, 1], half, "project_partner"
        )
        flags, partner_kept, *partner_away = lax.optimization_barrier((flags, partner_kept, *partner_away))
        far_kept, *far_away = project(
            flags, [hidden, partner_hidden], opposite + far, [far_block], [2], half, "project_far"
        )
        others = [lax.ppermute(piece, "mp", SWAP) for piece in away + partner_away + far_away]
        summands = [kept, partner_kept, far_kept] + others
        pieces = [(0, (0, at), [(3, 0), (3, 1), (4, 0)][at], at) for at in range(3)]
        pieces += [(1, (1, at), (5 + at // 2, at % 2), at) for at in range(3)]
        pieces += [(source, (2, source), (7, source), 3) for source in range(2)]
        origin = high
    else:
        queries = lax.all_gather(queries, ("high", "low"), axis=0, tiled=True)
        own_queries, partner_queries = (queries[:, slot].reshape(-1, held) for slot in range(2))
        leaving = jnp.concatenate([leaving, partner_queries], axis=0)
        weight = lax.all_gather(down_weight, ("high", "low"), axis=0, tiled=True)
        weight = jnp.where(core == 0, weight, jnp.roll(weight, held, axis=0))
        spots = jnp.zeros((2, 1), jnp.int32)
        own_residual = features(passages, side)
        summands, pieces = [], []
        for source, flat in enumerate((hidden, partner_hidden)):
            kept, away = (
                lax.dot_general(flat, part, (((1,), (1,)), ((), ())), preferred_element_type=jnp.float32)[None]
                for part in (weight[:held], weight[held:])
            )
            summands += [kept, lax.ppermute(away, "mp", SWAP)]
            pieces.append((source, (2 * source, 0), (2 * source + 1, 0), 0))
        origin = 0

    questions = block_question[:, 0]
    question_ids = jnp.arange(slot_total, dtype=jnp.int32)
    owners = jnp.sum(jnp.where(questions[:, None] == question_ids[None, :], question_owner[None, :], 0), axis=1)
    owner_high, owner_side, owner_low = owners // (2 * lows), (owners // lows) % 2, owners % lows
    owner_high = lax.rem(owner_high - origin + highs, highs)
    owner_place = (owner_high * lows + owner_low) * 2 + (owner_side != side)
    own_at = ((high * 2 + side) * lows + low) * blocks
    partner_at = ((high * 2 + 1 - side) * lows + low) * blocks
    places = jnp.concatenate(
        [lax.dynamic_slice_in_dim(owner_place, at, blocks) for at in (own_at, partner_at)]
    )

    partner = lax.ppermute(leaving, "side", SWAP)
    packed = (members, 2 * held // 128 * query_len + 8, 128)
    operands = summands + [own_residual, partner]
    partials = pl.pallas_call(
        functools.partial(attend_kernel, pieces=pieces),
        out_shape=jax.ShapeDtypeStruct(packed, jnp.float32),
        in_specs=in_smem(2) + in_vmem(1 + len(operands)),
        out_specs=pl.BlockSpec(memory_space=pltpu.VMEM),
        scratch_shapes=[pltpu.VMEM((2 * blocks, block_len, held), jnp.bfloat16)],
        compiler_params=pltpu.CompilerParams(vmem_limit_bytes=VMEM_LIMIT),
        name="attend",
    )(places, spots, own_queries, *operands)
    if lined:
        received = [partials[0:1]] + [shifted(partials[ahead : ahead + 1], ahead) for ahead in range(1, highs)]
    else:
        received = [lax.all_to_all(partials, ("high", "low"), split_axis=0, concat_axis=0, tiled=True)]
    merged = pl.pallas_call(
        merge_kernel,
        out_shape=jax.ShapeDtypeStruct((2, query_len, held), decoder_states.dtype),
        in_specs=in_vmem(len(received)),
        out_specs=pl.BlockSpec(memory_space=pltpu.VMEM),
        compiler_params=pltpu.CompilerParams(vmem_limit_bytes=VMEM_LIMIT),
        name="merge",
    )(*received)

    mine, away = merged[0:1], merged[1:2]
    by_core = lax.ppermute(mine, "mp", SWAP)
    by_side = lax.ppermute(away, "side", SWAP)
    by_both = lax.ppermute(away, ("side", "mp"), CROSS)
    if lined:
        order = [(at, of_side, of) for at in range(spans) for of_side in range(2) for of in range(cores)]
    else:
        order = [(at, of_side, of) for of in range(cores) for at in range(spans) for of_side in range(2)]
    flags = jnp.stack([side, core])
    order = [(of_side, of, at * span) for at, of_side, of in order]
    return pl.pallas_call(
        functools.partial(assemble_kernel, order=order, span=span),
        out_shape=jax.ShapeDtypeStruct((1, query_len, width), decoder_states.dtype),
        in_specs=in_smem(1) + in_vmem(4),
        out_specs=pl.BlockSpec(memory_space=pltpu.VMEM),
        compiler_params=pltpu.CompilerParams(vmem_limit_bytes=VMEM_LIMIT),
        name="assemble",
    )(flags, mine, by_core, by_side, by_both)


def solution(mesh):
    groups, dp, cores = mesh.shape["groups"], mesh.shape["dp"], mesh.shape["mp"]

    def run(hidden_states, passage_states, down_weight, block_question, question_owner, decoder_states):
        lows = max(1, HEAD_DIM * dp // down_weight.shape[0])
        fine = Mesh(
            mesh.devices.reshape(groups, dp // (2 * lows), 2, lows, cores),
            ("groups", "high", "side", "low", "mp"),
        )
        split = ("groups", "high", "side", "low")
        placed = (
            P(split, None, "mp"),
            P(split, None, None),
            P(("high", "side", "low"), "mp"),
            P("groups", None),
            P("groups"),
            P(split, None, None),
        )
        return jax.shard_map(
            body, mesh=fine, in_specs=placed, out_specs=P(split, None, None), check_vma=False
        )(hidden_states, passage_states, down_weight, block_question, question_owner, decoder_states)

    return run
```

```python
import functools
import math

import jax
import jax.numpy as jnp
from jax import lax
from jax.experimental import pallas as pl
from jax.experimental.pallas import tpu as pltpu
from jax.sharding import Mesh, PartitionSpec as P

HEAD_DIM = 64
EMPTY = -3e38
FIRST_EIGHTHS = 4
ROW_COPIES = 4
PROJECT_LIMIT = 30 * 1024 * 1024
VMEM_LIMIT = 22 * 1024 * 1024
SWAP = [(0, 1), (1, 0)]
CROSS = [(0, 3), (3, 0), (1, 2), (2, 1)]


def head_pick(tall, query_len):
    lanes = tall.shape[1]
    lane_head = lax.broadcasted_iota(jnp.int32, (query_len, lanes), 1) // HEAD_DIM
    picked = jnp.zeros((query_len, lanes), jnp.float32)
    for head in range(lanes // HEAD_DIM):
        picked = jnp.where(lane_head == head, tall[head * query_len : (head + 1) * query_len, :], picked)
    return picked


def project_kernel(flag_ref, hidden_ref, partner_ref, *refs, blocks, sends):
    *refs, rows_ref, block_ref, semaphores = refs
    keep_ref, *send_refs = refs[-1 - len(sends) :]
    slots = [(ref, at) for ref in send_refs for at in range(ref.shape[0])]
    core, same = flag_ref[0], flag_ref[1]
    half = keep_ref.shape[2]
    step = rows_ref.shape[0] // ROW_COPIES
    copies = []
    for part in range(ROW_COPIES):
        rows = pl.ds(part * step, step)
        copies.append(pltpu.make_async_copy(partner_ref.at[rows], rows_ref.at[rows], semaphores.at[part]))
        copies[-1].start()
    for at, (came, swapped) in enumerate(blocks):
        if not swapped:
            block_ref[at, :half] = refs[came][pl.ds(pl.multiple_of(core * half, half), half), :]
            block_ref[at, half:] = refs[came][pl.ds(pl.multiple_of((1 - core) * half, half), half), :]
        for pieces, where in ((came, (1 - same) * half), (swapped, same * half)) if swapped else ():
            for operand, first, length in pieces:
                place = pl.multiple_of(where + first, 16)
                block_ref[at, pl.ds(place, length)] = refs[operand][:length]
    for source, source_ref in enumerate((hidden_ref, rows_ref)):
        for copy in copies if source else []:
            copy.wait()
        for at in range(len(blocks)):
            product = lax.dot_general(
                source_ref[...], block_ref[at], (((1,), (1,)), ((), ())), preferred_element_type=jnp.float32
            )
            keep_ref[source * len(blocks) + at] = product[:, :half]
            send_ref, slot = slots[source * len(blocks) + at]
            send_ref[slot] = product[:, half:]


def attend_kernel(place_ref, spot_ref, query_ref, *refs, pieces):
    *refs, own_ref, partner_ref, out_ref, key_ref = refs
    residuals = own_ref, partner_ref
    partner_queries = own_ref.shape[0]
    held = query_ref.shape[1]
    query_len = query_ref.shape[0] // out_ref.shape[0]
    block_len = key_ref.shape[1]
    heads = held // HEAD_DIM
    tall = heads * query_len
    members, packed_rows, lanes_packed = out_ref.shape
    extra = packed_rows - 8
    row = lax.broadcasted_iota(jnp.int32, out_ref.shape, 1)
    out_ref[...] = jnp.where((row == extra) | (row == extra + 1), EMPTY, 0.0)
    row_head = lax.broadcasted_iota(jnp.int32, (tall, held), 0) // query_len
    lane_head = lax.broadcasted_iota(jnp.int32, (tall, held), 1) // HEAD_DIM
    diagonal = row_head == lane_head
    square = lax.broadcasted_iota(jnp.int32, (tall, tall), 0) == lax.broadcasted_iota(jnp.int32, (tall, tall), 1)
    ext = lax.broadcasted_iota(jnp.int32, (8, tall), 0)
    blocks = key_ref.shape[0] // 2
    for source, kept, sent, spot in pieces:
        keep, other = (refs[summand].at[piece] for summand, piece in (kept, sent))
        residual = residuals[source]
        span = keep.shape[1]
        lanes, given = (pl.ds(pl.multiple_of(spot_ref[of, spot], 128), span) for of in (1, source))
        for block in range(blocks):
            rows = slice(block * block_len, (block + 1) * block_len)
            key_ref[source * blocks + block, :, lanes] = (
                residual[rows, given].astype(jnp.float32) + (keep[rows, :] + other[rows, :])
            ).astype(jnp.bfloat16)
    places, scores, tops = [], [], []
    for at in range(key_ref.shape[0]):
        place = place_ref[at]
        first = pl.multiple_of(place // 2 * query_len, query_len)
        own_query = query_ref[pl.ds(first, query_len), :]
        partner_query = partner_ref[pl.ds(partner_queries + first, query_len), :]
        query = jnp.where(place % 2 == 0, own_query, partner_query)
        query = jnp.concatenate([query] * heads, axis=0)
        query = jnp.where(diagonal, query, jnp.zeros_like(query))
        score = lax.dot_general(
            query, key_ref[at], (((1,), (1,)), ((), ())), preferred_element_type=jnp.float32
        )
        places.append(place)
        scores.append(score)
        tops.append(jnp.max(score, axis=1, keepdims=True))
    for at, place in enumerate(places):
        top = tops[at]
        for other_at, other_place in enumerate(places):
            if other_at != at:
                top = jnp.maximum(top, jnp.where(other_place == place, tops[other_at], EMPTY))
        weights = jnp.exp(scores[at] - top)
        total = jnp.sum(weights, axis=1, keepdims=True)
        blend = lax.dot_general(
            weights.astype(jnp.bfloat16), key_ref[at], (((1,), (0,)), ((), ())),
            preferred_element_type=jnp.float32,
        )
        top_row = jnp.sum(jnp.where(square, top, 0.0), axis=0, keepdims=True)
        total_row = jnp.sum(jnp.where(square, total, 0.0), axis=0, keepdims=True)
        blend = head_pick(blend, query_len)
        member, slot = place // 2, place % 2
        for block in range(held // lanes_packed):
            first = pl.multiple_of(slot * (extra // 2) + block * query_len, query_len)
            lanes = slice(block * lanes_packed, (block + 1) * lanes_packed)
            spot = pl.ds(first, query_len)
            out_ref[member, spot, :] = out_ref[member, spot, :] + blend[:, lanes]
        before = out_ref[member, extra:, :]
        out_ref[member, extra:, :] = jnp.where(
            ext == slot, top_row, jnp.where(ext == slot + 2, before + total_row, before)
        )


def merge_kernel(*refs):
    out_ref = refs[-1]
    parts = refs[:-1]
    query_len, held = out_ref.shape[1:]
    tall = held // HEAD_DIM * query_len
    square = lax.broadcasted_iota(jnp.int32, (tall, tall), 0) == lax.broadcasted_iota(jnp.int32, (tall, tall), 1)

    def over(start, step):
        for part in parts:
            start = lax.fori_loop(
                0, part.shape[0], functools.partial(step, part), start, unroll=part.shape[0] <= 8
            )
        return start

    packed_rows, lanes_packed = parts[0].shape[1:]
    extra = packed_rows - 8
    for slot in range(out_ref.shape[0]):
        top_row, total_row = (slice(extra + slot + at, extra + slot + at + 1) for at in (0, 2))

        def top_step(part, at, top):
            return jnp.maximum(top, part[at, top_row, :])

        def total_step(part, at, total):
            return total + jnp.exp(part[at, top_row, :] - top) * part[at, total_row, :]

        def blend_step(part, at, blend):
            share = jnp.exp(part[at, top_row, :] - top) / total
            column = jnp.sum(jnp.where(square, share, 0.0), axis=1, keepdims=True)
            spread = head_pick(jnp.broadcast_to(column, (tall, held)), query_len)
            first = slot * (extra // 2)
            rows = [
                part[at, first + block * query_len : first + (block + 1) * query_len, :]
                for block in range(held // lanes_packed)
            ]
            return blend + spread * jnp.concatenate(rows, axis=1)

        top = over(jnp.full((1, tall), EMPTY, jnp.float32), top_step)
        total = over(jnp.zeros((1, tall), jnp.float32), total_step)
        blend = over(jnp.zeros((query_len, held), jnp.float32), blend_step)
        out_ref[slot] = blend.astype(out_ref.dtype)


def assemble_kernel(flag_ref, mine_ref, core_ref, side_ref, both_ref, out_ref, *, order, span):
    side, core = flag_ref[0], flag_ref[1]
    mine, by_core, by_side, by_both = (ref[0] for ref in (mine_ref, core_ref, side_ref, both_ref))
    taken = {}
    for of_side in range(2):
        for of in range(2):
            near = jnp.where(core == of, mine, by_core)
            far = jnp.where(core == of, by_side, by_both)
            taken[of_side, of] = jnp.where(side == of_side, near, far)
    out_ref[0] = jnp.concatenate(
        [taken[of_side, of][:, first : first + span] for of_side, of, first in order], axis=1
    )


def in_vmem(count):
    return [pl.BlockSpec(memory_space=pltpu.VMEM)] * count


def in_smem(count):
    return [pl.BlockSpec(memory_space=pltpu.SMEM)] * count


def project(flags, hidden, partner, weights, blocks, sends, half):
    rows, units = hidden.shape
    counts = [2 * len(blocks)] + sends
    return pl.pallas_call(
        functools.partial(project_kernel, blocks=blocks, sends=sends),
        out_shape=[jax.ShapeDtypeStruct((count, rows, half), jnp.float32) for count in counts],
        in_specs=in_smem(1) + in_vmem(1) + [pl.BlockSpec(memory_space=pl.ANY)] + in_vmem(len(weights)),
        out_specs=in_vmem(len(counts)),
        scratch_shapes=[
            pltpu.VMEM((rows, units), hidden.dtype),
            pltpu.VMEM((len(blocks), 2 * half, units), hidden.dtype),
            pltpu.SemaphoreType.DMA((ROW_COPIES,)),
        ],
        compiler_params=pltpu.CompilerParams(vmem_limit_bytes=PROJECT_LIMIT),
        cost_estimate=pl.CostEstimate(flops=1, bytes_accessed=1, transcendentals=0),
        name="project",
    )(flags, hidden, partner, *weights)


def after(array, earlier):
    return lax.optimization_barrier((array, *earlier))[0] if earlier else array


def with_rows(array, units):
    flat = array.reshape(-1, array.shape[-1])
    spread = jnp.concatenate([flat[at : at + 8] for at in range(0, flat.shape[0], 8)], axis=1)
    return jnp.pad(spread, ((0, 0), (0, units - spread.shape[1])))


def from_rows(spreads, slot, shape):
    taken = []
    for spread in spreads:
        for at in range(shape[0] // 8):
            first = (slot * shape[0] // 8 + at) * shape[1]
            taken.append(spread[-8:, first : first + shape[1]])
    return jnp.concatenate(taken, axis=0)


def body(hidden_states, passage_states, down_weight, block_question, question_owner, decoder_states):
    blocks, block_len, units = hidden_states.shape
    width = passage_states.shape[2]
    query_len = decoder_states.shape[1]
    highs, lows, cores = lax.axis_size("high"), lax.axis_size("low"), lax.axis_size("mp")
    group, high, side, low, core = (lax.axis_index(name) for name in ("groups", "high", "side", "low", "mp"))
    shard = down_weight.shape[0]
    stride = lows * shard
    held = width // 2 // cores
    heads = held // HEAD_DIM
    members = highs * lows
    slot_total = question_owner.shape[0]
    rows = blocks * block_len
    lined = highs == 4 and lows == 1 and stride % (cores * 128) == 0
    span = stride // cores if lined else stride
    spans = held // span

    def features(array, of_side):
        if lined:
            starts = [(at * 2 + of_side) * stride + core * span for at in range(spans)]
        else:
            starts = [((core * spans + at) * 2 + of_side) * stride for at in range(spans)]
        taken = [lax.dynamic_slice_in_dim(array, start, span, axis=array.ndim - 1) for start in starts]
        return jnp.concatenate(taken, axis=-1)

    def shifted(array, shift):
        return lax.ppermute(array, "high", [(at, (at + shift) % highs) for at in range(highs)])

    hidden = hidden_states.reshape(rows, units)
    partner_hidden = lax.ppermute(hidden, "side", SWAP)
    queries = jnp.concatenate([features(decoder_states, side), features(decoder_states, 1 - side)], axis=0)[None]
    passages = passage_states.reshape(rows, width)
    leaving = features(passages, 1 - side)

    if lined:
        half = shard // 2
        lengths = [half * FIRST_EIGHTHS // 8, half - half * FIRST_EIGHTHS // 8]
        sent = [
            lax.dynamic_slice_in_dim(down_weight, group * half + first, length, axis=0)
            for first, length in zip((0, lengths[0]), lengths)
        ]
        sent[1] = jnp.concatenate([sent[1], with_rows(queries, units)], axis=0)
        below, above = [], []
        for at in range(2):
            below.append(shifted(after(sent[at], below[-1:]), 1))
            above.append(shifted(after(sent[at], above[-1:]), -1))
        opposite = [shifted(piece, 1) for piece in below]
        spreads = [piece[1][-8:] for piece in (sent, above, opposite, below)]
        *spreads, leaving, _ = lax.optimization_barrier(
            (*spreads, jnp.pad(leaving, ((0, highs * query_len), (0, 0))), partner_hidden)
        )
        own_queries, partner_queries = (from_rows(spreads, slot, (query_len, held)) for slot in range(2))
        leaving = lax.dynamic_update_slice(leaving, partner_queries, (rows, 0))
        first, second = lengths
        swapped = []
        for at, piece in enumerate([below[0], above[0], opposite[0], below[1], above[1], opposite[1]]):
            swapped.append(lax.ppermute(after(piece, swapped[max(at - 2, 0) : max(at - 1, 0)]), "groups", SWAP))
        flags = jnp.stack([core, (group == core).astype(core.dtype)])
        weights = [down_weight] + above + below + opposite + swapped
        starts = list(zip((0, first), lengths))
        blocks_of = [(0, None)]
        for came, other in ((1, 8), (3, 7), (5, 9)):
            blocks_of.append(tuple([(of + at * hop, *starts[at]) for at in range(2)] for of, hop in ((came, 1), (other, 3))))
        spots = lax.rem(high + jnp.array([0, 1, 3, 2], jnp.int32), highs)
        spots = jnp.stack([(spots * 2 + side) * stride + core * span, spots * span])
        own_residual = passages

        kept, *away = project(flags, hidden, partner_hidden, weights, blocks_of, [2, 2, 2, 2], half)
        summands = [kept] + [lax.ppermute(piece, "mp", SWAP) for piece in away]
        pieces = [(at // 4, (0, at), (1 + at // 2, at % 2), at % 4) for at in range(8)]
        origin = high
    else:
        queries = lax.all_gather(queries, ("high", "low"), axis=0, tiled=True)
        own_queries, partner_queries = (queries[:, slot].reshape(-1, held) for slot in range(2))
        leaving = jnp.concatenate([leaving, partner_queries], axis=0)
        weight = lax.all_gather(down_weight, ("high", "low"), axis=0, tiled=True)
        weight = jnp.where(core == 0, weight, jnp.roll(weight, held, axis=0))
        spots = jnp.zeros((2, 1), jnp.int32)
        own_residual = features(passages, side)
        summands, pieces = [], []
        for source, flat in enumerate((hidden, partner_hidden)):
            kept, away = (
                lax.dot_general(flat, part, (((1,), (1,)), ((), ())), preferred_element_type=jnp.float32)[None]
                for part in (weight[:held], weight[held:])
            )
            summands += [kept, lax.ppermute(away, "mp", SWAP)]
            pieces.append((source, (2 * source, 0), (2 * source + 1, 0), 0))
        origin = 0

    questions = block_question[:, 0]
    question_ids = jnp.arange(slot_total, dtype=jnp.int32)
    owners = jnp.sum(jnp.where(questions[:, None] == question_ids[None, :], question_owner[None, :], 0), axis=1)
    owner_high, owner_side, owner_low = owners // (2 * lows), (owners // lows) % 2, owners % lows
    owner_high = lax.rem(owner_high - origin + highs, highs)
    owner_place = (owner_high * lows + owner_low) * 2 + (owner_side != side)
    own_at = ((high * 2 + side) * lows + low) * blocks
    partner_at = ((high * 2 + 1 - side) * lows + low) * blocks
    places = jnp.concatenate(
        [lax.dynamic_slice_in_dim(owner_place, at, blocks) for at in (own_at, partner_at)]
    )

    partner = lax.ppermute(leaving, "side", SWAP)
    packed = (members, 2 * held // 128 * query_len + 8, 128)
    operands = summands + [own_residual, partner]
    partials = pl.pallas_call(
        functools.partial(attend_kernel, pieces=pieces),
        out_shape=jax.ShapeDtypeStruct(packed, jnp.float32),
        in_specs=in_smem(2) + in_vmem(1 + len(operands)),
        out_specs=pl.BlockSpec(memory_space=pltpu.VMEM),
        scratch_shapes=[pltpu.VMEM((2 * blocks, block_len, held), jnp.bfloat16)],
        compiler_params=pltpu.CompilerParams(vmem_limit_bytes=VMEM_LIMIT),
        name="attend",
    )(places, spots, own_queries, *operands)
    if lined:
        received = [partials[0:1]] + [shifted(partials[ahead : ahead + 1], ahead) for ahead in range(1, highs)]
    else:
        received = [lax.all_to_all(partials, ("high", "low"), split_axis=0, concat_axis=0, tiled=True)]
    merged = pl.pallas_call(
        merge_kernel,
        out_shape=jax.ShapeDtypeStruct((2, query_len, held), decoder_states.dtype),
        in_specs=in_vmem(len(received)),
        out_specs=pl.BlockSpec(memory_space=pltpu.VMEM),
        compiler_params=pltpu.CompilerParams(vmem_limit_bytes=VMEM_LIMIT),
        name="merge",
    )(*received)

    mine, away = merged[0:1], merged[1:2]
    by_core = lax.ppermute(mine, "mp", SWAP)
    by_side = lax.ppermute(away, "side", SWAP)
    by_both = lax.ppermute(away, ("side", "mp"), CROSS)
    if lined:
        order = [(at, of_side, of) for at in range(spans) for of_side in range(2) for of in range(cores)]
    else:
        order = [(at, of_side, of) for of in range(cores) for at in range(spans) for of_side in range(2)]
    flags = jnp.stack([side, core])
    order = [(of_side, of, at * span) for at, of_side, of in order]
    return pl.pallas_call(
        functools.partial(assemble_kernel, order=order, span=span),
        out_shape=jax.ShapeDtypeStruct((1, query_len, width), decoder_states.dtype),
        in_specs=in_smem(1) + in_vmem(4),
        out_specs=pl.BlockSpec(memory_space=pltpu.VMEM),
        compiler_params=pltpu.CompilerParams(vmem_limit_bytes=VMEM_LIMIT),
        name="assemble",
    )(flags, mine, by_core, by_side, by_both)


def solution(mesh):
    groups, dp, cores = mesh.shape["groups"], mesh.shape["dp"], mesh.shape["mp"]

    def run(hidden_states, passage_states, down_weight, block_question, question_owner, decoder_states):
        lows = max(1, HEAD_DIM * dp // down_weight.shape[0])
        fine = Mesh(
            mesh.devices.reshape(groups, dp // (2 * lows), 2, lows, cores),
            ("groups", "high", "side", "low", "mp"),
        )
        split = ("groups", "high", "side", "low")
        placed = (
            P(split, None, "mp"),
            P(split, None, None),
            P(("high", "side", "low"), "mp"),
            P("groups", None),
            P("groups"),
            P(split, None, None),
        )
        return jax.shard_map(
            body, mesh=fine, in_specs=placed, out_specs=P(split, None, None), check_vma=False
        )(hidden_states, passage_states, down_weight, block_question, question_owner, decoder_states)

    return run
```

```python
import functools
import math

import jax
import jax.numpy as jnp
from jax import lax
from jax.experimental import pallas as pl
from jax.experimental.pallas import tpu as pltpu
from jax.sharding import Mesh, PartitionSpec as P

HEAD_DIM = 64
EMPTY = -3e38
FIRST_EIGHTHS = 3
ROW_COPIES = 4
PROJECT_LIMIT = 24 * 1024 * 1024
VMEM_LIMIT = 22 * 1024 * 1024
SWAP = [(0, 1), (1, 0)]
CROSS = [(0, 3), (3, 0), (1, 2), (2, 1)]


def head_pick(tall, query_len):
    lanes = tall.shape[1]
    lane_head = lax.broadcasted_iota(jnp.int32, (query_len, lanes), 1) // HEAD_DIM
    picked = jnp.zeros((query_len, lanes), jnp.float32)
    for head in range(lanes // HEAD_DIM):
        picked = jnp.where(lane_head == head, tall[head * query_len : (head + 1) * query_len, :], picked)
    return picked


def join(block_ref, at, block, refs, core, same):
    came, swapped = block
    half = block_ref.shape[1] // 2
    if not swapped:
        block_ref[at, :half] = refs[came][pl.ds(pl.multiple_of(core * half, half), half), :]
        block_ref[at, half:] = refs[came][pl.ds(pl.multiple_of((1 - core) * half, half), half), :]
        return
    for pieces, where in ((came, (1 - same) * half), (swapped, same * half)):
        for operand, first, length in pieces:
            block_ref[at, pl.ds(pl.multiple_of(where + first, 16), length)] = refs[operand][:length]


def multiply(rows, block, keep_ref, send_ref, at, where):
    slot = at % send_ref.shape[0]
    product = lax.dot_general(rows, block, (((1,), (1,)), ((), ())), preferred_element_type=jnp.float32)
    half = product.shape[1] // 2
    keep_ref[at, where, :] = product[:, :half]
    send_ref[slot, where, :] = product[:, half:]


def join_kernel(flag_ref, *refs, sources, blocks):
    *refs, keep_ref, send_ref, block_ref = refs
    for at, block in enumerate(blocks):
        join(block_ref, at, block, refs[sources:], flag_ref[0], flag_ref[1])
    for source in range(sources):
        for at in range(len(blocks)):
            multiply(
                refs[source][...], block_ref[at], keep_ref, send_ref, source * len(blocks) + at, slice(None)
            )


def partner_kernel(partner_ref, block_ref, keep_ref, send_ref, rows_ref, last_ref, semaphores):
    step = rows_ref.shape[0] // ROW_COPIES
    copies = []
    for part in range(ROW_COPIES):
        rows = pl.ds(part * step, step)
        copies.append(pltpu.make_async_copy(partner_ref.at[rows], rows_ref.at[rows], semaphores.at[part]))
        copies[-1].start()
    for part in range(2):
        where = slice(part * rows_ref.shape[0] // 2, (part + 1) * rows_ref.shape[0] // 2)
        for copy in copies[part * ROW_COPIES // 2 : (part + 1) * ROW_COPIES // 2]:
            copy.wait()
        for at in range(block_ref.shape[0]):
            last = at == block_ref.shape[0] - 1
            multiply(rows_ref[where, :], block_ref[at], keep_ref, last_ref if last else send_ref, at, where)


def attend_kernel(place_ref, spot_ref, query_ref, *refs, pieces):
    *refs, own_ref, partner_ref, out_ref, key_ref = refs
    residuals = own_ref, partner_ref
    partner_queries = own_ref.shape[0]
    held = query_ref.shape[1]
    query_len = query_ref.shape[0] // out_ref.shape[0]
    block_len = key_ref.shape[1]
    heads = held // HEAD_DIM
    tall = heads * query_len
    members, packed_rows, lanes_packed = out_ref.shape
    extra = packed_rows - 8
    row = lax.broadcasted_iota(jnp.int32, out_ref.shape, 1)
    out_ref[...] = jnp.where((row == extra) | (row == extra + 1), EMPTY, 0.0)
    row_head = lax.broadcasted_iota(jnp.int32, (tall, held), 0) // query_len
    lane_head = lax.broadcasted_iota(jnp.int32, (tall, held), 1) // HEAD_DIM
    diagonal = row_head == lane_head
    square = lax.broadcasted_iota(jnp.int32, (tall, tall), 0) == lax.broadcasted_iota(jnp.int32, (tall, tall), 1)
    ext = lax.broadcasted_iota(jnp.int32, (8, tall), 0)
    blocks = key_ref.shape[0] // 2
    for source, kept, sent, spot in pieces:
        keep, other = (refs[summand].at[piece] for summand, piece in (kept, sent))
        residual = residuals[source]
        span = keep.shape[1]
        lanes, given = (pl.ds(pl.multiple_of(spot_ref[of, spot], 128), span) for of in (1, source))
        for block in range(blocks):
            rows = slice(block * block_len, (block + 1) * block_len)
            key_ref[source * blocks + block, :, lanes] = (
                residual[rows, given].astype(jnp.float32) + (keep[rows, :] + other[rows, :])
            ).astype(jnp.bfloat16)
    places, scores, tops = [], [], []
    for at in range(key_ref.shape[0]):
        place = place_ref[at]
        first = pl.multiple_of(place // 2 * query_len, query_len)
        own_query = query_ref[pl.ds(first, query_len), :]
        partner_query = partner_ref[pl.ds(partner_queries + first, query_len), :]
        query = jnp.where(place % 2 == 0, own_query, partner_query)
        query = jnp.concatenate([query] * heads, axis=0)
        query = jnp.where(diagonal, query, jnp.zeros_like(query))
        score = lax.dot_general(
            query, key_ref[at], (((1,), (1,)), ((), ())), preferred_element_type=jnp.float32
        )
        places.append(place)
        scores.append(score)
        tops.append(jnp.max(score, axis=1, keepdims=True))
    for at, place in enumerate(places):
        top = tops[at]
        for other_at, other_place in enumerate(places):
            if other_at != at:
                top = jnp.maximum(top, jnp.where(other_place == place, tops[other_at], EMPTY))
        weights = jnp.exp(scores[at] - top)
        total = jnp.sum(weights, axis=1, keepdims=True)
        blend = lax.dot_general(
            weights.astype(jnp.bfloat16), key_ref[at], (((1,), (0,)), ((), ())),
            preferred_element_type=jnp.float32,
        )
        top_row = jnp.sum(jnp.where(square, top, 0.0), axis=0, keepdims=True)
        total_row = jnp.sum(jnp.where(square, total, 0.0), axis=0, keepdims=True)
        blend = head_pick(blend, query_len)
        member, slot = place // 2, place % 2
        for block in range(held // lanes_packed):
            first = pl.multiple_of(slot * (extra // 2) + block * query_len, query_len)
            lanes = slice(block * lanes_packed, (block + 1) * lanes_packed)
            spot = pl.ds(first, query_len)
            out_ref[member, spot, :] = out_ref[member, spot, :] + blend[:, lanes]
        before = out_ref[member, extra:, :]
        out_ref[member, extra:, :] = jnp.where(
            ext == slot, top_row, jnp.where(ext == slot + 2, before + total_row, before)
        )


def merge_kernel(*refs):
    out_ref = refs[-1]
    parts = refs[:-1]
    query_len, held = out_ref.shape[1:]
    tall = held // HEAD_DIM * query_len
    square = lax.broadcasted_iota(jnp.int32, (tall, tall), 0) == lax.broadcasted_iota(jnp.int32, (tall, tall), 1)

    def over(start, step):
        for part in parts:
            start = lax.fori_loop(
                0, part.shape[0], functools.partial(step, part), start, unroll=part.shape[0] <= 8
            )
        return start

    packed_rows, lanes_packed = parts[0].shape[1:]
    extra = packed_rows - 8
    for slot in range(out_ref.shape[0]):
        top_row, total_row = (slice(extra + slot + at, extra + slot + at + 1) for at in (0, 2))

        def top_step(part, at, top):
            return jnp.maximum(top, part[at, top_row, :])

        def total_step(part, at, total):
            return total + jnp.exp(part[at, top_row, :] - top) * part[at, total_row, :]

        def blend_step(part, at, blend):
            share = jnp.exp(part[at, top_row, :] - top) / total
            column = jnp.sum(jnp.where(square, share, 0.0), axis=1, keepdims=True)
            spread = head_pick(jnp.broadcast_to(column, (tall, held)), query_len)
            first = slot * (extra // 2)
            rows = [
                part[at, first + block * query_len : first + (block + 1) * query_len, :]
                for block in range(held // lanes_packed)
            ]
            return blend + spread * jnp.concatenate(rows, axis=1)

        top = over(jnp.full((1, tall), EMPTY, jnp.float32), top_step)
        total = over(jnp.zeros((1, tall), jnp.float32), total_step)
        blend = over(jnp.zeros((query_len, held), jnp.float32), blend_step)
        out_ref[slot] = blend.astype(out_ref.dtype)


def assemble_kernel(flag_ref, mine_ref, core_ref, side_ref, both_ref, out_ref, *, order, span):
    side, core = flag_ref[0], flag_ref[1]
    mine, by_core, by_side, by_both = (ref[0] for ref in (mine_ref, core_ref, side_ref, both_ref))
    taken = {}
    for of_side in range(2):
        for of in range(2):
            near = jnp.where(core == of, mine, by_core)
            far = jnp.where(core == of, by_side, by_both)
            taken[of_side, of] = jnp.where(side == of_side, near, far)
    out_ref[0] = jnp.concatenate(
        [taken[of_side, of][:, first : first + span] for of_side, of, first in order], axis=1
    )


def in_vmem(count):
    return [pl.BlockSpec(memory_space=pltpu.VMEM)] * count


def in_smem(count):
    return [pl.BlockSpec(memory_space=pltpu.SMEM)] * count


def project(kernel, name, operands, placed, counts, rows, half, handed, scratch):
    return pl.pallas_call(
        kernel,
        out_shape=[jax.ShapeDtypeStruct((count, rows, half), jnp.float32) for count in counts] + handed,
        in_specs=placed,
        out_specs=in_vmem(2 + len(handed)),
        scratch_shapes=scratch,
        compiler_params=pltpu.CompilerParams(vmem_limit_bytes=PROJECT_LIMIT),
        cost_estimate=pl.CostEstimate(flops=1, bytes_accessed=1, transcendentals=0),
        name=name,
    )(*operands)


def after(array, earlier):
    return lax.optimization_barrier((array, *earlier))[0] if earlier else array


def with_rows(array, units):
    flat = array.reshape(-1, array.shape[-1])
    spread = jnp.concatenate([flat[at : at + 8] for at in range(0, flat.shape[0], 8)], axis=1)
    return jnp.pad(spread, ((0, 0), (0, units - spread.shape[1])))


def from_rows(spreads, slot, shape):
    taken = []
    for spread in spreads:
        for at in range(shape[0] // 8):
            first = (slot * shape[0] // 8 + at) * shape[1]
            taken.append(spread[-8:, first : first + shape[1]])
    return jnp.concatenate(taken, axis=0)


def body(hidden_states, passage_states, down_weight, block_question, question_owner, decoder_states):
    blocks, block_len, units = hidden_states.shape
    width = passage_states.shape[2]
    query_len = decoder_states.shape[1]
    highs, lows, cores = lax.axis_size("high"), lax.axis_size("low"), lax.axis_size("mp")
    group, high, side, low, core = (lax.axis_index(name) for name in ("groups", "high", "side", "low", "mp"))
    shard = down_weight.shape[0]
    stride = lows * shard
    held = width // 2 // cores
    heads = held // HEAD_DIM
    members = highs * lows
    slot_total = question_owner.shape[0]
    rows = blocks * block_len
    lined = highs == 4 and lows == 1 and stride % (cores * 128) == 0
    span = stride // cores if lined else stride
    spans = held // span

    def features(array, of_side):
        if lined:
            starts = [(at * 2 + of_side) * stride + core * span for at in range(spans)]
        else:
            starts = [((core * spans + at) * 2 + of_side) * stride for at in range(spans)]
        taken = [lax.dynamic_slice_in_dim(array, start, span, axis=array.ndim - 1) for start in starts]
        return jnp.concatenate(taken, axis=-1)

    def shifted(array, shift):
        return lax.ppermute(array, "high", [(at, (at + shift) % highs) for at in range(highs)])

    hidden = hidden_states.reshape(rows, units)
    partner_hidden = lax.ppermute(hidden, "side", SWAP)
    queries = jnp.concatenate([features(decoder_states, side), features(decoder_states, 1 - side)], axis=0)[None]
    passages = passage_states.reshape(rows, width)
    leaving = features(passages, 1 - side)

    if lined:
        half = shard // 2
        lengths = [half * FIRST_EIGHTHS // 8, half - half * FIRST_EIGHTHS // 8]
        sent = [
            lax.dynamic_slice_in_dim(down_weight, group * half + first, length, axis=0)
            for first, length in zip((0, lengths[0]), lengths)
        ]
        sent[1] = jnp.concatenate([sent[1], with_rows(queries, units)], axis=0)
        below, above = [], []
        for at in range(2):
            below.append(shifted(after(sent[at], below[-1:]), 1))
            above.append(shifted(after(sent[at], above[-1:]), -1))
        opposite = [shifted(piece, 1) for piece in below]
        spreads = [piece[1][-8:] for piece in (sent, above, opposite, below)]
        *spreads, leaving, _ = lax.optimization_barrier(
            (*spreads, jnp.pad(leaving, ((0, highs * query_len), (0, 0))), partner_hidden)
        )
        own_queries, partner_queries = (from_rows(spreads, slot, (query_len, held)) for slot in range(2))
        leaving = lax.dynamic_update_slice(leaving, partner_queries, (rows, 0))
        first, second = lengths
        swapped = []
        for at, piece in enumerate([below[0], above[0], opposite[0], below[1], above[1], opposite[1]]):
            swapped.append(lax.ppermute(after(piece, swapped[max(at - 2, 0) : max(at - 1, 0)]), "groups", SWAP))
        flags = jnp.stack([core, (group == core).astype(core.dtype)])
        near_pieces = [down_weight] + above + below + swapped[:2] + swapped[3:5]
        far_pieces = opposite + swapped[2::3]
        starts = list(zip((0, first), lengths))
        near = [(0, None)]
        for came, other in ((1, 6), (3, 5)):
            near.append(tuple([(of + at * hop, *starts[at]) for at in range(2)] for of, hop in ((came, 1), (other, 2))))
        far = [tuple([(of + at, *starts[at]) for at in range(2)] for of in (0, 2))]
        spots = lax.rem(high + jnp.array([0, 1, 3, 2], jnp.int32), highs)
        spots = jnp.stack([(spots * 2 + side) * stride + core * span, spots * span])
        own_residual = passages

        joined = jax.ShapeDtypeStruct((len(near), shard, units), down_weight.dtype)
        kept, away, joined = project(
            functools.partial(join_kernel, sources=1, blocks=near), "project_own", [flags, hidden] + near_pieces,
            in_smem(1) + in_vmem(1 + len(near_pieces)), [len(near)] * 2, rows, half, [joined], [],
        )
        partner_kept, partner_away, partner_rows, partner_last = project(
            partner_kernel, "project_partner", [partner_hidden, joined],
            [pl.BlockSpec(memory_space=pl.ANY)] + in_vmem(1), [len(near), len(near) - 1], rows, half,
            [jax.ShapeDtypeStruct(hidden.shape, hidden.dtype), jax.ShapeDtypeStruct((1, rows, half), jnp.float32)],
            [pltpu.SemaphoreType.DMA((ROW_COPIES,))],
        )
        far_kept, far_away = project(
            functools.partial(join_kernel, sources=2, blocks=far), "project_far",
            [flags, hidden, partner_rows] + far_pieces, in_smem(1) + in_vmem(2 + len(far_pieces)), [2, 2], rows, half,
            [], [pltpu.VMEM((1, shard, units), down_weight.dtype)],
        )
        summands = [kept, partner_kept, far_kept]
        summands += [lax.ppermute(piece, "mp", SWAP) for piece in (away, partner_away, partner_last, far_away)]
        pieces = [(0, (0, at), (3, at), at) for at in range(3)]
        pieces += [(1, (1, at), (4 + at // 2, at % 2), at) for at in range(3)]
        pieces += [(source, (2, source), (6, source), 3) for source in range(2)]
        origin = high
    else:
        queries = lax.all_gather(queries, ("high", "low"), axis=0, tiled=True)
        own_queries, partner_queries = (queries[:, slot].reshape(-1, held) for slot in range(2))
        leaving = jnp.concatenate([leaving, partner_queries], axis=0)
        weight = lax.all_gather(down_weight, ("high", "low"), axis=0, tiled=True)
        weight = jnp.where(core == 0, weight, jnp.roll(weight, held, axis=0))
        spots = jnp.zeros((2, 1), jnp.int32)
        own_residual = features(passages, side)
        summands, pieces = [], []
        for source, flat in enumerate((hidden, partner_hidden)):
            kept, away = (
                lax.dot_general(flat, part, (((1,), (1,)), ((), ())), preferred_element_type=jnp.float32)[None]
                for part in (weight[:held], weight[held:])
            )
            summands += [kept, lax.ppermute(away, "mp", SWAP)]
            pieces.append((source, (2 * source, 0), (2 * source + 1, 0), 0))
        origin = 0

    questions = block_question[:, 0]
    question_ids = jnp.arange(slot_total, dtype=jnp.int32)
    owners = jnp.sum(jnp.where(questions[:, None] == question_ids[None, :], question_owner[None, :], 0), axis=1)
    owner_high, owner_side, owner_low = owners // (2 * lows), (owners // lows) % 2, owners % lows
    owner_high = lax.rem(owner_high - origin + highs, highs)
    owner_place = (owner_high * lows + owner_low) * 2 + (owner_side != side)
    own_at = ((high * 2 + side) * lows + low) * blocks
    partner_at = ((high * 2 + 1 - side) * lows + low) * blocks
    places = jnp.concatenate(
        [lax.dynamic_slice_in_dim(owner_place, at, blocks) for at in (own_at, partner_at)]
    )

    partner = lax.ppermute(leaving, "side", SWAP)
    packed = (members, 2 * held // 128 * query_len + 8, 128)
    operands = summands + [own_residual, partner]
    partials = pl.pallas_call(
        functools.partial(attend_kernel, pieces=pieces),
        out_shape=jax.ShapeDtypeStruct(packed, jnp.float32),
        in_specs=in_smem(2) + in_vmem(1 + len(operands)),
        out_specs=pl.BlockSpec(memory_space=pltpu.VMEM),
        scratch_shapes=[pltpu.VMEM((2 * blocks, block_len, held), jnp.bfloat16)],
        compiler_params=pltpu.CompilerParams(vmem_limit_bytes=VMEM_LIMIT),
        name="attend",
    )(places, spots, own_queries, *operands)
    if lined:
        received = [partials[0:1]] + [shifted(partials[ahead : ahead + 1], ahead) for ahead in range(1, highs)]
    else:
        received = [lax.all_to_all(partials, ("high", "low"), split_axis=0, concat_axis=0, tiled=True)]
    merged = pl.pallas_call(
        merge_kernel,
        out_shape=jax.ShapeDtypeStruct((2, query_len, held), decoder_states.dtype),
        in_specs=in_vmem(len(received)),
        out_specs=pl.BlockSpec(memory_space=pltpu.VMEM),
        compiler_params=pltpu.CompilerParams(vmem_limit_bytes=VMEM_LIMIT),
        name="merge",
    )(*received)

    mine, away = merged[0:1], merged[1:2]
    by_core = lax.ppermute(mine, "mp", SWAP)
    by_side = lax.ppermute(away, "side", SWAP)
    by_both = lax.ppermute(away, ("side", "mp"), CROSS)
    if lined:
        order = [(at, of_side, of) for at in range(spans) for of_side in range(2) for of in range(cores)]
    else:
        order = [(at, of_side, of) for of in range(cores) for at in range(spans) for of_side in range(2)]
    flags = jnp.stack([side, core])
    order = [(of_side, of, at * span) for at, of_side, of in order]
    return pl.pallas_call(
        functools.partial(assemble_kernel, order=order, span=span),
        out_shape=jax.ShapeDtypeStruct((1, query_len, width), decoder_states.dtype),
        in_specs=in_smem(1) + in_vmem(4),
        out_specs=pl.BlockSpec(memory_space=pltpu.VMEM),
        compiler_params=pltpu.CompilerParams(vmem_limit_bytes=VMEM_LIMIT),
        name="assemble",
    )(flags, mine, by_core, by_side, by_both)


def solution(mesh):
    groups, dp, cores = mesh.shape["groups"], mesh.shape["dp"], mesh.shape["mp"]

    def run(hidden_states, passage_states, down_weight, block_question, question_owner, decoder_states):
        lows = max(1, HEAD_DIM * dp // down_weight.shape[0])
        fine = Mesh(
            mesh.devices.reshape(groups, dp // (2 * lows), 2, lows, cores),
            ("groups", "high", "side", "low", "mp"),
        )
        split = ("groups", "high", "side", "low")
        placed = (
            P(split, None, "mp"),
            P(split, None, None),
            P(("high", "side", "low"), "mp"),
            P("groups", None),
            P("groups"),
            P(split, None, None),
        )
        return jax.shard_map(
            body, mesh=fine, in_specs=placed, out_specs=P(split, None, None), check_vma=False
        )(hidden_states, passage_states, down_weight, block_question, question_owner, decoder_states)

    return run
```

```python
import functools
import math

import jax
import jax.numpy as jnp
from jax import lax
from jax.experimental import pallas as pl
from jax.experimental.pallas import tpu as pltpu
from jax.sharding import Mesh, PartitionSpec as P

HEAD_DIM = 64
EMPTY = -3e38
FIRST_EIGHTHS = 4
ROW_COPIES = 4
PROJECT_LIMIT = 24 * 1024 * 1024
VMEM_LIMIT = 22 * 1024 * 1024
SWAP = [(0, 1), (1, 0)]
CROSS = [(0, 3), (3, 0), (1, 2), (2, 1)]


def head_pick(tall, query_len):
    lanes = tall.shape[1]
    lane_head = lax.broadcasted_iota(jnp.int32, (query_len, lanes), 1) // HEAD_DIM
    picked = jnp.zeros((query_len, lanes), jnp.float32)
    for head in range(lanes // HEAD_DIM):
        picked = jnp.where(lane_head == head, tall[head * query_len : (head + 1) * query_len, :], picked)
    return picked


def join(block_ref, at, block, refs, core, same):
    came, swapped = block
    half = block_ref.shape[1] // 2
    if not swapped:
        block_ref[at, :half] = refs[came][pl.ds(pl.multiple_of(core * half, half), half), :]
        block_ref[at, half:] = refs[came][pl.ds(pl.multiple_of((1 - core) * half, half), half), :]
        return
    for pieces, where in ((came, (1 - same) * half), (swapped, same * half)):
        for operand, first, length in pieces:
            block_ref[at, pl.ds(pl.multiple_of(where + first, 16), length)] = refs[operand][:length]


def multiply(rows, block, keep_ref, send_ref, at, where):
    slot = at % send_ref.shape[0]
    product = lax.dot_general(rows, block, (((1,), (1,)), ((), ())), preferred_element_type=jnp.float32)
    half = product.shape[1] // 2
    keep_ref[at, where, :] = product[:, :half]
    send_ref[slot, where, :] = product[:, half:]


def join_kernel(flag_ref, *refs, sources, blocks):
    *refs, keep_ref, send_ref, block_ref = refs
    for at, block in enumerate(blocks):
        join(block_ref, at, block, refs[sources:], flag_ref[0], flag_ref[1])
    for source in range(sources):
        for at in range(len(blocks)):
            multiply(
                refs[source][...], block_ref[at], keep_ref, send_ref, source * len(blocks) + at, slice(None)
            )


def near_kernel(flag_ref, hidden_ref, partner_ref, *refs, blocks, sends):
    *refs, keep_ref, rows_ref, block_ref, semaphores = refs
    refs, send_refs = refs[: len(refs) - len(sends)], refs[len(refs) - len(sends) :]
    step = rows_ref.shape[0] // ROW_COPIES
    copies = []
    for part in range(ROW_COPIES):
        rows = pl.ds(part * step, step)
        copies.append(pltpu.make_async_copy(partner_ref.at[rows], rows_ref.at[rows], semaphores.at[part]))
        copies[-1].start()
    for source, source_ref in enumerate((hidden_ref, rows_ref)):
        for copy in copies if source else []:
            copy.wait()
        for at, block in enumerate(blocks):
            if not source:
                join(block_ref, at, block, refs, flag_ref[0], flag_ref[1])
            slot = source * len(blocks) + at
            multiply(source_ref[...], block_ref[at], keep_ref, send_refs[slot // 2], slot, slice(None))


def attend_kernel(place_ref, spot_ref, query_ref, *refs, pieces):
    *refs, own_ref, partner_ref, out_ref, key_ref = refs
    residuals = own_ref, partner_ref
    partner_queries = own_ref.shape[0]
    held = query_ref.shape[1]
    query_len = query_ref.shape[0] // out_ref.shape[0]
    block_len = key_ref.shape[1]
    heads = held // HEAD_DIM
    tall = heads * query_len
    members, packed_rows, lanes_packed = out_ref.shape
    extra = packed_rows - 8
    row = lax.broadcasted_iota(jnp.int32, out_ref.shape, 1)
    out_ref[...] = jnp.where((row == extra) | (row == extra + 1), EMPTY, 0.0)
    row_head = lax.broadcasted_iota(jnp.int32, (tall, held), 0) // query_len
    lane_head = lax.broadcasted_iota(jnp.int32, (tall, held), 1) // HEAD_DIM
    diagonal = row_head == lane_head
    square = lax.broadcasted_iota(jnp.int32, (tall, tall), 0) == lax.broadcasted_iota(jnp.int32, (tall, tall), 1)
    ext = lax.broadcasted_iota(jnp.int32, (8, tall), 0)
    blocks = key_ref.shape[0] // 2
    for source, kept, sent, spot in pieces:
        keep, other = (refs[summand].at[piece] for summand, piece in (kept, sent))
        residual = residuals[source]
        span = keep.shape[1]
        lanes, given = (pl.ds(pl.multiple_of(spot_ref[of, spot], 128), span) for of in (1, source))
        for block in range(blocks):
            rows = slice(block * block_len, (block + 1) * block_len)
            key_ref[source * blocks + block, :, lanes] = (
                residual[rows, given].astype(jnp.float32) + (keep[rows, :] + other[rows, :])
            ).astype(jnp.bfloat16)
    places, scores, tops = [], [], []
    for at in range(key_ref.shape[0]):
        place = place_ref[at]
        first = pl.multiple_of(place // 2 * query_len, query_len)
        own_query = query_ref[pl.ds(first, query_len), :]
        partner_query = partner_ref[pl.ds(partner_queries + first, query_len), :]
        query = jnp.where(place % 2 == 0, own_query, partner_query)
        query = jnp.concatenate([query] * heads, axis=0)
        query = jnp.where(diagonal, query, jnp.zeros_like(query))
        score = lax.dot_general(
            query, key_ref[at], (((1,), (1,)), ((), ())), preferred_element_type=jnp.float32
        )
        places.append(place)
        scores.append(score)
        tops.append(jnp.max(score, axis=1, keepdims=True))
    for at, place in enumerate(places):
        top = tops[at]
        for other_at, other_place in enumerate(places):
            if other_at != at:
                top = jnp.maximum(top, jnp.where(other_place == place, tops[other_at], EMPTY))
        weights = jnp.exp(scores[at] - top)
        total = jnp.sum(weights, axis=1, keepdims=True)
        blend = lax.dot_general(
            weights.astype(jnp.bfloat16), key_ref[at], (((1,), (0,)), ((), ())),
            preferred_element_type=jnp.float32,
        )
        top_row = jnp.sum(jnp.where(square, top, 0.0), axis=0, keepdims=True)
        total_row = jnp.sum(jnp.where(square, total, 0.0), axis=0, keepdims=True)
        blend = head_pick(blend, query_len)
        member, slot = place // 2, place % 2
        for block in range(held // lanes_packed):
            first = pl.multiple_of(slot * (extra // 2) + block * query_len, query_len)
            lanes = slice(block * lanes_packed, (block + 1) * lanes_packed)
            spot = pl.ds(first, query_len)
            out_ref[member, spot, :] = out_ref[member, spot, :] + blend[:, lanes]
        before = out_ref[member, extra:, :]
        out_ref[member, extra:, :] = jnp.where(
            ext == slot, top_row, jnp.where(ext == slot + 2, before + total_row, before)
        )


def merge_kernel(*refs):
    out_ref = refs[-1]
    parts = refs[:-1]
    query_len, held = out_ref.shape[1:]
    tall = held // HEAD_DIM * query_len
    square = lax.broadcasted_iota(jnp.int32, (tall, tall), 0) == lax.broadcasted_iota(jnp.int32, (tall, tall), 1)

    def over(start, step):
        for part in parts:
            start = lax.fori_loop(
                0, part.shape[0], functools.partial(step, part), start, unroll=part.shape[0] <= 8
            )
        return start

    packed_rows, lanes_packed = parts[0].shape[1:]
    extra = packed_rows - 8
    for slot in range(out_ref.shape[0]):
        top_row, total_row = (slice(extra + slot + at, extra + slot + at + 1) for at in (0, 2))

        def top_step(part, at, top):
            return jnp.maximum(top, part[at, top_row, :])

        def total_step(part, at, total):
            return total + jnp.exp(part[at, top_row, :] - top) * part[at, total_row, :]

        def blend_step(part, at, blend):
            share = jnp.exp(part[at, top_row, :] - top) / total
            column = jnp.sum(jnp.where(square, share, 0.0), axis=1, keepdims=True)
            spread = head_pick(jnp.broadcast_to(column, (tall, held)), query_len)
            first = slot * (extra // 2)
            rows = [
                part[at, first + block * query_len : first + (block + 1) * query_len, :]
                for block in range(held // lanes_packed)
            ]
            return blend + spread * jnp.concatenate(rows, axis=1)

        top = over(jnp.full((1, tall), EMPTY, jnp.float32), top_step)
        total = over(jnp.zeros((1, tall), jnp.float32), total_step)
        blend = over(jnp.zeros((query_len, held), jnp.float32), blend_step)
        out_ref[slot] = blend.astype(out_ref.dtype)


def assemble_kernel(flag_ref, mine_ref, core_ref, side_ref, both_ref, out_ref, *, order, span):
    side, core = flag_ref[0], flag_ref[1]
    mine, by_core, by_side, by_both = (ref[0] for ref in (mine_ref, core_ref, side_ref, both_ref))
    taken = {}
    for of_side in range(2):
        for of in range(2):
            near = jnp.where(core == of, mine, by_core)
            far = jnp.where(core == of, by_side, by_both)
            taken[of_side, of] = jnp.where(side == of_side, near, far)
    out_ref[0] = jnp.concatenate(
        [taken[of_side, of][:, first : first + span] for of_side, of, first in order], axis=1
    )


def in_vmem(count):
    return [pl.BlockSpec(memory_space=pltpu.VMEM)] * count


def in_smem(count):
    return [pl.BlockSpec(memory_space=pltpu.SMEM)] * count


def project(kernel, name, operands, placed, counts, rows, half, handed, scratch):
    return pl.pallas_call(
        kernel,
        out_shape=[jax.ShapeDtypeStruct((count, rows, half), jnp.float32) for count in counts] + handed,
        in_specs=placed,
        out_specs=in_vmem(len(counts) + len(handed)),
        scratch_shapes=scratch,
        compiler_params=pltpu.CompilerParams(vmem_limit_bytes=PROJECT_LIMIT),
        cost_estimate=pl.CostEstimate(flops=1, bytes_accessed=1, transcendentals=0),
        name=name,
    )(*operands)


def after(array, earlier):
    return lax.optimization_barrier((array, *earlier))[0] if earlier else array


def with_rows(array, units):
    flat = array.reshape(-1, array.shape[-1])
    spread = jnp.concatenate([flat[at : at + 8] for at in range(0, flat.shape[0], 8)], axis=1)
    return jnp.pad(spread, ((0, 0), (0, units - spread.shape[1])))


def from_rows(spreads, slot, shape):
    taken = []
    for spread in spreads:
        for at in range(shape[0] // 8):
            first = (slot * shape[0] // 8 + at) * shape[1]
            taken.append(spread[-8:, first : first + shape[1]])
    return jnp.concatenate(taken, axis=0)


def body(hidden_states, passage_states, down_weight, block_question, question_owner, decoder_states):
    blocks, block_len, units = hidden_states.shape
    width = passage_states.shape[2]
    query_len = decoder_states.shape[1]
    highs, lows, cores = lax.axis_size("high"), lax.axis_size("low"), lax.axis_size("mp")
    group, high, side, low, core = (lax.axis_index(name) for name in ("groups", "high", "side", "low", "mp"))
    shard = down_weight.shape[0]
    stride = lows * shard
    held = width // 2 // cores
    heads = held // HEAD_DIM
    members = highs * lows
    slot_total = question_owner.shape[0]
    rows = blocks * block_len
    lined = highs == 4 and lows == 1 and stride % (cores * 128) == 0
    span = stride // cores if lined else stride
    spans = held // span

    def features(array, of_side):
        if lined:
            starts = [(at * 2 + of_side) * stride + core * span for at in range(spans)]
        else:
            starts = [((core * spans + at) * 2 + of_side) * stride for at in range(spans)]
        taken = [lax.dynamic_slice_in_dim(array, start, span, axis=array.ndim - 1) for start in starts]
        return jnp.concatenate(taken, axis=-1)

    def shifted(array, shift):
        return lax.ppermute(array, "high", [(at, (at + shift) % highs) for at in range(highs)])

    hidden = hidden_states.reshape(rows, units)
    partner_hidden = lax.ppermute(hidden, "side", SWAP)
    queries = jnp.concatenate([features(decoder_states, side), features(decoder_states, 1 - side)], axis=0)[None]
    passages = passage_states.reshape(rows, width)
    leaving = features(passages, 1 - side)

    if lined:
        half = shard // 2
        lengths = [half * FIRST_EIGHTHS // 8, half - half * FIRST_EIGHTHS // 8]
        sent = [
            lax.dynamic_slice_in_dim(down_weight, group * half + first, length, axis=0)
            for first, length in zip((0, lengths[0]), lengths)
        ]
        sent[1] = jnp.concatenate([sent[1], with_rows(queries, units)], axis=0)
        below, above = [], []
        for at in range(2):
            below.append(shifted(after(sent[at], below[-1:]), 1))
            above.append(shifted(after(sent[at], above[-1:]), -1))
        opposite = [shifted(piece, 1) for piece in below]
        spreads = [piece[1][-8:] for piece in (sent, above, opposite, below)]
        *spreads, leaving, _ = lax.optimization_barrier(
            (*spreads, jnp.pad(leaving, ((0, highs * query_len), (0, 0))), partner_hidden)
        )
        own_queries, partner_queries = (from_rows(spreads, slot, (query_len, held)) for slot in range(2))
        leaving = lax.dynamic_update_slice(leaving, partner_queries, (rows, 0))
        first, second = lengths
        swapped = []
        for at, piece in enumerate([below[0], above[0], opposite[0], below[1], above[1], opposite[1]]):
            swapped.append(lax.ppermute(after(piece, swapped[max(at - 2, 0) : max(at - 1, 0)]), "groups", SWAP))
        flags = jnp.stack([core, (group == core).astype(core.dtype)])
        near_pieces = [down_weight] + above + below + swapped[:2] + swapped[3:5]
        far_pieces = opposite + swapped[2::3]
        starts = list(zip((0, first), lengths))
        near = [(0, None)]
        for came, other in ((1, 6), (3, 5)):
            near.append(tuple([(of + at * hop, *starts[at]) for at in range(2)] for of, hop in ((came, 1), (other, 2))))
        far = [tuple([(of + at, *starts[at]) for at in range(2)] for of in (0, 2))]
        spots = lax.rem(high + jnp.array([0, 1, 3, 2], jnp.int32), highs)
        spots = jnp.stack([(spots * 2 + side) * stride + core * span, spots * span])
        own_residual = passages

        sends = [2] * len(near)
        *away, kept, partner_rows = project(
            functools.partial(near_kernel, blocks=near, sends=sends), "project_near",
            [flags, hidden, partner_hidden] + near_pieces,
            in_smem(1) + in_vmem(1) + [pl.BlockSpec(memory_space=pl.ANY)] + in_vmem(len(near_pieces)),
            sends + [2 * len(near)], rows, half, [jax.ShapeDtypeStruct(hidden.shape, hidden.dtype)],
            [pltpu.VMEM((len(near), shard, units), down_weight.dtype), pltpu.SemaphoreType.DMA((ROW_COPIES,))],
        )
        far_kept, far_away = project(
            functools.partial(join_kernel, sources=2, blocks=far), "project_far",
            [flags, hidden, partner_rows] + far_pieces, in_smem(1) + in_vmem(2 + len(far_pieces)), [2, 2], rows, half,
            [], [pltpu.VMEM((1, shard, units), down_weight.dtype)],
        )
        summands = [kept, far_kept]
        summands += [lax.ppermute(piece, "mp", SWAP) for piece in (*away, far_away)]
        pieces = [(at // 3, (0, at), (2 + at // 2, at % 2), at % 3) for at in range(6)]
        pieces += [(source, (1, source), (5, source), 3) for source in range(2)]
        origin = high
    else:
        queries = lax.all_gather(queries, ("high", "low"), axis=0, tiled=True)
        own_queries, partner_queries = (queries[:, slot].reshape(-1, held) for slot in range(2))
        leaving = jnp.concatenate([leaving, partner_queries], axis=0)
        weight = lax.all_gather(down_weight, ("high", "low"), axis=0, tiled=True)
        weight = jnp.where(core == 0, weight, jnp.roll(weight, held, axis=0))
        spots = jnp.zeros((2, 1), jnp.int32)
        own_residual = features(passages, side)
        summands, pieces = [], []
        for source, flat in enumerate((hidden, partner_hidden)):
            kept, away = (
                lax.dot_general(flat, part, (((1,), (1,)), ((), ())), preferred_element_type=jnp.float32)[None]
                for part in (weight[:held], weight[held:])
            )
            summands += [kept, lax.ppermute(away, "mp", SWAP)]
            pieces.append((source, (2 * source, 0), (2 * source + 1, 0), 0))
        origin = 0

    questions = block_question[:, 0]
    question_ids = jnp.arange(slot_total, dtype=jnp.int32)
    owners = jnp.sum(jnp.where(questions[:, None] == question_ids[None, :], question_owner[None, :], 0), axis=1)
    owner_high, owner_side, owner_low = owners // (2 * lows), (owners // lows) % 2, owners % lows
    owner_high = lax.rem(owner_high - origin + highs, highs)
    owner_place = (owner_high * lows + owner_low) * 2 + (owner_side != side)
    own_at = ((high * 2 + side) * lows + low) * blocks
    partner_at = ((high * 2 + 1 - side) * lows + low) * blocks
    places = jnp.concatenate(
        [lax.dynamic_slice_in_dim(owner_place, at, blocks) for at in (own_at, partner_at)]
    )

    partner = lax.ppermute(leaving, "side", SWAP)
    packed = (members, 2 * held // 128 * query_len + 8, 128)
    operands = summands + [own_residual, partner]
    partials = pl.pallas_call(
        functools.partial(attend_kernel, pieces=pieces),
        out_shape=jax.ShapeDtypeStruct(packed, jnp.float32),
        in_specs=in_smem(2) + in_vmem(1 + len(operands)),
        out_specs=pl.BlockSpec(memory_space=pltpu.VMEM),
        scratch_shapes=[pltpu.VMEM((2 * blocks, block_len, held), jnp.bfloat16)],
        compiler_params=pltpu.CompilerParams(vmem_limit_bytes=VMEM_LIMIT),
        name="attend",
    )(places, spots, own_queries, *operands)
    if lined:
        received = [partials[0:1]] + [shifted(partials[ahead : ahead + 1], ahead) for ahead in range(1, highs)]
    else:
        received = [lax.all_to_all(partials, ("high", "low"), split_axis=0, concat_axis=0, tiled=True)]
    merged = pl.pallas_call(
        merge_kernel,
        out_shape=jax.ShapeDtypeStruct((2, query_len, held), decoder_states.dtype),
        in_specs=in_vmem(len(received)),
        out_specs=pl.BlockSpec(memory_space=pltpu.VMEM),
        compiler_params=pltpu.CompilerParams(vmem_limit_bytes=VMEM_LIMIT),
        name="merge",
    )(*received)

    mine, away = merged[0:1], merged[1:2]
    by_core = lax.ppermute(mine, "mp", SWAP)
    by_side = lax.ppermute(away, "side", SWAP)
    by_both = lax.ppermute(away, ("side", "mp"), CROSS)
    if lined:
        order = [(at, of_side, of) for at in range(spans) for of_side in range(2) for of in range(cores)]
    else:
        order = [(at, of_side, of) for of in range(cores) for at in range(spans) for of_side in range(2)]
    flags = jnp.stack([side, core])
    order = [(of_side, of, at * span) for at, of_side, of in order]
    return pl.pallas_call(
        functools.partial(assemble_kernel, order=order, span=span),
        out_shape=jax.ShapeDtypeStruct((1, query_len, width), decoder_states.dtype),
        in_specs=in_smem(1) + in_vmem(4),
        out_specs=pl.BlockSpec(memory_space=pltpu.VMEM),
        compiler_params=pltpu.CompilerParams(vmem_limit_bytes=VMEM_LIMIT),
        name="assemble",
    )(flags, mine, by_core, by_side, by_both)


def solution(mesh):
    groups, dp, cores = mesh.shape["groups"], mesh.shape["dp"], mesh.shape["mp"]

    def run(hidden_states, passage_states, down_weight, block_question, question_owner, decoder_states):
        lows = max(1, HEAD_DIM * dp // down_weight.shape[0])
        fine = Mesh(
            mesh.devices.reshape(groups, dp // (2 * lows), 2, lows, cores),
            ("groups", "high", "side", "low", "mp"),
        )
        split = ("groups", "high", "side", "low")
        placed = (
            P(split, None, "mp"),
            P(split, None, None),
            P(("high", "side", "low"), "mp"),
            P("groups", None),
            P("groups"),
            P(split, None, None),
        )
        return jax.shard_map(
            body, mesh=fine, in_specs=placed, out_specs=P(split, None, None), check_vma=False
        )(hidden_states, passage_states, down_weight, block_question, question_owner, decoder_states)

    return run
```

```python
import functools
import math

import jax
import jax.numpy as jnp
from jax import lax
from jax.experimental import pallas as pl
from jax.experimental.pallas import tpu as pltpu
from jax.sharding import Mesh, PartitionSpec as P

HEAD_DIM = 64
EMPTY = -3e38
FIRST_EIGHTHS = 4
VMEM_LIMIT = 22 * 1024 * 1024
SWAP = [(0, 1), (1, 0)]
CROSS = [(0, 3), (3, 0), (1, 2), (2, 1)]


def head_pick(tall, query_len):
    lanes = tall.shape[1]
    lane_head = lax.broadcasted_iota(jnp.int32, (query_len, lanes), 1) // HEAD_DIM
    picked = jnp.zeros((query_len, lanes), jnp.float32)
    for head in range(lanes // HEAD_DIM):
        picked = jnp.where(lane_head == head, tall[head * query_len : (head + 1) * query_len, :], picked)
    return picked


def project_kernel(flag_ref, *refs, jobs, sends):
    keep_ref, *send_refs = refs[-1 - len(sends) :]
    slots = [(ref, at) for ref in send_refs for at in range(ref.shape[0])]
    core, same = flag_ref[0], flag_ref[1]
    half = keep_ref.shape[2]
    for at, (rows_of, blocks_of) in enumerate(jobs):
        if len(blocks_of) == 1:
            whole = refs[blocks_of[0][0]]
            keep = whole[pl.ds(pl.multiple_of(core * half, half), half), :]
            send = whole[pl.ds(pl.multiple_of((1 - core) * half, half), half), :]
        else:
            parts = [refs[block][:length] for block, length in blocks_of]
            first, second = (
                jnp.concatenate(part, axis=0) for part in (parts[: len(parts) // 2], parts[len(parts) // 2 :])
            )
            keep = jnp.where(same == 1, first, second)
            send = jnp.where(same == 1, second, first)
        product = lax.dot_general(
            refs[rows_of][...],
            jnp.concatenate([keep, send], axis=0),
            (((1,), (1,)), ((), ())),
            preferred_element_type=jnp.float32,
        )
        keep_ref[at] = product[:, :half]
        send_ref, slot = slots[at]
        send_ref[slot] = product[:, half:]


def attend_kernel(place_ref, spot_ref, query_ref, *refs, pieces):
    *refs, own_ref, partner_ref, out_ref, key_ref = refs
    residuals = own_ref, partner_ref
    partner_queries = own_ref.shape[0]
    query_len, held = query_ref.shape[1:]
    block_len = key_ref.shape[1]
    heads = held // HEAD_DIM
    tall = heads * query_len
    members, packed_rows, lanes_packed = out_ref.shape
    extra = packed_rows - 8
    row = lax.broadcasted_iota(jnp.int32, out_ref.shape, 1)
    out_ref[...] = jnp.where((row == extra) | (row == extra + 1), EMPTY, 0.0)
    row_head = lax.broadcasted_iota(jnp.int32, (tall, held), 0) // query_len
    lane_head = lax.broadcasted_iota(jnp.int32, (tall, held), 1) // HEAD_DIM
    diagonal = row_head == lane_head
    square = lax.broadcasted_iota(jnp.int32, (tall, tall), 0) == lax.broadcasted_iota(jnp.int32, (tall, tall), 1)
    ext = lax.broadcasted_iota(jnp.int32, (8, tall), 0)
    blocks = key_ref.shape[0] // 2
    for source, kept, sent, spot in pieces:
        keep, other = (refs[summand].at[piece] for summand, piece in (kept, sent))
        residual = residuals[source]
        span = keep.shape[1]
        lanes, given = (pl.ds(pl.multiple_of(spot_ref[of, spot], 128), span) for of in (1, source))
        for block in range(blocks):
            rows = slice(block * block_len, (block + 1) * block_len)
            key_ref[source * blocks + block, :, lanes] = (
                residual[rows, given].astype(jnp.float32) + (keep[rows, :] + other[rows, :])
            ).astype(jnp.bfloat16)
    places, scores, tops = [], [], []
    for at in range(key_ref.shape[0]):
        place = place_ref[at]
        first = pl.multiple_of(partner_queries + place // 2 * query_len, query_len)
        query = jnp.where(place % 2 == 0, query_ref[place // 2], partner_ref[pl.ds(first, query_len), :])
        query = jnp.concatenate([query] * heads, axis=0)
        query = jnp.where(diagonal, query, jnp.zeros_like(query))
        score = lax.dot_general(
            query, key_ref[at], (((1,), (1,)), ((), ())), preferred_element_type=jnp.float32
        )
        places.append(place)
        scores.append(score)
        tops.append(jnp.max(score, axis=1, keepdims=True))
    for at, place in enumerate(places):
        top = tops[at]
        for other_at, other_place in enumerate(places):
            if other_at != at:
                top = jnp.maximum(top, jnp.where(other_place == place, tops[other_at], EMPTY))
        weights = jnp.exp(scores[at] - top)
        total = jnp.sum(weights, axis=1, keepdims=True)
        blend = lax.dot_general(
            weights.astype(jnp.bfloat16), key_ref[at], (((1,), (0,)), ((), ())),
            preferred_element_type=jnp.float32,
        )
        top_row = jnp.sum(jnp.where(square, top, 0.0), axis=0, keepdims=True)
        total_row = jnp.sum(jnp.where(square, total, 0.0), axis=0, keepdims=True)
        blend = head_pick(blend, query_len)
        member, slot = place // 2, place % 2
        for block in range(held // lanes_packed):
            first = pl.multiple_of(slot * (extra // 2) + block * query_len, query_len)
            lanes = slice(block * lanes_packed, (block + 1) * lanes_packed)
            spot = pl.ds(first, query_len)
            out_ref[member, spot, :] = out_ref[member, spot, :] + blend[:, lanes]
        before = out_ref[member, extra:, :]
        out_ref[member, extra:, :] = jnp.where(
            ext == slot, top_row, jnp.where(ext == slot + 2, before + total_row, before)
        )


def merge_kernel(*refs):
    out_ref = refs[-1]
    parts = refs[:-1]
    query_len, held = out_ref.shape[1:]
    tall = held // HEAD_DIM * query_len
    square = lax.broadcasted_iota(jnp.int32, (tall, tall), 0) == lax.broadcasted_iota(jnp.int32, (tall, tall), 1)

    def over(start, step):
        for part in parts:
            start = lax.fori_loop(
                0, part.shape[0], functools.partial(step, part), start, unroll=part.shape[0] <= 8
            )
        return start

    packed_rows, lanes_packed = parts[0].shape[1:]
    extra = packed_rows - 8
    for slot in range(out_ref.shape[0]):
        top_row, total_row = (slice(extra + slot + at, extra + slot + at + 1) for at in (0, 2))

        def top_step(part, at, top):
            return jnp.maximum(top, part[at, top_row, :])

        def total_step(part, at, total):
            return total + jnp.exp(part[at, top_row, :] - top) * part[at, total_row, :]

        def blend_step(part, at, blend):
            share = jnp.exp(part[at, top_row, :] - top) / total
            column = jnp.sum(jnp.where(square, share, 0.0), axis=1, keepdims=True)
            spread = head_pick(jnp.broadcast_to(column, (tall, held)), query_len)
            first = slot * (extra // 2)
            rows = [
                part[at, first + block * query_len : first + (block + 1) * query_len, :]
                for block in range(held // lanes_packed)
            ]
            return blend + spread * jnp.concatenate(rows, axis=1)

        top = over(jnp.full((1, tall), EMPTY, jnp.float32), top_step)
        total = over(jnp.zeros((1, tall), jnp.float32), total_step)
        blend = over(jnp.zeros((query_len, held), jnp.float32), blend_step)
        out_ref[slot] = blend.astype(out_ref.dtype)


def assemble_kernel(flag_ref, mine_ref, core_ref, side_ref, both_ref, out_ref, *, order, span):
    side, core = flag_ref[0], flag_ref[1]
    mine, by_core, by_side, by_both = (ref[0] for ref in (mine_ref, core_ref, side_ref, both_ref))
    taken = {}
    for of_side in range(2):
        for of in range(2):
            near = jnp.where(core == of, mine, by_core)
            far = jnp.where(core == of, by_side, by_both)
            taken[of_side, of] = jnp.where(side == of_side, near, far)
    out_ref[0] = jnp.concatenate(
        [taken[of_side, of][:, first : first + span] for of_side, of, first in order], axis=1
    )


def in_vmem(count):
    return [pl.BlockSpec(memory_space=pltpu.VMEM)] * count


def in_smem(count):
    return [pl.BlockSpec(memory_space=pltpu.SMEM)] * count


def project(flags, operands, jobs, sends, half, flops, name):
    rows, units = operands[0].shape
    shapes = [jax.ShapeDtypeStruct((count, rows, half), jnp.float32) for count in [len(jobs)] + sends]
    return pl.pallas_call(
        functools.partial(project_kernel, jobs=jobs, sends=sends),
        out_shape=shapes,
        in_specs=in_smem(1) + in_vmem(len(operands)),
        out_specs=in_vmem(len(shapes)),
        compiler_params=pltpu.CompilerParams(vmem_limit_bytes=VMEM_LIMIT),
        cost_estimate=pl.CostEstimate(flops=flops, bytes_accessed=1, transcendentals=0),
        name=name,
    )(flags, *operands)


def after(array, earlier):
    return lax.optimization_barrier((array, *earlier))[0] if earlier else array


def with_rows(array, units):
    flat = array.reshape(-1, array.shape[-1])
    spread = jnp.concatenate([flat[at : at + 8] for at in range(0, flat.shape[0], 8)], axis=1)
    return jnp.pad(spread, ((0, 0), (0, units - spread.shape[1])))


def from_rows(spread, shape):
    pieces = [spread[:, at : at + shape[-1]] for at in range(0, math.prod(shape) // 8, shape[-1])]
    return jnp.concatenate(pieces, axis=0).reshape(shape)


def body(hidden_states, passage_states, down_weight, block_question, question_owner, decoder_states):
    blocks, block_len, units = hidden_states.shape
    width = passage_states.shape[2]
    query_len = decoder_states.shape[1]
    highs, lows, cores = lax.axis_size("high"), lax.axis_size("low"), lax.axis_size("mp")
    group, high, side, low, core = (lax.axis_index(name) for name in ("groups", "high", "side", "low", "mp"))
    shard = down_weight.shape[0]
    stride = lows * shard
    held = width // 2 // cores
    heads = held // HEAD_DIM
    members = highs * lows
    slot_total = question_owner.shape[0]
    rows = blocks * block_len
    lined = highs == 4 and lows == 1 and stride % (cores * 128) == 0
    span = stride // cores if lined else stride
    spans = held // span

    def features(array, of_side):
        if lined:
            starts = [(at * 2 + of_side) * stride + core * span for at in range(spans)]
        else:
            starts = [((core * spans + at) * 2 + of_side) * stride for at in range(spans)]
        taken = [lax.dynamic_slice_in_dim(array, start, span, axis=array.ndim - 1) for start in starts]
        return jnp.concatenate(taken, axis=-1)

    def shifted(array, shift):
        return lax.ppermute(array, "high", [(at, (at + shift) % highs) for at in range(highs)])

    hidden = hidden_states.reshape(rows, units)
    partner_hidden = lax.ppermute(hidden, "side", SWAP)
    queries = jnp.concatenate([features(decoder_states, side), features(decoder_states, 1 - side)], axis=0)[None]
    passages = passage_states.reshape(rows, width)
    leaving = features(passages, 1 - side)

    if lined:
        half = shard // 2
        lengths = [half * FIRST_EIGHTHS // 8, half - half * FIRST_EIGHTHS // 8]
        sent = [
            lax.dynamic_slice_in_dim(down_weight, group * half + first, length, axis=0)
            for first, length in zip((0, lengths[0]), lengths)
        ]
        sent[1] = jnp.concatenate([sent[1], with_rows(queries, units)], axis=0)
        below, above = [], []
        for at in range(2):
            below.append(shifted(after(sent[at], below[-1:]), 1))
            above.append(shifted(after(sent[at], above[-1:] or below[:1]), -1))
        opposite = [jnp.concatenate([shifted(after(below[0], below[1:]), 1), shifted(below[1], 1)], axis=0)]
        around = [from_rows(piece[-1][-8:], queries.shape) for piece in (above, opposite, below)]
        queries = jnp.concatenate([queries] + around, axis=0)
        swapped = []
        for at, piece in enumerate([below[0], above[0], below[1], above[1]] + opposite):
            swapped.append(lax.ppermute(after(piece, swapped[max(at - 2, 0) : max(at - 1, 0)]), "groups", SWAP))
        weights = [down_weight] + above + swapped[1:4:2] + below + swapped[0:4:2] + opposite + swapped[4:]
        flags = jnp.stack([core, (group == core).astype(core.dtype)])
        blocks_of = [[(2, shard)], list(zip(range(3, 7), 2 * lengths)), list(zip(range(7, 11), 2 * lengths))]
        spots = lax.rem(high + jnp.array([0, 1, 3, 2], jnp.int32), highs)
        spots = jnp.stack([(spots * 2 + side) * stride + core * span, spots * span])
        own_residual = passages

        kept, *away = project(
            flags,
            [hidden, partner_hidden] + weights[:9],
            [(source, blocks_of[at]) for source in range(2) for at in range(3)],
            [2, 2, 2],
            half,
            24 * rows * half * units,
            "project_near",
        )
        flags, kept, *away = lax.optimization_barrier((flags, kept, *away))
        late_kept, *late_away = project(
            flags,
            [hidden, partner_hidden] + weights[9:],
            [(source, [(2, half), (3, half)]) for source in range(2)],
            [2],
            half,
            1,
            "project_far",
        )
        others = [lax.ppermute(piece, "mp", SWAP) for piece in away + late_away]
        summands = [kept, late_kept] + others
        pieces = [(at // 3, (0, at), (2 + at // 2, at % 2), at % 3) for at in range(6)]
        pieces += [(source, (1, source), (5, source), 3) for source in range(2)]
        origin = high
    else:
        queries = lax.all_gather(queries, ("high", "low"), axis=0, tiled=True)
        weight = lax.all_gather(down_weight, ("high", "low"), axis=0, tiled=True)
        weight = jnp.where(core == 0, weight, jnp.roll(weight, held, axis=0))
        spots = jnp.zeros((2, 1), jnp.int32)
        own_residual = features(passages, side)
        summands, pieces = [], []
        for source, flat in enumerate((hidden, partner_hidden)):
            kept, away = (
                lax.dot_general(flat, part, (((1,), (1,)), ((), ())), preferred_element_type=jnp.float32)[None]
                for part in (weight[:held], weight[held:])
            )
            summands += [kept, lax.ppermute(away, "mp", SWAP)]
            pieces.append((source, (2 * source, 0), (2 * source + 1, 0), 0))
        origin = 0

    questions = block_question[:, 0]
    question_ids = jnp.arange(slot_total, dtype=jnp.int32)
    owners = jnp.sum(jnp.where(questions[:, None] == question_ids[None, :], question_owner[None, :], 0), axis=1)
    owner_high, owner_side, owner_low = owners // (2 * lows), (owners // lows) % 2, owners % lows
    owner_high = lax.rem(owner_high - origin + highs, highs)
    owner_place = (owner_high * lows + owner_low) * 2 + (owner_side != side)
    own_at = ((high * 2 + side) * lows + low) * blocks
    partner_at = ((high * 2 + 1 - side) * lows + low) * blocks
    places = jnp.concatenate(
        [lax.dynamic_slice_in_dim(owner_place, at, blocks) for at in (own_at, partner_at)]
    )

    leaving = jnp.concatenate([leaving, queries[:, 1].reshape(-1, held)], axis=0)
    partner = lax.ppermute(leaving, "side", SWAP)
    packed = (members, 2 * held // 128 * query_len + 8, 128)
    operands = summands + [own_residual, partner]
    partials = pl.pallas_call(
        functools.partial(attend_kernel, pieces=pieces),
        out_shape=jax.ShapeDtypeStruct(packed, jnp.float32),
        in_specs=in_smem(2) + in_vmem(1 + len(operands)),
        out_specs=pl.BlockSpec(memory_space=pltpu.VMEM),
        scratch_shapes=[pltpu.VMEM((2 * blocks, block_len, held), jnp.bfloat16)],
        compiler_params=pltpu.CompilerParams(vmem_limit_bytes=VMEM_LIMIT),
        name="attend",
    )(places, spots, queries[:, 0], *operands)
    if lined:
        received = [partials[0:1]] + [shifted(partials[ahead : ahead + 1], ahead) for ahead in range(1, highs)]
    else:
        received = [lax.all_to_all(partials, ("high", "low"), split_axis=0, concat_axis=0, tiled=True)]
    merged = pl.pallas_call(
        merge_kernel,
        out_shape=jax.ShapeDtypeStruct((2, query_len, held), decoder_states.dtype),
        in_specs=in_vmem(len(received)),
        out_specs=pl.BlockSpec(memory_space=pltpu.VMEM),
        compiler_params=pltpu.CompilerParams(vmem_limit_bytes=VMEM_LIMIT),
        name="merge",
    )(*received)

    mine, away = merged[0:1], merged[1:2]
    by_core = lax.ppermute(mine, "mp", SWAP)
    by_side = lax.ppermute(away, "side", SWAP)
    by_both = lax.ppermute(away, ("side", "mp"), CROSS)
    if lined:
        order = [(at, of_side, of) for at in range(spans) for of_side in range(2) for of in range(cores)]
    else:
        order = [(at, of_side, of) for of in range(cores) for at in range(spans) for of_side in range(2)]
    flags = jnp.stack([side, core])
    order = [(of_side, of, at * span) for at, of_side, of in order]
    return pl.pallas_call(
        functools.partial(assemble_kernel, order=order, span=span),
        out_shape=jax.ShapeDtypeStruct((1, query_len, width), decoder_states.dtype),
        in_specs=in_smem(1) + in_vmem(4),
        out_specs=pl.BlockSpec(memory_space=pltpu.VMEM),
        compiler_params=pltpu.CompilerParams(vmem_limit_bytes=VMEM_LIMIT),
        name="assemble",
    )(flags, mine, by_core, by_side, by_both)


def solution(mesh):
    groups, dp, cores = mesh.shape["groups"], mesh.shape["dp"], mesh.shape["mp"]

    def run(hidden_states, passage_states, down_weight, block_question, question_owner, decoder_states):
        lows = max(1, HEAD_DIM * dp // down_weight.shape[0])
        fine = Mesh(
            mesh.devices.reshape(groups, dp // (2 * lows), 2, lows, cores),
            ("groups", "high", "side", "low", "mp"),
        )
        split = ("groups", "high", "side", "low")
        placed = (
            P(split, None, "mp"),
            P(split, None, None),
            P(("high", "side", "low"), "mp"),
            P("groups", None),
            P("groups"),
            P(split, None, None),
        )
        return jax.shard_map(
            body, mesh=fine, in_specs=placed, out_specs=P(split, None, None), check_vma=False
        )(hidden_states, passage_states, down_weight, block_question, question_owner, decoder_states)

    return run
```

```python
import functools
import math

import jax
import jax.numpy as jnp
from jax import lax
from jax.experimental import pallas as pl
from jax.experimental.pallas import tpu as pltpu
from jax.sharding import Mesh, PartitionSpec as P

HEAD_DIM = 64
EMPTY = -3e38
FIRST_EIGHTHS = 5
VMEM_LIMIT = 22 * 1024 * 1024
SWAP = [(0, 1), (1, 0)]
CROSS = [(0, 3), (3, 0), (1, 2), (2, 1)]


def head_pick(tall, query_len):
    lanes = tall.shape[1]
    lane_head = lax.broadcasted_iota(jnp.int32, (query_len, lanes), 1) // HEAD_DIM
    picked = jnp.zeros((query_len, lanes), jnp.float32)
    for head in range(lanes // HEAD_DIM):
        picked = jnp.where(lane_head == head, tall[head * query_len : (head + 1) * query_len, :], picked)
    return picked


def project_kernel(flag_ref, *refs, jobs, sends):
    keep_ref, *send_refs = refs[-1 - len(sends) :]
    slots = [(ref, at) for ref in send_refs for at in range(ref.shape[0])]
    core, same = flag_ref[0], flag_ref[1]
    half = keep_ref.shape[2]
    for at, (rows_of, blocks_of) in enumerate(jobs):
        if len(blocks_of) == 1:
            whole = refs[blocks_of[0][0]]
            keep = whole[pl.ds(pl.multiple_of(core * half, half), half), :]
            send = whole[pl.ds(pl.multiple_of((1 - core) * half, half), half), :]
        else:
            parts = [refs[block][:length] for block, length in blocks_of]
            first, second = (
                jnp.concatenate(part, axis=0) for part in (parts[: len(parts) // 2], parts[len(parts) // 2 :])
            )
            keep = jnp.where(same == 1, first, second)
            send = jnp.where(same == 1, second, first)
        product = lax.dot_general(
            refs[rows_of][...],
            jnp.concatenate([keep, send], axis=0),
            (((1,), (1,)), ((), ())),
            preferred_element_type=jnp.float32,
        )
        keep_ref[at] = product[:, :half]
        send_ref, slot = slots[at]
        send_ref[slot] = product[:, half:]


def attend_kernel(place_ref, spot_ref, query_ref, *refs, pieces):
    *refs, own_ref, partner_ref, out_ref, key_ref = refs
    residuals = own_ref, partner_ref
    partner_queries = own_ref.shape[0]
    query_len, held = query_ref.shape[1:]
    block_len = key_ref.shape[1]
    heads = held // HEAD_DIM
    tall = heads * query_len
    members, packed_rows, lanes_packed = out_ref.shape
    extra = packed_rows - 8
    row = lax.broadcasted_iota(jnp.int32, out_ref.shape, 1)
    out_ref[...] = jnp.where((row == extra) | (row == extra + 1), EMPTY, 0.0)
    row_head = lax.broadcasted_iota(jnp.int32, (tall, held), 0) // query_len
    lane_head = lax.broadcasted_iota(jnp.int32, (tall, held), 1) // HEAD_DIM
    diagonal = row_head == lane_head
    square = lax.broadcasted_iota(jnp.int32, (tall, tall), 0) == lax.broadcasted_iota(jnp.int32, (tall, tall), 1)
    ext = lax.broadcasted_iota(jnp.int32, (8, tall), 0)
    blocks = key_ref.shape[0] // 2
    for source, kept, sent, spot in pieces:
        keep, other = (refs[summand].at[piece] for summand, piece in (kept, sent))
        residual = residuals[source]
        span = keep.shape[1]
        lanes, given = (pl.ds(pl.multiple_of(spot_ref[of, spot], 128), span) for of in (1, source))
        for block in range(blocks):
            rows = slice(block * block_len, (block + 1) * block_len)
            key_ref[source * blocks + block, :, lanes] = (
                residual[rows, given].astype(jnp.float32) + (keep[rows, :] + other[rows, :])
            ).astype(jnp.bfloat16)
    places, scores, tops = [], [], []
    for at in range(key_ref.shape[0]):
        place = place_ref[at]
        first = pl.multiple_of(partner_queries + place // 2 * query_len, query_len)
        query = jnp.where(place % 2 == 0, query_ref[place // 2], partner_ref[pl.ds(first, query_len), :])
        query = jnp.concatenate([query] * heads, axis=0)
        query = jnp.where(diagonal, query, jnp.zeros_like(query))
        score = lax.dot_general(
            query, key_ref[at], (((1,), (1,)), ((), ())), preferred_element_type=jnp.float32
        )
        places.append(place)
        scores.append(score)
        tops.append(jnp.max(score, axis=1, keepdims=True))
    for at, place in enumerate(places):
        top = tops[at]
        for other_at, other_place in enumerate(places):
            if other_at != at:
                top = jnp.maximum(top, jnp.where(other_place == place, tops[other_at], EMPTY))
        weights = jnp.exp(scores[at] - top)
        total = jnp.sum(weights, axis=1, keepdims=True)
        blend = lax.dot_general(
            weights.astype(jnp.bfloat16), key_ref[at], (((1,), (0,)), ((), ())),
            preferred_element_type=jnp.float32,
        )
        top_row = jnp.sum(jnp.where(square, top, 0.0), axis=0, keepdims=True)
        total_row = jnp.sum(jnp.where(square, total, 0.0), axis=0, keepdims=True)
        blend = head_pick(blend, query_len)
        member, slot = place // 2, place % 2
        for block in range(held // lanes_packed):
            first = pl.multiple_of(slot * (extra // 2) + block * query_len, query_len)
            lanes = slice(block * lanes_packed, (block + 1) * lanes_packed)
            spot = pl.ds(first, query_len)
            out_ref[member, spot, :] = out_ref[member, spot, :] + blend[:, lanes]
        before = out_ref[member, extra:, :]
        out_ref[member, extra:, :] = jnp.where(
            ext == slot, top_row, jnp.where(ext == slot + 2, before + total_row, before)
        )


def merge_kernel(*refs):
    out_ref = refs[-1]
    parts = refs[:-1]
    query_len, held = out_ref.shape[1:]
    tall = held // HEAD_DIM * query_len
    square = lax.broadcasted_iota(jnp.int32, (tall, tall), 0) == lax.broadcasted_iota(jnp.int32, (tall, tall), 1)

    def over(start, step):
        for part in parts:
            start = lax.fori_loop(
                0, part.shape[0], functools.partial(step, part), start, unroll=part.shape[0] <= 8
            )
        return start

    packed_rows, lanes_packed = parts[0].shape[1:]
    extra = packed_rows - 8
    for slot in range(out_ref.shape[0]):
        top_row, total_row = (slice(extra + slot + at, extra + slot + at + 1) for at in (0, 2))

        def top_step(part, at, top):
            return jnp.maximum(top, part[at, top_row, :])

        def total_step(part, at, total):
            return total + jnp.exp(part[at, top_row, :] - top) * part[at, total_row, :]

        def blend_step(part, at, blend):
            share = jnp.exp(part[at, top_row, :] - top) / total
            column = jnp.sum(jnp.where(square, share, 0.0), axis=1, keepdims=True)
            spread = head_pick(jnp.broadcast_to(column, (tall, held)), query_len)
            first = slot * (extra // 2)
            rows = [
                part[at, first + block * query_len : first + (block + 1) * query_len, :]
                for block in range(held // lanes_packed)
            ]
            return blend + spread * jnp.concatenate(rows, axis=1)

        top = over(jnp.full((1, tall), EMPTY, jnp.float32), top_step)
        total = over(jnp.zeros((1, tall), jnp.float32), total_step)
        blend = over(jnp.zeros((query_len, held), jnp.float32), blend_step)
        out_ref[slot] = blend.astype(out_ref.dtype)


def assemble_kernel(flag_ref, mine_ref, core_ref, side_ref, both_ref, out_ref, *, order, span):
    side, core = flag_ref[0], flag_ref[1]
    mine, by_core, by_side, by_both = (ref[0] for ref in (mine_ref, core_ref, side_ref, both_ref))
    taken = {}
    for of_side in range(2):
        for of in range(2):
            near = jnp.where(core == of, mine, by_core)
            far = jnp.where(core == of, by_side, by_both)
            taken[of_side, of] = jnp.where(side == of_side, near, far)
    out_ref[0] = jnp.concatenate(
        [taken[of_side, of][:, first : first + span] for of_side, of, first in order], axis=1
    )


def in_vmem(count):
    return [pl.BlockSpec(memory_space=pltpu.VMEM)] * count


def in_smem(count):
    return [pl.BlockSpec(memory_space=pltpu.SMEM)] * count


def project(flags, operands, jobs, sends, half, flops, name):
    rows, units = operands[0].shape
    shapes = [jax.ShapeDtypeStruct((count, rows, half), jnp.float32) for count in [len(jobs)] + sends]
    return pl.pallas_call(
        functools.partial(project_kernel, jobs=jobs, sends=sends),
        out_shape=shapes,
        in_specs=in_smem(1) + in_vmem(len(operands)),
        out_specs=in_vmem(len(shapes)),
        compiler_params=pltpu.CompilerParams(vmem_limit_bytes=VMEM_LIMIT),
        cost_estimate=pl.CostEstimate(flops=flops, bytes_accessed=1, transcendentals=0),
        name=name,
    )(flags, *operands)


def after(array, earlier):
    return lax.optimization_barrier((array, *earlier))[0] if earlier else array


def with_rows(array, units):
    flat = array.reshape(-1, array.shape[-1])
    spread = jnp.concatenate([flat[at : at + 8] for at in range(0, flat.shape[0], 8)], axis=1)
    return jnp.pad(spread, ((0, 0), (0, units - spread.shape[1])))


def from_rows(spread, shape):
    pieces = [spread[:, at : at + shape[-1]] for at in range(0, math.prod(shape) // 8, shape[-1])]
    return jnp.concatenate(pieces, axis=0).reshape(shape)


def body(hidden_states, passage_states, down_weight, block_question, question_owner, decoder_states):
    blocks, block_len, units = hidden_states.shape
    width = passage_states.shape[2]
    query_len = decoder_states.shape[1]
    highs, lows, cores = lax.axis_size("high"), lax.axis_size("low"), lax.axis_size("mp")
    group, high, side, low, core = (lax.axis_index(name) for name in ("groups", "high", "side", "low", "mp"))
    shard = down_weight.shape[0]
    stride = lows * shard
    held = width // 2 // cores
    heads = held // HEAD_DIM
    members = highs * lows
    slot_total = question_owner.shape[0]
    rows = blocks * block_len
    lined = highs == 4 and lows == 1 and stride % (cores * 128) == 0
    span = stride // cores if lined else stride
    spans = held // span

    def features(array, of_side):
        if lined:
            starts = [(at * 2 + of_side) * stride + core * span for at in range(spans)]
        else:
            starts = [((core * spans + at) * 2 + of_side) * stride for at in range(spans)]
        taken = [lax.dynamic_slice_in_dim(array, start, span, axis=array.ndim - 1) for start in starts]
        return jnp.concatenate(taken, axis=-1)

    def shifted(array, shift):
        return lax.ppermute(array, "high", [(at, (at + shift) % highs) for at in range(highs)])

    hidden = hidden_states.reshape(rows, units)
    partner_hidden = lax.ppermute(hidden, "side", SWAP)
    queries = jnp.concatenate([features(decoder_states, side), features(decoder_states, 1 - side)], axis=0)[None]
    passages = passage_states.reshape(rows, width)
    leaving = features(passages, 1 - side)

    if lined:
        half = shard // 2
        lengths = [half * FIRST_EIGHTHS // 8, half - half * FIRST_EIGHTHS // 8]
        sent = [
            lax.dynamic_slice_in_dim(down_weight, group * half + first, length, axis=0)
            for first, length in zip((0, lengths[0]), lengths)
        ]
        sent[1] = jnp.concatenate([sent[1], with_rows(queries, units)], axis=0)
        below, above = [], []
        for at in range(2):
            below.append(shifted(after(sent[at], below[-1:]), 1))
            above.append(shifted(after(sent[at], above[-1:] or below[:1]), -1))
        opposite = [shifted(after(below[0], below[1:]), 1), shifted(below[1], 1)]
        around = [from_rows(piece[-1][-8:], queries.shape) for piece in (above, opposite, below)]
        opposite = [jnp.concatenate([opposite[0], opposite[1][: lengths[1]]], axis=0)]
        queries = jnp.concatenate([queries] + around, axis=0)
        swapped = []
        for at, piece in enumerate([below[0], above[0], below[1], above[1]] + opposite):
            swapped.append(lax.ppermute(after(piece, swapped[2:] if at == 4 else swapped[max(at - 2, 0) : max(at - 1, 0)]), "groups", SWAP))
        weights = [down_weight] + above + swapped[1:4:2] + below + swapped[0:4:2] + opposite + swapped[4:]
        flags = jnp.stack([core, (group == core).astype(core.dtype)])
        blocks_of = [[(2, shard)], list(zip(range(3, 7), 2 * lengths)), list(zip(range(7, 11), 2 * lengths))]
        spots = lax.rem(high + jnp.array([0, 1, 3, 2], jnp.int32), highs)
        spots = jnp.stack([(spots * 2 + side) * stride + core * span, spots * span])
        own_residual = passages

        kept, *away = project(
            flags,
            [hidden, partner_hidden] + weights[:9],
            [(source, blocks_of[at]) for source in range(2) for at in range(3)],
            [2, 2, 2],
            half,
            24 * rows * half * units,
            "project_near",
        )
        flags, kept, *away = lax.optimization_barrier((flags, kept, *away))
        late_kept, *late_away = project(
            flags,
            [hidden, partner_hidden] + weights[9:],
            [(source, [(2, half), (3, half)]) for source in range(2)],
            [2],
            half,
            1,
            "project_far",
        )
        others = [lax.ppermute(piece, "mp", SWAP) for piece in away + late_away]
        summands = [kept, late_kept] + others
        pieces = [(at // 3, (0, at), (2 + at // 2, at % 2), at % 3) for at in range(6)]
        pieces += [(source, (1, source), (5, source), 3) for source in range(2)]
        origin = high
    else:
        queries = lax.all_gather(queries, ("high", "low"), axis=0, tiled=True)
        weight = lax.all_gather(down_weight, ("high", "low"), axis=0, tiled=True)
        weight = jnp.where(core == 0, weight, jnp.roll(weight, held, axis=0))
        spots = jnp.zeros((2, 1), jnp.int32)
        own_residual = features(passages, side)
        summands, pieces = [], []
        for source, flat in enumerate((hidden, partner_hidden)):
            kept, away = (
                lax.dot_general(flat, part, (((1,), (1,)), ((), ())), preferred_element_type=jnp.float32)[None]
                for part in (weight[:held], weight[held:])
            )
            summands += [kept, lax.ppermute(away, "mp", SWAP)]
            pieces.append((source, (2 * source, 0), (2 * source + 1, 0), 0))
        origin = 0

    questions = block_question[:, 0]
    question_ids = jnp.arange(slot_total, dtype=jnp.int32)
    owners = jnp.sum(jnp.where(questions[:, None] == question_ids[None, :], question_owner[None, :], 0), axis=1)
    owner_high, owner_side, owner_low = owners // (2 * lows), (owners // lows) % 2, owners % lows
    owner_high = lax.rem(owner_high - origin + highs, highs)
    owner_place = (owner_high * lows + owner_low) * 2 + (owner_side != side)
    own_at = ((high * 2 + side) * lows + low) * blocks
    partner_at = ((high * 2 + 1 - side) * lows + low) * blocks
    places = jnp.concatenate(
        [lax.dynamic_slice_in_dim(owner_place, at, blocks) for at in (own_at, partner_at)]
    )

    leaving = jnp.concatenate([leaving, queries[:, 1].reshape(-1, held)], axis=0)
    partner = lax.ppermute(leaving, "side", SWAP)
    packed = (members, 2 * held // 128 * query_len + 8, 128)
    operands = summands + [own_residual, partner]
    partials = pl.pallas_call(
        functools.partial(attend_kernel, pieces=pieces),
        out_shape=jax.ShapeDtypeStruct(packed, jnp.float32),
        in_specs=in_smem(2) + in_vmem(1 + len(operands)),
        out_specs=pl.BlockSpec(memory_space=pltpu.VMEM),
        scratch_shapes=[pltpu.VMEM((2 * blocks, block_len, held), jnp.bfloat16)],
        compiler_params=pltpu.CompilerParams(vmem_limit_bytes=VMEM_LIMIT),
        name="attend",
    )(places, spots, queries[:, 0], *operands)
    if lined:
        received = [partials[0:1]] + [shifted(partials[ahead : ahead + 1], ahead) for ahead in range(1, highs)]
    else:
        received = [lax.all_to_all(partials, ("high", "low"), split_axis=0, concat_axis=0, tiled=True)]
    merged = pl.pallas_call(
        merge_kernel,
        out_shape=jax.ShapeDtypeStruct((2, query_len, held), decoder_states.dtype),
        in_specs=in_vmem(len(received)),
        out_specs=pl.BlockSpec(memory_space=pltpu.VMEM),
        compiler_params=pltpu.CompilerParams(vmem_limit_bytes=VMEM_LIMIT),
        name="merge",
    )(*received)

    mine, away = merged[0:1], merged[1:2]
    by_core = lax.ppermute(mine, "mp", SWAP)
    by_side = lax.ppermute(away, "side", SWAP)
    by_both = lax.ppermute(away, ("side", "mp"), CROSS)
    if lined:
        order = [(at, of_side, of) for at in range(spans) for of_side in range(2) for of in range(cores)]
    else:
        order = [(at, of_side, of) for of in range(cores) for at in range(spans) for of_side in range(2)]
    flags = jnp.stack([side, core])
    order = [(of_side, of, at * span) for at, of_side, of in order]
    return pl.pallas_call(
        functools.partial(assemble_kernel, order=order, span=span),
        out_shape=jax.ShapeDtypeStruct((1, query_len, width), decoder_states.dtype),
        in_specs=in_smem(1) + in_vmem(4),
        out_specs=pl.BlockSpec(memory_space=pltpu.VMEM),
        compiler_params=pltpu.CompilerParams(vmem_limit_bytes=VMEM_LIMIT),
        name="assemble",
    )(flags, mine, by_core, by_side, by_both)


def solution(mesh):
    groups, dp, cores = mesh.shape["groups"], mesh.shape["dp"], mesh.shape["mp"]

    def run(hidden_states, passage_states, down_weight, block_question, question_owner, decoder_states):
        lows = max(1, HEAD_DIM * dp // down_weight.shape[0])
        fine = Mesh(
            mesh.devices.reshape(groups, dp // (2 * lows), 2, lows, cores),
            ("groups", "high", "side", "low", "mp"),
        )
        split = ("groups", "high", "side", "low")
        placed = (
            P(split, None, "mp"),
            P(split, None, None),
            P(("high", "side", "low"), "mp"),
            P("groups", None),
            P("groups"),
            P(split, None, None),
        )
        return jax.shard_map(
            body, mesh=fine, in_specs=placed, out_specs=P(split, None, None), check_vma=False
        )(hidden_states, passage_states, down_weight, block_question, question_owner, decoder_states)

    return run
```

```python
import functools
import math

import jax
import jax.numpy as jnp
from jax import lax
from jax.experimental import pallas as pl
from jax.experimental.pallas import tpu as pltpu
from jax.sharding import Mesh, PartitionSpec as P

HEAD_DIM = 64
EMPTY = -3e38
FIRST_EIGHTHS = 4
ROW_COPIES = 4
VMEM_LIMIT = 22 * 1024 * 1024
SWAP = [(0, 1), (1, 0)]
CROSS = [(0, 3), (3, 0), (1, 2), (2, 1)]


def head_pick(tall, query_len):
    lanes = tall.shape[1]
    lane_head = lax.broadcasted_iota(jnp.int32, (query_len, lanes), 1) // HEAD_DIM
    picked = jnp.zeros((query_len, lanes), jnp.float32)
    for head in range(lanes // HEAD_DIM):
        picked = jnp.where(lane_head == head, tall[head * query_len : (head + 1) * query_len, :], picked)
    return picked


def project_kernel(flag_ref, *refs, jobs, sends, copied):
    copies = []
    if copied:
        *refs, rows_ref, semaphores = refs
        step = rows_ref.shape[0] // ROW_COPIES
        for part in range(ROW_COPIES):
            rows = pl.ds(part * step, step)
            copies.append(
                pltpu.make_async_copy(refs[copied].at[rows], rows_ref.at[rows], semaphores.at[part])
            )
            copies[-1].start()
        refs[copied] = rows_ref
    keep_ref, *send_refs = refs[-1 - len(sends) :]
    slots = [(ref, at) for ref in send_refs for at in range(ref.shape[0])]
    core, same = flag_ref[0], flag_ref[1]
    half = keep_ref.shape[2]
    for at, (rows_of, blocks_of) in enumerate(jobs):
        if len(blocks_of) == 1:
            whole = refs[blocks_of[0][0]]
            keep = whole[pl.ds(pl.multiple_of(core * half, half), half), :]
            send = whole[pl.ds(pl.multiple_of((1 - core) * half, half), half), :]
        else:
            parts = [refs[block][:length] for block, length in blocks_of]
            first, second = (
                jnp.concatenate(part, axis=0) for part in (parts[: len(parts) // 2], parts[len(parts) // 2 :])
            )
            keep = jnp.where(same == 1, first, second)
            send = jnp.where(same == 1, second, first)
        if copied and rows_of == copied:
            for copy in copies:
                copy.wait()
            copies = []
        product = lax.dot_general(
            refs[rows_of][...],
            jnp.concatenate([keep, send], axis=0),
            (((1,), (1,)), ((), ())),
            preferred_element_type=jnp.float32,
        )
        keep_ref[at] = product[:, :half]
        send_ref, slot = slots[at]
        send_ref[slot] = product[:, half:]


def attend_kernel(place_ref, spot_ref, query_ref, *refs, pieces):
    *refs, own_ref, partner_ref, out_ref, key_ref = refs
    residuals = own_ref, partner_ref
    partner_queries = own_ref.shape[0]
    query_len, held = query_ref.shape[1:]
    block_len = key_ref.shape[1]
    heads = held // HEAD_DIM
    tall = heads * query_len
    members, packed_rows, lanes_packed = out_ref.shape
    extra = packed_rows - 8
    row = lax.broadcasted_iota(jnp.int32, out_ref.shape, 1)
    out_ref[...] = jnp.where((row == extra) | (row == extra + 1), EMPTY, 0.0)
    row_head = lax.broadcasted_iota(jnp.int32, (tall, held), 0) // query_len
    lane_head = lax.broadcasted_iota(jnp.int32, (tall, held), 1) // HEAD_DIM
    diagonal = row_head == lane_head
    square = lax.broadcasted_iota(jnp.int32, (tall, tall), 0) == lax.broadcasted_iota(jnp.int32, (tall, tall), 1)
    ext = lax.broadcasted_iota(jnp.int32, (8, tall), 0)
    blocks = key_ref.shape[0] // 2
    for source, kept, sent, spot in pieces:
        keep, other = (refs[summand].at[piece] for summand, piece in (kept, sent))
        residual = residuals[source]
        span = keep.shape[1]
        lanes, given = (pl.ds(pl.multiple_of(spot_ref[of, spot], 128), span) for of in (1, source))
        for block in range(blocks):
            rows = slice(block * block_len, (block + 1) * block_len)
            key_ref[source * blocks + block, :, lanes] = (
                residual[rows, given].astype(jnp.float32) + (keep[rows, :] + other[rows, :])
            ).astype(jnp.bfloat16)
    places, scores, tops = [], [], []
    for at in range(key_ref.shape[0]):
        place = place_ref[at]
        first = pl.multiple_of(partner_queries + place // 2 * query_len, query_len)
        query = jnp.where(place % 2 == 0, query_ref[place // 2], partner_ref[pl.ds(first, query_len), :])
        query = jnp.concatenate([query] * heads, axis=0)
        query = jnp.where(diagonal, query, jnp.zeros_like(query))
        score = lax.dot_general(
            query, key_ref[at], (((1,), (1,)), ((), ())), preferred_element_type=jnp.float32
        )
        places.append(place)
        scores.append(score)
        tops.append(jnp.max(score, axis=1, keepdims=True))
    for at, place in enumerate(places):
        top = tops[at]
        for other_at, other_place in enumerate(places):
            if other_at != at:
                top = jnp.maximum(top, jnp.where(other_place == place, tops[other_at], EMPTY))
        weights = jnp.exp(scores[at] - top)
        total = jnp.sum(weights, axis=1, keepdims=True)
        blend = lax.dot_general(
            weights.astype(jnp.bfloat16), key_ref[at], (((1,), (0,)), ((), ())),
            preferred_element_type=jnp.float32,
        )
        top_row = jnp.sum(jnp.where(square, top, 0.0), axis=0, keepdims=True)
        total_row = jnp.sum(jnp.where(square, total, 0.0), axis=0, keepdims=True)
        blend = head_pick(blend, query_len)
        member, slot = place // 2, place % 2
        for block in range(held // lanes_packed):
            first = pl.multiple_of(slot * (extra // 2) + block * query_len, query_len)
            lanes = slice(block * lanes_packed, (block + 1) * lanes_packed)
            spot = pl.ds(first, query_len)
            out_ref[member, spot, :] = out_ref[member, spot, :] + blend[:, lanes]
        before = out_ref[member, extra:, :]
        out_ref[member, extra:, :] = jnp.where(
            ext == slot, top_row, jnp.where(ext == slot + 2, before + total_row, before)
        )


def merge_kernel(*refs):
    out_ref = refs[-1]
    parts = refs[:-1]
    query_len, held = out_ref.shape[1:]
    tall = held // HEAD_DIM * query_len
    square = lax.broadcasted_iota(jnp.int32, (tall, tall), 0) == lax.broadcasted_iota(jnp.int32, (tall, tall), 1)

    def over(start, step):
        for part in parts:
            start = lax.fori_loop(
                0, part.shape[0], functools.partial(step, part), start, unroll=part.shape[0] <= 8
            )
        return start

    packed_rows, lanes_packed = parts[0].shape[1:]
    extra = packed_rows - 8
    for slot in range(out_ref.shape[0]):
        top_row, total_row = (slice(extra + slot + at, extra + slot + at + 1) for at in (0, 2))

        def top_step(part, at, top):
            return jnp.maximum(top, part[at, top_row, :])

        def total_step(part, at, total):
            return total + jnp.exp(part[at, top_row, :] - top) * part[at, total_row, :]

        def blend_step(part, at, blend):
            share = jnp.exp(part[at, top_row, :] - top) / total
            column = jnp.sum(jnp.where(square, share, 0.0), axis=1, keepdims=True)
            spread = head_pick(jnp.broadcast_to(column, (tall, held)), query_len)
            first = slot * (extra // 2)
            rows = [
                part[at, first + block * query_len : first + (block + 1) * query_len, :]
                for block in range(held // lanes_packed)
            ]
            return blend + spread * jnp.concatenate(rows, axis=1)

        top = over(jnp.full((1, tall), EMPTY, jnp.float32), top_step)
        total = over(jnp.zeros((1, tall), jnp.float32), total_step)
        blend = over(jnp.zeros((query_len, held), jnp.float32), blend_step)
        out_ref[slot] = blend.astype(out_ref.dtype)


def assemble_kernel(flag_ref, mine_ref, core_ref, side_ref, both_ref, out_ref, *, order, span):
    side, core = flag_ref[0], flag_ref[1]
    mine, by_core, by_side, by_both = (ref[0] for ref in (mine_ref, core_ref, side_ref, both_ref))
    taken = {}
    for of_side in range(2):
        for of in range(2):
            near = jnp.where(core == of, mine, by_core)
            far = jnp.where(core == of, by_side, by_both)
            taken[of_side, of] = jnp.where(side == of_side, near, far)
    out_ref[0] = jnp.concatenate(
        [taken[of_side, of][:, first : first + span] for of_side, of, first in order], axis=1
    )


def in_vmem(count):
    return [pl.BlockSpec(memory_space=pltpu.VMEM)] * count


def in_smem(count):
    return [pl.BlockSpec(memory_space=pltpu.SMEM)] * count


def project(flags, operands, jobs, sends, half, flops, copied, name):
    rows, units = operands[0].shape
    shapes = [jax.ShapeDtypeStruct((count, rows, half), jnp.float32) for count in [len(jobs)] + sends]
    placed = in_vmem(len(operands))
    if copied:
        placed[copied] = pl.BlockSpec(memory_space=pl.ANY)
    rows_held = [pltpu.VMEM((rows, units), operands[0].dtype), pltpu.SemaphoreType.DMA((ROW_COPIES,))]
    return pl.pallas_call(
        functools.partial(project_kernel, jobs=jobs, sends=sends, copied=copied),
        out_shape=shapes,
        in_specs=in_smem(1) + placed,
        out_specs=in_vmem(len(shapes)),
        scratch_shapes=rows_held if copied else [],
        compiler_params=pltpu.CompilerParams(vmem_limit_bytes=VMEM_LIMIT),
        cost_estimate=pl.CostEstimate(flops=flops, bytes_accessed=1, transcendentals=0),
        name=name,
    )(flags, *operands)


def after(array, earlier):
    return lax.optimization_barrier((array, *earlier))[0] if earlier else array


def with_rows(array, units):
    flat = array.reshape(-1, array.shape[-1])
    spread = jnp.concatenate([flat[at : at + 8] for at in range(0, flat.shape[0], 8)], axis=1)
    return jnp.pad(spread, ((0, 0), (0, units - spread.shape[1])))


def from_rows(spread, shape):
    pieces = [spread[:, at : at + shape[-1]] for at in range(0, math.prod(shape) // 8, shape[-1])]
    return jnp.concatenate(pieces, axis=0).reshape(shape)


def body(hidden_states, passage_states, down_weight, block_question, question_owner, decoder_states):
    blocks, block_len, units = hidden_states.shape
    width = passage_states.shape[2]
    query_len = decoder_states.shape[1]
    highs, lows, cores = lax.axis_size("high"), lax.axis_size("low"), lax.axis_size("mp")
    group, high, side, low, core = (lax.axis_index(name) for name in ("groups", "high", "side", "low", "mp"))
    shard = down_weight.shape[0]
    stride = lows * shard
    held = width // 2 // cores
    heads = held // HEAD_DIM
    members = highs * lows
    slot_total = question_owner.shape[0]
    rows = blocks * block_len
    lined = highs == 4 and lows == 1 and stride % (cores * 128) == 0
    span = stride // cores if lined else stride
    spans = held // span

    def features(array, of_side):
        if lined:
            starts = [(at * 2 + of_side) * stride + core * span for at in range(spans)]
        else:
            starts = [((core * spans + at) * 2 + of_side) * stride for at in range(spans)]
        taken = [lax.dynamic_slice_in_dim(array, start, span, axis=array.ndim - 1) for start in starts]
        return jnp.concatenate(taken, axis=-1)

    def shifted(array, shift):
        return lax.ppermute(array, "high", [(at, (at + shift) % highs) for at in range(highs)])

    hidden = hidden_states.reshape(rows, units)
    partner_hidden = lax.ppermute(hidden, "side", SWAP)
    queries = jnp.concatenate([features(decoder_states, side), features(decoder_states, 1 - side)], axis=0)[None]
    passages = passage_states.reshape(rows, width)
    leaving = features(passages, 1 - side)

    if lined:
        half = shard // 2
        lengths = [half * FIRST_EIGHTHS // 8, half - half * FIRST_EIGHTHS // 8]
        sent = [
            lax.dynamic_slice_in_dim(down_weight, group * half + first, length, axis=0)
            for first, length in zip((0, lengths[0]), lengths)
        ]
        sent[1] = jnp.concatenate([sent[1], with_rows(queries, units)], axis=0)
        below, above = [], []
        for at in range(2):
            below.append(shifted(after(sent[at], below[-1:]), 1))
            above.append(shifted(after(sent[at], above[-1:] or below[:1]), -1))
        opposite = [shifted(after(below[0], below[1:]), 1), shifted(below[1], 1)]
        around = [from_rows(piece[-1][-8:], queries.shape) for piece in (above, opposite, below)]
        opposite = [jnp.concatenate([opposite[0], opposite[1][: lengths[1]]], axis=0)]
        queries = jnp.concatenate([queries] + around, axis=0)
        swapped = []
        for at, piece in enumerate([below[0], above[0], below[1], above[1]] + opposite):
            swapped.append(lax.ppermute(after(piece, swapped[max(at - 2, 0) : max(at - 1, 0)]), "groups", SWAP))
        weights = [down_weight] + above + swapped[1:4:2] + below + swapped[0:4:2] + opposite + swapped[4:]
        flags = jnp.stack([core, (group == core).astype(core.dtype)])
        blocks_of = [[(2, shard)], list(zip(range(3, 7), 2 * lengths)), list(zip(range(7, 11), 2 * lengths))]
        spots = lax.rem(high + jnp.array([0, 1, 3, 2], jnp.int32), highs)
        spots = jnp.stack([(spots * 2 + side) * stride + core * span, spots * span])
        own_residual = passages

        kept, *away = project(
            flags,
            [hidden, partner_hidden] + weights[:9],
            [(source, blocks_of[at]) for source in range(2) for at in range(3)],
            [2, 2, 2],
            half,
            24 * rows * half * units,
            0,
            "project_near",
        )
        flags, kept, *away = lax.optimization_barrier((flags, kept, *away))
        late_kept, *late_away = project(
            flags,
            [hidden, partner_hidden] + weights[9:],
            [(source, [(2, half), (3, half)]) for source in range(2)],
            [2],
            half,
            1,
            1,
            "project_far",
        )
        others = [lax.ppermute(piece, "mp", SWAP) for piece in away + late_away]
        summands = [kept, late_kept] + others
        pieces = [(at // 3, (0, at), (2 + at // 2, at % 2), at % 3) for at in range(6)]
        pieces += [(source, (1, source), (5, source), 3) for source in range(2)]
        origin = high
    else:
        queries = lax.all_gather(queries, ("high", "low"), axis=0, tiled=True)
        weight = lax.all_gather(down_weight, ("high", "low"), axis=0, tiled=True)
        weight = jnp.where(core == 0, weight, jnp.roll(weight, held, axis=0))
        spots = jnp.zeros((2, 1), jnp.int32)
        own_residual = features(passages, side)
        summands, pieces = [], []
        for source, flat in enumerate((hidden, partner_hidden)):
            kept, away = (
                lax.dot_general(flat, part, (((1,), (1,)), ((), ())), preferred_element_type=jnp.float32)[None]
                for part in (weight[:held], weight[held:])
            )
            summands += [kept, lax.ppermute(away, "mp", SWAP)]
            pieces.append((source, (2 * source, 0), (2 * source + 1, 0), 0))
        origin = 0

    questions = block_question[:, 0]
    question_ids = jnp.arange(slot_total, dtype=jnp.int32)
    owners = jnp.sum(jnp.where(questions[:, None] == question_ids[None, :], question_owner[None, :], 0), axis=1)
    owner_high, owner_side, owner_low = owners // (2 * lows), (owners // lows) % 2, owners % lows
    owner_high = lax.rem(owner_high - origin + highs, highs)
    owner_place = (owner_high * lows + owner_low) * 2 + (owner_side != side)
    own_at = ((high * 2 + side) * lows + low) * blocks
    partner_at = ((high * 2 + 1 - side) * lows + low) * blocks
    places = jnp.concatenate(
        [lax.dynamic_slice_in_dim(owner_place, at, blocks) for at in (own_at, partner_at)]
    )

    leaving = jnp.concatenate([leaving, queries[:, 1].reshape(-1, held)], axis=0)
    partner = lax.ppermute(leaving, "side", SWAP)
    packed = (members, 2 * held // 128 * query_len + 8, 128)
    operands = summands + [own_residual, partner]
    partials = pl.pallas_call(
        functools.partial(attend_kernel, pieces=pieces),
        out_shape=jax.ShapeDtypeStruct(packed, jnp.float32),
        in_specs=in_smem(2) + in_vmem(1 + len(operands)),
        out_specs=pl.BlockSpec(memory_space=pltpu.VMEM),
        scratch_shapes=[pltpu.VMEM((2 * blocks, block_len, held), jnp.bfloat16)],
        compiler_params=pltpu.CompilerParams(vmem_limit_bytes=VMEM_LIMIT),
        name="attend",
    )(places, spots, queries[:, 0], *operands)
    if lined:
        received = [partials[0:1]] + [shifted(partials[ahead : ahead + 1], ahead) for ahead in range(1, highs)]
    else:
        received = [lax.all_to_all(partials, ("high", "low"), split_axis=0, concat_axis=0, tiled=True)]
    merged = pl.pallas_call(
        merge_kernel,
        out_shape=jax.ShapeDtypeStruct((2, query_len, held), decoder_states.dtype),
        in_specs=in_vmem(len(received)),
        out_specs=pl.BlockSpec(memory_space=pltpu.VMEM),
        compiler_params=pltpu.CompilerParams(vmem_limit_bytes=VMEM_LIMIT),
        name="merge",
    )(*received)

    mine, away = merged[0:1], merged[1:2]
    by_core = lax.ppermute(mine, "mp", SWAP)
    by_side = lax.ppermute(away, "side", SWAP)
    by_both = lax.ppermute(away, ("side", "mp"), CROSS)
    if lined:
        order = [(at, of_side, of) for at in range(spans) for of_side in range(2) for of in range(cores)]
    else:
        order = [(at, of_side, of) for of in range(cores) for at in range(spans) for of_side in range(2)]
    flags = jnp.stack([side, core])
    order = [(of_side, of, at * span) for at, of_side, of in order]
    return pl.pallas_call(
        functools.partial(assemble_kernel, order=order, span=span),
        out_shape=jax.ShapeDtypeStruct((1, query_len, width), decoder_states.dtype),
        in_specs=in_smem(1) + in_vmem(4),
        out_specs=pl.BlockSpec(memory_space=pltpu.VMEM),
        compiler_params=pltpu.CompilerParams(vmem_limit_bytes=VMEM_LIMIT),
        name="assemble",
    )(flags, mine, by_core, by_side, by_both)


def solution(mesh):
    groups, dp, cores = mesh.shape["groups"], mesh.shape["dp"], mesh.shape["mp"]

    def run(hidden_states, passage_states, down_weight, block_question, question_owner, decoder_states):
        lows = max(1, HEAD_DIM * dp // down_weight.shape[0])
        fine = Mesh(
            mesh.devices.reshape(groups, dp // (2 * lows), 2, lows, cores),
            ("groups", "high", "side", "low", "mp"),
        )
        split = ("groups", "high", "side", "low")
        placed = (
            P(split, None, "mp"),
            P(split, None, None),
            P(("high", "side", "low"), "mp"),
            P("groups", None),
            P("groups"),
            P(split, None, None),
        )
        return jax.shard_map(
            body, mesh=fine, in_specs=placed, out_specs=P(split, None, None), check_vma=False
        )(hidden_states, passage_states, down_weight, block_question, question_owner, decoder_states)

    return run
```

```python
import functools
import math

import jax
import jax.numpy as jnp
from jax import lax
from jax.experimental import pallas as pl
from jax.experimental.pallas import tpu as pltpu
from jax.sharding import Mesh, PartitionSpec as P

HEAD_DIM = 64
EMPTY = -3e38
FIRST_EIGHTHS = 4
VMEM_LIMIT = 22 * 1024 * 1024
SWAP = [(0, 1), (1, 0)]
CROSS = [(0, 3), (3, 0), (1, 2), (2, 1)]


def head_pick(tall, query_len):
    lanes = tall.shape[1]
    lane_head = lax.broadcasted_iota(jnp.int32, (query_len, lanes), 1) // HEAD_DIM
    picked = jnp.zeros((query_len, lanes), jnp.float32)
    for head in range(lanes // HEAD_DIM):
        picked = jnp.where(lane_head == head, tall[head * query_len : (head + 1) * query_len, :], picked)
    return picked


def project_kernel(flag_ref, *refs, jobs, sends):
    keep_ref, *send_refs = refs[-1 - len(sends) :]
    slots = [(ref, at) for ref in send_refs for at in range(ref.shape[0])]
    core, same = flag_ref[0], flag_ref[1]
    half = keep_ref.shape[2]
    for at, (rows_of, blocks_of) in enumerate(jobs):
        if len(blocks_of) == 1:
            whole = refs[blocks_of[0][0]]
            keep = whole[pl.ds(pl.multiple_of(core * half, half), half), :]
            send = whole[pl.ds(pl.multiple_of((1 - core) * half, half), half), :]
        else:
            parts = [refs[block][:length] for block, length in blocks_of]
            first, second = (
                jnp.concatenate(part, axis=0) for part in (parts[: len(parts) // 2], parts[len(parts) // 2 :])
            )
            keep = jnp.where(same == 1, first, second)
            send = jnp.where(same == 1, second, first)
        product = lax.dot_general(
            refs[rows_of][...],
            jnp.concatenate([keep, send], axis=0),
            (((1,), (1,)), ((), ())),
            preferred_element_type=jnp.float32,
        )
        keep_ref[at] = product[:, :half]
        send_ref, slot = slots[at]
        send_ref[slot] = product[:, half:]


def attend_kernel(place_ref, spot_ref, query_ref, *refs, pieces):
    *refs, own_ref, partner_ref, out_ref, key_ref = refs
    residuals = own_ref, partner_ref
    partner_queries = own_ref.shape[0]
    query_len, held = query_ref.shape[1:]
    block_len = key_ref.shape[1]
    heads = held // HEAD_DIM
    tall = heads * query_len
    members, packed_rows, lanes_packed = out_ref.shape
    extra = packed_rows - 8
    row = lax.broadcasted_iota(jnp.int32, out_ref.shape, 1)
    out_ref[...] = jnp.where((row == extra) | (row == extra + 1), EMPTY, 0.0)
    row_head = lax.broadcasted_iota(jnp.int32, (tall, held), 0) // query_len
    lane_head = lax.broadcasted_iota(jnp.int32, (tall, held), 1) // HEAD_DIM
    diagonal = row_head == lane_head
    square = lax.broadcasted_iota(jnp.int32, (tall, tall), 0) == lax.broadcasted_iota(jnp.int32, (tall, tall), 1)
    ext = lax.broadcasted_iota(jnp.int32, (8, tall), 0)
    blocks = key_ref.shape[0] // 2
    for source, kept, sent, spot in pieces:
        keep, other = (refs[summand].at[piece] for summand, piece in (kept, sent))
        residual = residuals[source]
        span = keep.shape[1]
        lanes, given = (pl.ds(pl.multiple_of(spot_ref[of, spot], 128), span) for of in (1, source))
        for block in range(blocks):
            rows = slice(block * block_len, (block + 1) * block_len)
            key_ref[source * blocks + block, :, lanes] = (
                residual[rows, given].astype(jnp.float32) + (keep[rows, :] + other[rows, :])
            ).astype(jnp.bfloat16)
    places, scores, tops = [], [], []
    for at in range(key_ref.shape[0]):
        place = place_ref[at]
        first = pl.multiple_of(partner_queries + place // 2 * query_len, query_len)
        query = jnp.where(place % 2 == 0, query_ref[place // 2], partner_ref[pl.ds(first, query_len), :])
        query = jnp.concatenate([query] * heads, axis=0)
        query = jnp.where(diagonal, query, jnp.zeros_like(query))
        score = lax.dot_general(
            query, key_ref[at], (((1,), (1,)), ((), ())), preferred_element_type=jnp.float32
        )
        places.append(place)
        scores.append(score)
        tops.append(jnp.max(score, axis=1, keepdims=True))
    for at, place in enumerate(places):
        top = tops[at]
        for other_at, other_place in enumerate(places):
            if other_at != at:
                top = jnp.maximum(top, jnp.where(other_place == place, tops[other_at], EMPTY))
        weights = jnp.exp(scores[at] - top)
        total = jnp.sum(weights, axis=1, keepdims=True)
        blend = lax.dot_general(
            weights.astype(jnp.bfloat16), key_ref[at], (((1,), (0,)), ((), ())),
            preferred_element_type=jnp.float32,
        )
        top_row = jnp.sum(jnp.where(square, top, 0.0), axis=0, keepdims=True)
        total_row = jnp.sum(jnp.where(square, total, 0.0), axis=0, keepdims=True)
        blend = head_pick(blend, query_len)
        member, slot = place // 2, place % 2
        for block in range(held // lanes_packed):
            first = pl.multiple_of(slot * (extra // 2) + block * query_len, query_len)
            lanes = slice(block * lanes_packed, (block + 1) * lanes_packed)
            spot = pl.ds(first, query_len)
            out_ref[member, spot, :] = out_ref[member, spot, :] + blend[:, lanes]
        before = out_ref[member, extra:, :]
        out_ref[member, extra:, :] = jnp.where(
            ext == slot, top_row, jnp.where(ext == slot + 2, before + total_row, before)
        )


def merge_kernel(*refs):
    out_ref = refs[-1]
    parts = refs[:-1]
    query_len, held = out_ref.shape[1:]
    tall = held // HEAD_DIM * query_len
    square = lax.broadcasted_iota(jnp.int32, (tall, tall), 0) == lax.broadcasted_iota(jnp.int32, (tall, tall), 1)

    def over(start, step):
        for part in parts:
            start = lax.fori_loop(
                0, part.shape[0], functools.partial(step, part), start, unroll=part.shape[0] <= 8
            )
        return start

    packed_rows, lanes_packed = parts[0].shape[1:]
    extra = packed_rows - 8
    for slot in range(out_ref.shape[0]):
        top_row, total_row = (slice(extra + slot + at, extra + slot + at + 1) for at in (0, 2))

        def top_step(part, at, top):
            return jnp.maximum(top, part[at, top_row, :])

        def total_step(part, at, total):
            return total + jnp.exp(part[at, top_row, :] - top) * part[at, total_row, :]

        def blend_step(part, at, blend):
            share = jnp.exp(part[at, top_row, :] - top) / total
            column = jnp.sum(jnp.where(square, share, 0.0), axis=1, keepdims=True)
            spread = head_pick(jnp.broadcast_to(column, (tall, held)), query_len)
            first = slot * (extra // 2)
            rows = [
                part[at, first + block * query_len : first + (block + 1) * query_len, :]
                for block in range(held // lanes_packed)
            ]
            return blend + spread * jnp.concatenate(rows, axis=1)

        top = over(jnp.full((1, tall), EMPTY, jnp.float32), top_step)
        total = over(jnp.zeros((1, tall), jnp.float32), total_step)
        blend = over(jnp.zeros((query_len, held), jnp.float32), blend_step)
        out_ref[slot] = blend.astype(out_ref.dtype)


def assemble_kernel(flag_ref, mine_ref, core_ref, side_ref, both_ref, out_ref, *, order, span):
    side, core = flag_ref[0], flag_ref[1]
    mine, by_core, by_side, by_both = (ref[0] for ref in (mine_ref, core_ref, side_ref, both_ref))
    taken = {}
    for of_side in range(2):
        for of in range(2):
            near = jnp.where(core == of, mine, by_core)
            far = jnp.where(core == of, by_side, by_both)
            taken[of_side, of] = jnp.where(side == of_side, near, far)
    out_ref[0] = jnp.concatenate(
        [taken[of_side, of][:, first : first + span] for of_side, of, first in order], axis=1
    )


def in_vmem(count):
    return [pl.BlockSpec(memory_space=pltpu.VMEM)] * count


def in_smem(count):
    return [pl.BlockSpec(memory_space=pltpu.SMEM)] * count


def project(flags, operands, jobs, sends, half, flops, name):
    rows, units = operands[0].shape
    shapes = [jax.ShapeDtypeStruct((count, rows, half), jnp.float32) for count in [len(jobs)] + sends]
    return pl.pallas_call(
        functools.partial(project_kernel, jobs=jobs, sends=sends),
        out_shape=shapes,
        in_specs=in_smem(1) + in_vmem(len(operands)),
        out_specs=in_vmem(len(shapes)),
        compiler_params=pltpu.CompilerParams(vmem_limit_bytes=VMEM_LIMIT),
        cost_estimate=pl.CostEstimate(flops=flops, bytes_accessed=1, transcendentals=0),
        name=name,
    )(flags, *operands)


def after(array, earlier):
    return lax.optimization_barrier((array, *earlier))[0] if earlier else array


def with_rows(array, units):
    flat = array.reshape(-1, array.shape[-1])
    spread = jnp.concatenate([flat[at : at + 8] for at in range(0, flat.shape[0], 8)], axis=1)
    return jnp.pad(spread, ((0, 0), (0, units - spread.shape[1])))


def from_rows(spread, shape):
    pieces = [spread[:, at : at + shape[-1]] for at in range(0, math.prod(shape) // 8, shape[-1])]
    return jnp.concatenate(pieces, axis=0).reshape(shape)


def body(hidden_states, passage_states, down_weight, block_question, question_owner, decoder_states):
    blocks, block_len, units = hidden_states.shape
    width = passage_states.shape[2]
    query_len = decoder_states.shape[1]
    highs, lows, cores = lax.axis_size("high"), lax.axis_size("low"), lax.axis_size("mp")
    group, high, side, low, core = (lax.axis_index(name) for name in ("groups", "high", "side", "low", "mp"))
    shard = down_weight.shape[0]
    stride = lows * shard
    held = width // 2 // cores
    heads = held // HEAD_DIM
    members = highs * lows
    slot_total = question_owner.shape[0]
    rows = blocks * block_len
    lined = highs == 4 and lows == 1 and stride % (cores * 128) == 0
    span = stride // cores if lined else stride
    spans = held // span

    def features(array, of_side):
        if lined:
            starts = [(at * 2 + of_side) * stride + core * span for at in range(spans)]
        else:
            starts = [((core * spans + at) * 2 + of_side) * stride for at in range(spans)]
        taken = [lax.dynamic_slice_in_dim(array, start, span, axis=array.ndim - 1) for start in starts]
        return jnp.concatenate(taken, axis=-1)

    def shifted(array, shift):
        return lax.ppermute(array, "high", [(at, (at + shift) % highs) for at in range(highs)])

    hidden = hidden_states.reshape(rows, units)
    partner_hidden = lax.ppermute(hidden, "side", SWAP)
    queries = jnp.concatenate([features(decoder_states, side), features(decoder_states, 1 - side)], axis=0)[None]
    passages = passage_states.reshape(rows, width)
    leaving = features(passages, 1 - side)

    if lined:
        half = shard // 2
        lengths = [half * FIRST_EIGHTHS // 8, half - half * FIRST_EIGHTHS // 8]
        sent = [
            lax.dynamic_slice_in_dim(down_weight, group * half + first, length, axis=0)
            for first, length in zip((0, lengths[0]), lengths)
        ]
        sent[1] = jnp.concatenate([sent[1], with_rows(queries, units)], axis=0)
        below, above = [], []
        for at in range(2):
            below.append(shifted(after(sent[at], below[-1:]), 1))
            above.append(shifted(after(sent[at], above[-1:] or below[:1]), -1))
        opposite = [shifted(after(below[0], below[1:]), 1), shifted(below[1], 1)]
        around = [from_rows(piece[-1][-8:], queries.shape) for piece in (above, opposite, below)]
        opposite = [jnp.concatenate([opposite[0], opposite[1][: lengths[1]]], axis=0)]
        queries = jnp.concatenate([queries] + around, axis=0)
        swapped = []
        for at, piece in enumerate([below[0], above[0], below[1], above[1]] + opposite):
            swapped.append(lax.ppermute(after(piece, swapped[max(at - 2, 0) : max(at - 1, 0)]), "groups", SWAP))
        weights = [down_weight] + above + swapped[1:4:2] + below + swapped[0:4:2] + opposite + swapped[4:]
        flags = jnp.stack([core, (group == core).astype(core.dtype)])
        blocks_of = [[(2, shard)], list(zip(range(3, 7), 2 * lengths)), list(zip(range(7, 11), 2 * lengths))]
        spots = lax.rem(high + jnp.array([0, 1, 3, 2], jnp.int32), highs)
        spots = jnp.stack([(spots * 2 + side) * stride + core * span, spots * span])
        own_residual = passages

        kept, *away = project(
            flags,
            [hidden, partner_hidden] + weights[:9],
            [(source, blocks_of[at]) for source in range(2) for at in range(3)],
            [2, 2, 2],
            half,
            24 * rows * half * units,
            "project_near",
        )
        flags, kept, *away = lax.optimization_barrier((flags, kept, *away))
        late_kept, *late_away = project(
            flags,
            [hidden, partner_hidden] + weights[9:],
            [(source, [(2, half), (3, half)]) for source in range(2)],
            [2],
            half,
            1,
            "project_far",
        )
        others = [lax.ppermute(piece, "mp", SWAP) for piece in away + late_away]
        summands = [kept, late_kept] + others
        pieces = [(at // 3, (0, at), (2 + at // 2, at % 2), at % 3) for at in range(6)]
        pieces += [(source, (1, source), (5, source), 3) for source in range(2)]
        origin = high
    else:
        queries = lax.all_gather(queries, ("high", "low"), axis=0, tiled=True)
        weight = lax.all_gather(down_weight, ("high", "low"), axis=0, tiled=True)
        weight = jnp.where(core == 0, weight, jnp.roll(weight, held, axis=0))
        spots = jnp.zeros((2, 1), jnp.int32)
        own_residual = features(passages, side)
        summands, pieces = [], []
        for source, flat in enumerate((hidden, partner_hidden)):
            kept, away = (
                lax.dot_general(flat, part, (((1,), (1,)), ((), ())), preferred_element_type=jnp.float32)[None]
                for part in (weight[:held], weight[held:])
            )
            summands += [kept, lax.ppermute(away, "mp", SWAP)]
            pieces.append((source, (2 * source, 0), (2 * source + 1, 0), 0))
        origin = 0

    questions = block_question[:, 0]
    question_ids = jnp.arange(slot_total, dtype=jnp.int32)
    owners = jnp.sum(jnp.where(questions[:, None] == question_ids[None, :], question_owner[None, :], 0), axis=1)
    owner_high, owner_side, owner_low = owners // (2 * lows), (owners // lows) % 2, owners % lows
    owner_high = lax.rem(owner_high - origin + highs, highs)
    owner_place = (owner_high * lows + owner_low) * 2 + (owner_side != side)
    own_at = ((high * 2 + side) * lows + low) * blocks
    partner_at = ((high * 2 + 1 - side) * lows + low) * blocks
    places = jnp.concatenate(
        [lax.dynamic_slice_in_dim(owner_place, at, blocks) for at in (own_at, partner_at)]
    )

    leaving = jnp.concatenate([leaving, queries[:, 1].reshape(-1, held)], axis=0)
    partner = lax.ppermute(leaving, "side", SWAP)
    packed = (members, 2 * held // 128 * query_len + 8, 128)
    operands = summands + [own_residual, partner]
    partials = pl.pallas_call(
        functools.partial(attend_kernel, pieces=pieces),
        out_shape=jax.ShapeDtypeStruct(packed, jnp.float32),
        in_specs=in_smem(2) + in_vmem(1 + len(operands)),
        out_specs=pl.BlockSpec(memory_space=pltpu.VMEM),
        scratch_shapes=[pltpu.VMEM((2 * blocks, block_len, held), jnp.bfloat16)],
        compiler_params=pltpu.CompilerParams(vmem_limit_bytes=VMEM_LIMIT),
        name="attend",
    )(places, spots, queries[:, 0], *operands)
    if lined:
        received = [partials[0:1]] + [shifted(partials[ahead : ahead + 1], ahead) for ahead in range(1, highs)]
    else:
        received = [lax.all_to_all(partials, ("high", "low"), split_axis=0, concat_axis=0, tiled=True)]
    merged = pl.pallas_call(
        merge_kernel,
        out_shape=jax.ShapeDtypeStruct((2, query_len, held), decoder_states.dtype),
        in_specs=in_vmem(len(received)),
        out_specs=pl.BlockSpec(memory_space=pltpu.VMEM),
        compiler_params=pltpu.CompilerParams(vmem_limit_bytes=VMEM_LIMIT),
        name="merge",
    )(*received)

    mine, away = merged[0:1], merged[1:2]
    by_core = lax.ppermute(mine, "mp", SWAP)
    by_side = lax.ppermute(away, "side", SWAP)
    by_both = lax.ppermute(away, ("side", "mp"), CROSS)
    if lined:
        order = [(at, of_side, of) for at in range(spans) for of_side in range(2) for of in range(cores)]
    else:
        order = [(at, of_side, of) for of in range(cores) for at in range(spans) for of_side in range(2)]
    flags = jnp.stack([side, core])
    order = [(of_side, of, at * span) for at, of_side, of in order]
    return pl.pallas_call(
        functools.partial(assemble_kernel, order=order, span=span),
        out_shape=jax.ShapeDtypeStruct((1, query_len, width), decoder_states.dtype),
        in_specs=in_smem(1) + in_vmem(4),
        out_specs=pl.BlockSpec(memory_space=pltpu.VMEM),
        compiler_params=pltpu.CompilerParams(vmem_limit_bytes=VMEM_LIMIT),
        name="assemble",
    )(flags, mine, by_core, by_side, by_both)


def solution(mesh):
    groups, dp, cores = mesh.shape["groups"], mesh.shape["dp"], mesh.shape["mp"]

    def run(hidden_states, passage_states, down_weight, block_question, question_owner, decoder_states):
        lows = max(1, HEAD_DIM * dp // down_weight.shape[0])
        fine = Mesh(
            mesh.devices.reshape(groups, dp // (2 * lows), 2, lows, cores),
            ("groups", "high", "side", "low", "mp"),
        )
        split = ("groups", "high", "side", "low")
        placed = (
            P(split, None, "mp"),
            P(split, None, None),
            P(("high", "side", "low"), "mp"),
            P("groups", None),
            P("groups"),
            P(split, None, None),
        )
        return jax.shard_map(
            body, mesh=fine, in_specs=placed, out_specs=P(split, None, None), check_vma=False
        )(hidden_states, passage_states, down_weight, block_question, question_owner, decoder_states)

    return run
```

```python
import functools
import math

import jax
import jax.numpy as jnp
from jax import lax
from jax.experimental import pallas as pl
from jax.experimental.pallas import tpu as pltpu
from jax.sharding import Mesh, PartitionSpec as P

HEAD_DIM = 64
EMPTY = -3e38
FIRST_EIGHTHS = 3
VMEM_LIMIT = 22 * 1024 * 1024
SWAP = [(0, 1), (1, 0)]
CROSS = [(0, 3), (3, 0), (1, 2), (2, 1)]


def head_pick(tall, query_len):
    lanes = tall.shape[1]
    lane_head = lax.broadcasted_iota(jnp.int32, (query_len, lanes), 1) // HEAD_DIM
    picked = jnp.zeros((query_len, lanes), jnp.float32)
    for head in range(lanes // HEAD_DIM):
        picked = jnp.where(lane_head == head, tall[head * query_len : (head + 1) * query_len, :], picked)
    return picked


def project_kernel(flag_ref, *refs, jobs, sends):
    keep_ref, *send_refs = refs[-1 - len(sends) :]
    slots = [(ref, at) for ref in send_refs for at in range(ref.shape[0])]
    core, same = flag_ref[0], flag_ref[1]
    half = keep_ref.shape[2]
    for at, (rows_of, blocks_of) in enumerate(jobs):
        if len(blocks_of) == 1:
            whole = refs[blocks_of[0][0]]
            keep = whole[pl.ds(pl.multiple_of(core * half, half), half), :]
            send = whole[pl.ds(pl.multiple_of((1 - core) * half, half), half), :]
        else:
            parts = [refs[block][:length] for block, length in blocks_of]
            first, second = (
                jnp.concatenate(part, axis=0) for part in (parts[: len(parts) // 2], parts[len(parts) // 2 :])
            )
            keep = jnp.where(same == 1, first, second)
            send = jnp.where(same == 1, second, first)
        product = lax.dot_general(
            refs[rows_of][...],
            jnp.concatenate([keep, send], axis=0),
            (((1,), (1,)), ((), ())),
            preferred_element_type=jnp.float32,
        )
        keep_ref[at] = product[:, :half]
        send_ref, slot = slots[at]
        send_ref[slot] = product[:, half:]


def attend_kernel(place_ref, spot_ref, query_ref, *refs, pieces):
    *refs, own_ref, partner_ref, out_ref, key_ref = refs
    residuals = own_ref, partner_ref
    partner_queries = own_ref.shape[0]
    query_len, held = query_ref.shape[1:]
    block_len = key_ref.shape[1]
    heads = held // HEAD_DIM
    tall = heads * query_len
    members, packed_rows, lanes_packed = out_ref.shape
    extra = packed_rows - 8
    row = lax.broadcasted_iota(jnp.int32, out_ref.shape, 1)
    out_ref[...] = jnp.where((row == extra) | (row == extra + 1), EMPTY, 0.0)
    row_head = lax.broadcasted_iota(jnp.int32, (tall, held), 0) // query_len
    lane_head = lax.broadcasted_iota(jnp.int32, (tall, held), 1) // HEAD_DIM
    diagonal = row_head == lane_head
    square = lax.broadcasted_iota(jnp.int32, (tall, tall), 0) == lax.broadcasted_iota(jnp.int32, (tall, tall), 1)
    ext = lax.broadcasted_iota(jnp.int32, (8, tall), 0)
    blocks = key_ref.shape[0] // 2
    for source, kept, sent, spot in pieces:
        keep, other = (refs[summand].at[piece] for summand, piece in (kept, sent))
        residual = residuals[source]
        span = keep.shape[1]
        lanes, given = (pl.ds(pl.multiple_of(spot_ref[of, spot], 128), span) for of in (1, source))
        for block in range(blocks):
            rows = slice(block * block_len, (block + 1) * block_len)
            key_ref[source * blocks + block, :, lanes] = (
                residual[rows, given].astype(jnp.float32) + (keep[rows, :] + other[rows, :])
            ).astype(jnp.bfloat16)
    places, scores, tops = [], [], []
    for at in range(key_ref.shape[0]):
        place = place_ref[at]
        first = pl.multiple_of(partner_queries + place // 2 * query_len, query_len)
        query = jnp.where(place % 2 == 0, query_ref[place // 2], partner_ref[pl.ds(first, query_len), :])
        query = jnp.concatenate([query] * heads, axis=0)
        query = jnp.where(diagonal, query, jnp.zeros_like(query))
        score = lax.dot_general(
            query, key_ref[at], (((1,), (1,)), ((), ())), preferred_element_type=jnp.float32
        )
        places.append(place)
        scores.append(score)
        tops.append(jnp.max(score, axis=1, keepdims=True))
    for at, place in enumerate(places):
        top = tops[at]
        for other_at, other_place in enumerate(places):
            if other_at != at:
                top = jnp.maximum(top, jnp.where(other_place == place, tops[other_at], EMPTY))
        weights = jnp.exp(scores[at] - top)
        total = jnp.sum(weights, axis=1, keepdims=True)
        blend = lax.dot_general(
            weights.astype(jnp.bfloat16), key_ref[at], (((1,), (0,)), ((), ())),
            preferred_element_type=jnp.float32,
        )
        top_row = jnp.sum(jnp.where(square, top, 0.0), axis=0, keepdims=True)
        total_row = jnp.sum(jnp.where(square, total, 0.0), axis=0, keepdims=True)
        blend = head_pick(blend, query_len)
        member, slot = place // 2, place % 2
        for block in range(held // lanes_packed):
            first = pl.multiple_of(slot * (extra // 2) + block * query_len, query_len)
            lanes = slice(block * lanes_packed, (block + 1) * lanes_packed)
            spot = pl.ds(first, query_len)
            out_ref[member, spot, :] = out_ref[member, spot, :] + blend[:, lanes]
        before = out_ref[member, extra:, :]
        out_ref[member, extra:, :] = jnp.where(
            ext == slot, top_row, jnp.where(ext == slot + 2, before + total_row, before)
        )


def merge_kernel(*refs):
    out_ref = refs[-1]
    parts = refs[:-1]
    query_len, held = out_ref.shape[1:]
    tall = held // HEAD_DIM * query_len
    square = lax.broadcasted_iota(jnp.int32, (tall, tall), 0) == lax.broadcasted_iota(jnp.int32, (tall, tall), 1)

    def over(start, step):
        for part in parts:
            start = lax.fori_loop(
                0, part.shape[0], functools.partial(step, part), start, unroll=part.shape[0] <= 8
            )
        return start

    packed_rows, lanes_packed = parts[0].shape[1:]
    extra = packed_rows - 8
    for slot in range(out_ref.shape[0]):
        top_row, total_row = (slice(extra + slot + at, extra + slot + at + 1) for at in (0, 2))

        def top_step(part, at, top):
            return jnp.maximum(top, part[at, top_row, :])

        def total_step(part, at, total):
            return total + jnp.exp(part[at, top_row, :] - top) * part[at, total_row, :]

        def blend_step(part, at, blend):
            share = jnp.exp(part[at, top_row, :] - top) / total
            column = jnp.sum(jnp.where(square, share, 0.0), axis=1, keepdims=True)
            spread = head_pick(jnp.broadcast_to(column, (tall, held)), query_len)
            first = slot * (extra // 2)
            rows = [
                part[at, first + block * query_len : first + (block + 1) * query_len, :]
                for block in range(held // lanes_packed)
            ]
            return blend + spread * jnp.concatenate(rows, axis=1)

        top = over(jnp.full((1, tall), EMPTY, jnp.float32), top_step)
        total = over(jnp.zeros((1, tall), jnp.float32), total_step)
        blend = over(jnp.zeros((query_len, held), jnp.float32), blend_step)
        out_ref[slot] = blend.astype(out_ref.dtype)


def assemble_kernel(flag_ref, mine_ref, core_ref, side_ref, both_ref, out_ref, *, order, span):
    side, core = flag_ref[0], flag_ref[1]
    mine, by_core, by_side, by_both = (ref[0] for ref in (mine_ref, core_ref, side_ref, both_ref))
    taken = {}
    for of_side in range(2):
        for of in range(2):
            near = jnp.where(core == of, mine, by_core)
            far = jnp.where(core == of, by_side, by_both)
            taken[of_side, of] = jnp.where(side == of_side, near, far)
    out_ref[0] = jnp.concatenate(
        [taken[of_side, of][:, first : first + span] for of_side, of, first in order], axis=1
    )


def in_vmem(count):
    return [pl.BlockSpec(memory_space=pltpu.VMEM)] * count


def in_smem(count):
    return [pl.BlockSpec(memory_space=pltpu.SMEM)] * count


def project(flags, operands, jobs, sends, half, flops, name):
    rows, units = operands[0].shape
    shapes = [jax.ShapeDtypeStruct((count, rows, half), jnp.float32) for count in [len(jobs)] + sends]
    return pl.pallas_call(
        functools.partial(project_kernel, jobs=jobs, sends=sends),
        out_shape=shapes,
        in_specs=in_smem(1) + in_vmem(len(operands)),
        out_specs=in_vmem(len(shapes)),
        compiler_params=pltpu.CompilerParams(vmem_limit_bytes=VMEM_LIMIT),
        cost_estimate=pl.CostEstimate(flops=flops, bytes_accessed=1, transcendentals=0),
        name=name,
    )(flags, *operands)


def after(array, earlier):
    return lax.optimization_barrier((array, *earlier))[0] if earlier else array


def with_rows(array, units):
    flat = array.reshape(-1, array.shape[-1])
    spread = jnp.concatenate([flat[at : at + 8] for at in range(0, flat.shape[0], 8)], axis=1)
    return jnp.pad(spread, ((0, 0), (0, units - spread.shape[1])))


def from_rows(spread, shape):
    pieces = [spread[:, at : at + shape[-1]] for at in range(0, math.prod(shape) // 8, shape[-1])]
    return jnp.concatenate(pieces, axis=0).reshape(shape)


def body(hidden_states, passage_states, down_weight, block_question, question_owner, decoder_states):
    blocks, block_len, units = hidden_states.shape
    width = passage_states.shape[2]
    query_len = decoder_states.shape[1]
    highs, lows, cores = lax.axis_size("high"), lax.axis_size("low"), lax.axis_size("mp")
    group, high, side, low, core = (lax.axis_index(name) for name in ("groups", "high", "side", "low", "mp"))
    shard = down_weight.shape[0]
    stride = lows * shard
    held = width // 2 // cores
    heads = held // HEAD_DIM
    members = highs * lows
    slot_total = question_owner.shape[0]
    rows = blocks * block_len
    lined = highs == 4 and lows == 1 and stride % (cores * 128) == 0
    span = stride // cores if lined else stride
    spans = held // span

    def features(array, of_side):
        if lined:
            starts = [(at * 2 + of_side) * stride + core * span for at in range(spans)]
        else:
            starts = [((core * spans + at) * 2 + of_side) * stride for at in range(spans)]
        taken = [lax.dynamic_slice_in_dim(array, start, span, axis=array.ndim - 1) for start in starts]
        return jnp.concatenate(taken, axis=-1)

    def shifted(array, shift):
        return lax.ppermute(array, "high", [(at, (at + shift) % highs) for at in range(highs)])

    hidden = hidden_states.reshape(rows, units)
    partner_hidden = lax.ppermute(hidden, "side", SWAP)
    queries = jnp.concatenate([features(decoder_states, side), features(decoder_states, 1 - side)], axis=0)[None]
    passages = passage_states.reshape(rows, width)
    leaving = features(passages, 1 - side)

    if lined:
        half = shard // 2
        lengths = [half * FIRST_EIGHTHS // 8, half - half * FIRST_EIGHTHS // 8]
        sent = [
            lax.dynamic_slice_in_dim(down_weight, group * half + first, length, axis=0)
            for first, length in zip((0, lengths[0]), lengths)
        ]
        sent[1] = jnp.concatenate([sent[1], with_rows(queries, units)], axis=0)
        below, above = [], []
        for at in range(2):
            below.append(shifted(after(sent[at], below[-1:]), 1))
            above.append(shifted(after(sent[at], above[-1:] or below[:1]), -1))
        opposite = [shifted(after(below[0], below[1:]), 1), shifted(below[1], 1)]
        around = [from_rows(piece[-1][-8:], queries.shape) for piece in (above, opposite, below)]
        opposite = [jnp.concatenate([opposite[0], opposite[1][: lengths[1]]], axis=0)]
        queries = jnp.concatenate([queries] + around, axis=0)
        swapped = []
        for at, piece in enumerate([below[0], above[0], below[1], above[1]] + opposite):
            swapped.append(lax.ppermute(after(piece, swapped[max(at - 2, 0) : max(at - 1, 0)]), "groups", SWAP))
        weights = [down_weight] + above + swapped[1:4:2] + below + swapped[0:4:2] + opposite + swapped[4:]
        flags = jnp.stack([core, (group == core).astype(core.dtype)])
        blocks_of = [[(2, shard)], list(zip(range(3, 7), 2 * lengths)), list(zip(range(7, 11), 2 * lengths))]
        spots = lax.rem(high + jnp.array([0, 1, 3, 2], jnp.int32), highs)
        spots = jnp.stack([(spots * 2 + side) * stride + core * span, spots * span])
        own_residual = passages

        kept, *away = project(
            flags,
            [hidden, partner_hidden] + weights[:9],
            [(source, blocks_of[at]) for source in range(2) for at in range(3)],
            [2, 2, 2],
            half,
            24 * rows * half * units,
            "project_near",
        )
        flags, kept, *away = lax.optimization_barrier((flags, kept, *away))
        late_kept, *late_away = project(
            flags,
            [hidden, partner_hidden] + weights[9:],
            [(source, [(2, half), (3, half)]) for source in range(2)],
            [2],
            half,
            1,
            "project_far",
        )
        others = [lax.ppermute(piece, "mp", SWAP) for piece in away + late_away]
        summands = [kept, late_kept] + others
        pieces = [(at // 3, (0, at), (2 + at // 2, at % 2), at % 3) for at in range(6)]
        pieces += [(source, (1, source), (5, source), 3) for source in range(2)]
        origin = high
    else:
        queries = lax.all_gather(queries, ("high", "low"), axis=0, tiled=True)
        weight = lax.all_gather(down_weight, ("high", "low"), axis=0, tiled=True)
        weight = jnp.where(core == 0, weight, jnp.roll(weight, held, axis=0))
        spots = jnp.zeros((2, 1), jnp.int32)
        own_residual = features(passages, side)
        summands, pieces = [], []
        for source, flat in enumerate((hidden, partner_hidden)):
            kept, away = (
                lax.dot_general(flat, part, (((1,), (1,)), ((), ())), preferred_element_type=jnp.float32)[None]
                for part in (weight[:held], weight[held:])
            )
            summands += [kept, lax.ppermute(away, "mp", SWAP)]
            pieces.append((source, (2 * source, 0), (2 * source + 1, 0), 0))
        origin = 0

    questions = block_question[:, 0]
    question_ids = jnp.arange(slot_total, dtype=jnp.int32)
    owners = jnp.sum(jnp.where(questions[:, None] == question_ids[None, :], question_owner[None, :], 0), axis=1)
    owner_high, owner_side, owner_low = owners // (2 * lows), (owners // lows) % 2, owners % lows
    owner_high = lax.rem(owner_high - origin + highs, highs)
    owner_place = (owner_high * lows + owner_low) * 2 + (owner_side != side)
    own_at = ((high * 2 + side) * lows + low) * blocks
    partner_at = ((high * 2 + 1 - side) * lows + low) * blocks
    places = jnp.concatenate(
        [lax.dynamic_slice_in_dim(owner_place, at, blocks) for at in (own_at, partner_at)]
    )

    leaving = jnp.concatenate([leaving, queries[:, 1].reshape(-1, held)], axis=0)
    partner = lax.ppermute(leaving, "side", SWAP)
    packed = (members, 2 * held // 128 * query_len + 8, 128)
    operands = summands + [own_residual, partner]
    partials = pl.pallas_call(
        functools.partial(attend_kernel, pieces=pieces),
        out_shape=jax.ShapeDtypeStruct(packed, jnp.float32),
        in_specs=in_smem(2) + in_vmem(1 + len(operands)),
        out_specs=pl.BlockSpec(memory_space=pltpu.VMEM),
        scratch_shapes=[pltpu.VMEM((2 * blocks, block_len, held), jnp.bfloat16)],
        compiler_params=pltpu.CompilerParams(vmem_limit_bytes=VMEM_LIMIT),
        name="attend",
    )(places, spots, queries[:, 0], *operands)
    if lined:
        received = [partials[0:1]] + [shifted(partials[ahead : ahead + 1], ahead) for ahead in range(1, highs)]
    else:
        received = [lax.all_to_all(partials, ("high", "low"), split_axis=0, concat_axis=0, tiled=True)]
    merged = pl.pallas_call(
        merge_kernel,
        out_shape=jax.ShapeDtypeStruct((2, query_len, held), decoder_states.dtype),
        in_specs=in_vmem(len(received)),
        out_specs=pl.BlockSpec(memory_space=pltpu.VMEM),
        compiler_params=pltpu.CompilerParams(vmem_limit_bytes=VMEM_LIMIT),
        name="merge",
    )(*received)

    mine, away = merged[0:1], merged[1:2]
    by_core = lax.ppermute(mine, "mp", SWAP)
    by_side = lax.ppermute(away, "side", SWAP)
    by_both = lax.ppermute(away, ("side", "mp"), CROSS)
    if lined:
        order = [(at, of_side, of) for at in range(spans) for of_side in range(2) for of in range(cores)]
    else:
        order = [(at, of_side, of) for of in range(cores) for at in range(spans) for of_side in range(2)]
    flags = jnp.stack([side, core])
    order = [(of_side, of, at * span) for at, of_side, of in order]
    return pl.pallas_call(
        functools.partial(assemble_kernel, order=order, span=span),
        out_shape=jax.ShapeDtypeStruct((1, query_len, width), decoder_states.dtype),
        in_specs=in_smem(1) + in_vmem(4),
        out_specs=pl.BlockSpec(memory_space=pltpu.VMEM),
        compiler_params=pltpu.CompilerParams(vmem_limit_bytes=VMEM_LIMIT),
        name="assemble",
    )(flags, mine, by_core, by_side, by_both)


def solution(mesh):
    groups, dp, cores = mesh.shape["groups"], mesh.shape["dp"], mesh.shape["mp"]

    def run(hidden_states, passage_states, down_weight, block_question, question_owner, decoder_states):
        lows = max(1, HEAD_DIM * dp // down_weight.shape[0])
        fine = Mesh(
            mesh.devices.reshape(groups, dp // (2 * lows), 2, lows, cores),
            ("groups", "high", "side", "low", "mp"),
        )
        split = ("groups", "high", "side", "low")
        placed = (
            P(split, None, "mp"),
            P(split, None, None),
            P(("high", "side", "low"), "mp"),
            P("groups", None),
            P("groups"),
            P(split, None, None),
        )
        return jax.shard_map(
            body, mesh=fine, in_specs=placed, out_specs=P(split, None, None), check_vma=False
        )(hidden_states, passage_states, down_weight, block_question, question_owner, decoder_states)

    return run
```

```python
import functools
import math

import jax
import jax.numpy as jnp
from jax import lax
from jax.experimental import pallas as pl
from jax.experimental.pallas import tpu as pltpu
from jax.sharding import Mesh, PartitionSpec as P

HEAD_DIM = 64
EMPTY = -3e38
FIRST_EIGHTHS = 4
VMEM_LIMIT = 22 * 1024 * 1024
SWAP = [(0, 1), (1, 0)]
CROSS = [(0, 3), (3, 0), (1, 2), (2, 1)]


def head_pick(tall, query_len):
    lanes = tall.shape[1]
    lane_head = lax.broadcasted_iota(jnp.int32, (query_len, lanes), 1) // HEAD_DIM
    picked = jnp.zeros((query_len, lanes), jnp.float32)
    for head in range(lanes // HEAD_DIM):
        picked = jnp.where(lane_head == head, tall[head * query_len : (head + 1) * query_len, :], picked)
    return picked


def project_kernel(flag_ref, *refs, jobs, sends):
    keep_ref, *send_refs = refs[-1 - len(sends) :]
    slots = [(ref, at) for ref in send_refs for at in range(ref.shape[0])]
    core, same = flag_ref[0], flag_ref[1]
    half = keep_ref.shape[2]
    for at, (rows_of, blocks_of) in enumerate(jobs):
        if len(blocks_of) == 1:
            whole = refs[blocks_of[0][0]]
            keep = whole[pl.ds(pl.multiple_of(core * half, half), half), :]
            send = whole[pl.ds(pl.multiple_of((1 - core) * half, half), half), :]
        else:
            parts = [refs[block][:length] for block, length in blocks_of]
            first, second = (
                jnp.concatenate(part, axis=0) for part in (parts[: len(parts) // 2], parts[len(parts) // 2 :])
            )
            keep = jnp.where(same == 1, first, second)
            send = jnp.where(same == 1, second, first)
        product = lax.dot_general(
            refs[rows_of][...],
            jnp.concatenate([keep, send], axis=0),
            (((1,), (1,)), ((), ())),
            preferred_element_type=jnp.float32,
        )
        keep_ref[at] = product[:, :half]
        send_ref, slot = slots[at]
        send_ref[slot] = product[:, half:]


def attend_kernel(place_ref, spot_ref, query_ref, *refs, pieces):
    *refs, own_ref, partner_ref, out_ref, key_ref = refs
    residuals = own_ref, partner_ref
    partner_queries = own_ref.shape[0]
    query_len, held = query_ref.shape[1:]
    block_len = key_ref.shape[1]
    heads = held // HEAD_DIM
    tall = heads * query_len
    members, packed_rows, lanes_packed = out_ref.shape
    extra = packed_rows - 8
    row = lax.broadcasted_iota(jnp.int32, out_ref.shape, 1)
    out_ref[...] = jnp.where((row == extra) | (row == extra + 1), EMPTY, 0.0)
    row_head = lax.broadcasted_iota(jnp.int32, (tall, held), 0) // query_len
    lane_head = lax.broadcasted_iota(jnp.int32, (tall, held), 1) // HEAD_DIM
    diagonal = row_head == lane_head
    square = lax.broadcasted_iota(jnp.int32, (tall, tall), 0) == lax.broadcasted_iota(jnp.int32, (tall, tall), 1)
    ext = lax.broadcasted_iota(jnp.int32, (8, tall), 0)
    blocks = key_ref.shape[0] // 2
    for source, kept, sent, spot in pieces:
        keep, other = (refs[summand].at[piece] for summand, piece in (kept, sent))
        residual = residuals[source]
        span = keep.shape[1]
        lanes, given = (pl.ds(pl.multiple_of(spot_ref[of, spot], 128), span) for of in (1, source))
        for block in range(blocks):
            rows = slice(block * block_len, (block + 1) * block_len)
            key_ref[source * blocks + block, :, lanes] = (
                residual[rows, given].astype(jnp.float32) + (keep[rows, :] + other[rows, :])
            ).astype(jnp.bfloat16)
    places, scores, tops = [], [], []
    for at in range(key_ref.shape[0]):
        place = place_ref[at]
        first = pl.multiple_of(partner_queries + place // 2 * query_len, query_len)
        query = jnp.where(place % 2 == 0, query_ref[place // 2], partner_ref[pl.ds(first, query_len), :])
        query = jnp.concatenate([query] * heads, axis=0)
        query = jnp.where(diagonal, query, jnp.zeros_like(query))
        score = lax.dot_general(
            query, key_ref[at], (((1,), (1,)), ((), ())), preferred_element_type=jnp.float32
        )
        places.append(place)
        scores.append(score)
        tops.append(jnp.max(score, axis=1, keepdims=True))
    for at, place in enumerate(places):
        top = tops[at]
        for other_at, other_place in enumerate(places):
            if other_at != at:
                top = jnp.maximum(top, jnp.where(other_place == place, tops[other_at], EMPTY))
        weights = jnp.exp(scores[at] - top)
        total = jnp.sum(weights, axis=1, keepdims=True)
        blend = lax.dot_general(
            weights.astype(jnp.bfloat16), key_ref[at], (((1,), (0,)), ((), ())),
            preferred_element_type=jnp.float32,
        )
        top_row = jnp.sum(jnp.where(square, top, 0.0), axis=0, keepdims=True)
        total_row = jnp.sum(jnp.where(square, total, 0.0), axis=0, keepdims=True)
        blend = head_pick(blend, query_len)
        member, slot = place // 2, place % 2
        for block in range(held // lanes_packed):
            first = pl.multiple_of(slot * (extra // 2) + block * query_len, query_len)
            lanes = slice(block * lanes_packed, (block + 1) * lanes_packed)
            spot = pl.ds(first, query_len)
            out_ref[member, spot, :] = out_ref[member, spot, :] + blend[:, lanes]
        before = out_ref[member, extra:, :]
        out_ref[member, extra:, :] = jnp.where(
            ext == slot, top_row, jnp.where(ext == slot + 2, before + total_row, before)
        )


def merge_kernel(*refs):
    out_ref = refs[-1]
    parts = refs[:-1]
    query_len, held = out_ref.shape[1:]
    tall = held // HEAD_DIM * query_len
    square = lax.broadcasted_iota(jnp.int32, (tall, tall), 0) == lax.broadcasted_iota(jnp.int32, (tall, tall), 1)

    def over(start, step):
        for part in parts:
            start = lax.fori_loop(
                0, part.shape[0], functools.partial(step, part), start, unroll=part.shape[0] <= 8
            )
        return start

    packed_rows, lanes_packed = parts[0].shape[1:]
    extra = packed_rows - 8
    for slot in range(out_ref.shape[0]):
        top_row, total_row = (slice(extra + slot + at, extra + slot + at + 1) for at in (0, 2))

        def top_step(part, at, top):
            return jnp.maximum(top, part[at, top_row, :])

        def total_step(part, at, total):
            return total + jnp.exp(part[at, top_row, :] - top) * part[at, total_row, :]

        def blend_step(part, at, blend):
            share = jnp.exp(part[at, top_row, :] - top) / total
            column = jnp.sum(jnp.where(square, share, 0.0), axis=1, keepdims=True)
            spread = head_pick(jnp.broadcast_to(column, (tall, held)), query_len)
            first = slot * (extra // 2)
            rows = [
                part[at, first + block * query_len : first + (block + 1) * query_len, :]
                for block in range(held // lanes_packed)
            ]
            return blend + spread * jnp.concatenate(rows, axis=1)

        top = over(jnp.full((1, tall), EMPTY, jnp.float32), top_step)
        total = over(jnp.zeros((1, tall), jnp.float32), total_step)
        blend = over(jnp.zeros((query_len, held), jnp.float32), blend_step)
        out_ref[slot] = blend.astype(out_ref.dtype)


def assemble_kernel(flag_ref, mine_ref, core_ref, side_ref, both_ref, out_ref, *, order, span):
    side, core = flag_ref[0], flag_ref[1]
    mine, by_core, by_side, by_both = (ref[0] for ref in (mine_ref, core_ref, side_ref, both_ref))
    taken = {}
    for of_side in range(2):
        for of in range(2):
            near = jnp.where(core == of, mine, by_core)
            far = jnp.where(core == of, by_side, by_both)
            taken[of_side, of] = jnp.where(side == of_side, near, far)
    out_ref[0] = jnp.concatenate(
        [taken[of_side, of][:, first : first + span] for of_side, of, first in order], axis=1
    )


def in_vmem(count):
    return [pl.BlockSpec(memory_space=pltpu.VMEM)] * count


def in_smem(count):
    return [pl.BlockSpec(memory_space=pltpu.SMEM)] * count


def project(flags, operands, jobs, sends, half, flops, name):
    rows, units = operands[0].shape
    shapes = [jax.ShapeDtypeStruct((count, rows, half), jnp.float32) for count in [len(jobs)] + sends]
    return pl.pallas_call(
        functools.partial(project_kernel, jobs=jobs, sends=sends),
        out_shape=shapes,
        in_specs=in_smem(1) + in_vmem(len(operands)),
        out_specs=in_vmem(len(shapes)),
        compiler_params=pltpu.CompilerParams(vmem_limit_bytes=VMEM_LIMIT),
        cost_estimate=pl.CostEstimate(flops=flops, bytes_accessed=1, transcendentals=0),
        name=name,
    )(flags, *operands)


def after(array, earlier):
    return lax.optimization_barrier((array, *earlier))[0] if earlier else array


def with_rows(array, units):
    flat = array.reshape(-1, array.shape[-1])
    spread = jnp.concatenate([flat[at : at + 8] for at in range(0, flat.shape[0], 8)], axis=1)
    return jnp.pad(spread, ((0, 0), (0, units - spread.shape[1])))


def from_rows(spread, shape):
    pieces = [spread[:, at : at + shape[-1]] for at in range(0, math.prod(shape) // 8, shape[-1])]
    return jnp.concatenate(pieces, axis=0).reshape(shape)


def body(hidden_states, passage_states, down_weight, block_question, question_owner, decoder_states):
    blocks, block_len, units = hidden_states.shape
    width = passage_states.shape[2]
    query_len = decoder_states.shape[1]
    highs, lows, cores = lax.axis_size("high"), lax.axis_size("low"), lax.axis_size("mp")
    group, high, side, low, core = (lax.axis_index(name) for name in ("groups", "high", "side", "low", "mp"))
    shard = down_weight.shape[0]
    stride = lows * shard
    held = width // 2 // cores
    heads = held // HEAD_DIM
    members = highs * lows
    slot_total = question_owner.shape[0]
    rows = blocks * block_len
    lined = highs == 4 and lows == 1 and stride % (cores * 128) == 0
    span = stride // cores if lined else stride
    spans = held // span

    def features(array, of_side):
        if lined:
            starts = [(at * 2 + of_side) * stride + core * span for at in range(spans)]
        else:
            starts = [((core * spans + at) * 2 + of_side) * stride for at in range(spans)]
        taken = [lax.dynamic_slice_in_dim(array, start, span, axis=array.ndim - 1) for start in starts]
        return jnp.concatenate(taken, axis=-1)

    def shifted(array, shift):
        return lax.ppermute(array, "high", [(at, (at + shift) % highs) for at in range(highs)])

    hidden = hidden_states.reshape(rows, units)
    partner_hidden = lax.ppermute(hidden, "side", SWAP)
    queries = jnp.concatenate([features(decoder_states, side), features(decoder_states, 1 - side)], axis=0)[None]
    passages = passage_states.reshape(rows, width)
    leaving = features(passages, 1 - side)

    if lined:
        half = shard // 2
        lengths = [half * FIRST_EIGHTHS // 8, half - half * FIRST_EIGHTHS // 8]
        sent = [
            lax.dynamic_slice_in_dim(down_weight, group * half + first, length, axis=0)
            for first, length in zip((0, lengths[0]), lengths)
        ]
        sent[1] = jnp.concatenate([sent[1], with_rows(queries, units)], axis=0)
        below, above = [], []
        for at in range(2):
            below.append(shifted(after(sent[at], below[-1:]), 1))
            above.append(shifted(after(sent[at], above[-1:] or below[:1]), -1))
        opposite = [shifted(after(below[0], below[1:]), 1), shifted(below[1], 1)]
        around = [from_rows(piece[-1][-8:], queries.shape) for piece in (above, opposite, below)]
        opposite = [jnp.concatenate([opposite[0], opposite[1][: lengths[1]]], axis=0)]
        queries = jnp.concatenate([queries] + around, axis=0)
        swapped = []
        for at, piece in enumerate([below[0], above[0], below[1][: lengths[1]], above[1][: lengths[1]]] + opposite):
            swapped.append(lax.ppermute(after(piece, swapped[max(at - 2, 0) : max(at - 1, 0)]), "groups", SWAP))
        weights = [down_weight] + above + swapped[1:4:2] + below + swapped[0:4:2] + opposite + swapped[4:]
        flags = jnp.stack([core, (group == core).astype(core.dtype)])
        blocks_of = [[(2, shard)], list(zip(range(3, 7), 2 * lengths)), list(zip(range(7, 11), 2 * lengths))]
        spots = lax.rem(high + jnp.array([0, 1, 3, 2], jnp.int32), highs)
        spots = jnp.stack([(spots * 2 + side) * stride + core * span, spots * span])
        own_residual = passages

        kept, *away = project(
            flags,
            [hidden, partner_hidden] + weights[:9],
            [(source, blocks_of[at]) for source in range(2) for at in range(3)],
            [2, 2, 2],
            half,
            24 * rows * half * units,
            "project_near",
        )
        flags, kept, *away = lax.optimization_barrier((flags, kept, *away))
        late_kept, *late_away = project(
            flags,
            [hidden, partner_hidden] + weights[9:],
            [(source, [(2, half), (3, half)]) for source in range(2)],
            [2],
            half,
            1,
            "project_far",
        )
        others = [lax.ppermute(piece, "mp", SWAP) for piece in away + late_away]
        summands = [kept, late_kept] + others
        pieces = [(at // 3, (0, at), (2 + at // 2, at % 2), at % 3) for at in range(6)]
        pieces += [(source, (1, source), (5, source), 3) for source in range(2)]
        origin = high
    else:
        queries = lax.all_gather(queries, ("high", "low"), axis=0, tiled=True)
        weight = lax.all_gather(down_weight, ("high", "low"), axis=0, tiled=True)
        weight = jnp.where(core == 0, weight, jnp.roll(weight, held, axis=0))
        spots = jnp.zeros((2, 1), jnp.int32)
        own_residual = features(passages, side)
        summands, pieces = [], []
        for source, flat in enumerate((hidden, partner_hidden)):
            kept, away = (
                lax.dot_general(flat, part, (((1,), (1,)), ((), ())), preferred_element_type=jnp.float32)[None]
                for part in (weight[:held], weight[held:])
            )
            summands += [kept, lax.ppermute(away, "mp", SWAP)]
            pieces.append((source, (2 * source, 0), (2 * source + 1, 0), 0))
        origin = 0

    questions = block_question[:, 0]
    question_ids = jnp.arange(slot_total, dtype=jnp.int32)
    owners = jnp.sum(jnp.where(questions[:, None] == question_ids[None, :], question_owner[None, :], 0), axis=1)
    owner_high, owner_side, owner_low = owners // (2 * lows), (owners // lows) % 2, owners % lows
    owner_high = lax.rem(owner_high - origin + highs, highs)
    owner_place = (owner_high * lows + owner_low) * 2 + (owner_side != side)
    own_at = ((high * 2 + side) * lows + low) * blocks
    partner_at = ((high * 2 + 1 - side) * lows + low) * blocks
    places = jnp.concatenate(
        [lax.dynamic_slice_in_dim(owner_place, at, blocks) for at in (own_at, partner_at)]
    )

    leaving = jnp.concatenate([leaving, queries[:, 1].reshape(-1, held)], axis=0)
    partner = lax.ppermute(leaving, "side", SWAP)
    packed = (members, 2 * held // 128 * query_len + 8, 128)
    operands = summands + [own_residual, partner]
    partials = pl.pallas_call(
        functools.partial(attend_kernel, pieces=pieces),
        out_shape=jax.ShapeDtypeStruct(packed, jnp.float32),
        in_specs=in_smem(2) + in_vmem(1 + len(operands)),
        out_specs=pl.BlockSpec(memory_space=pltpu.VMEM),
        scratch_shapes=[pltpu.VMEM((2 * blocks, block_len, held), jnp.bfloat16)],
        compiler_params=pltpu.CompilerParams(vmem_limit_bytes=VMEM_LIMIT),
        name="attend",
    )(places, spots, queries[:, 0], *operands)
    if lined:
        received = [partials[0:1]] + [shifted(partials[ahead : ahead + 1], ahead) for ahead in range(1, highs)]
    else:
        received = [lax.all_to_all(partials, ("high", "low"), split_axis=0, concat_axis=0, tiled=True)]
    merged = pl.pallas_call(
        merge_kernel,
        out_shape=jax.ShapeDtypeStruct((2, query_len, held), decoder_states.dtype),
        in_specs=in_vmem(len(received)),
        out_specs=pl.BlockSpec(memory_space=pltpu.VMEM),
        compiler_params=pltpu.CompilerParams(vmem_limit_bytes=VMEM_LIMIT),
        name="merge",
    )(*received)

    mine, away = merged[0:1], merged[1:2]
    by_core = lax.ppermute(mine, "mp", SWAP)
    by_side = lax.ppermute(away, "side", SWAP)
    by_both = lax.ppermute(away, ("side", "mp"), CROSS)
    if lined:
        order = [(at, of_side, of) for at in range(spans) for of_side in range(2) for of in range(cores)]
    else:
        order = [(at, of_side, of) for of in range(cores) for at in range(spans) for of_side in range(2)]
    flags = jnp.stack([side, core])
    order = [(of_side, of, at * span) for at, of_side, of in order]
    return pl.pallas_call(
        functools.partial(assemble_kernel, order=order, span=span),
        out_shape=jax.ShapeDtypeStruct((1, query_len, width), decoder_states.dtype),
        in_specs=in_smem(1) + in_vmem(4),
        out_specs=pl.BlockSpec(memory_space=pltpu.VMEM),
        compiler_params=pltpu.CompilerParams(vmem_limit_bytes=VMEM_LIMIT),
        name="assemble",
    )(flags, mine, by_core, by_side, by_both)


def solution(mesh):
    groups, dp, cores = mesh.shape["groups"], mesh.shape["dp"], mesh.shape["mp"]

    def run(hidden_states, passage_states, down_weight, block_question, question_owner, decoder_states):
        lows = max(1, HEAD_DIM * dp // down_weight.shape[0])
        fine = Mesh(
            mesh.devices.reshape(groups, dp // (2 * lows), 2, lows, cores),
            ("groups", "high", "side", "low", "mp"),
        )
        split = ("groups", "high", "side", "low")
        placed = (
            P(split, None, "mp"),
            P(split, None, None),
            P(("high", "side", "low"), "mp"),
            P("groups", None),
            P("groups"),
            P(split, None, None),
        )
        return jax.shard_map(
            body, mesh=fine, in_specs=placed, out_specs=P(split, None, None), check_vma=False
        )(hidden_states, passage_states, down_weight, block_question, question_owner, decoder_states)

    return run
```
